32 devices in a mesh: seq: 8 (over z, x), trow: 2 (over core), tcol: 2 (over y).
Axes of the slice: x: 2, y: 2, z: 4, core: 2. Of those that a mesh axis runs over, the one named last changes fastest.
Arguments:
- tokens: bfloat16 [4096, 4096], P('seq', ('trow', 'tcol')), may hold values from -24 to 24
- norm_gain: float32 [4096], replicated, may hold values from 0.1 to 1.9
- in_weight: bfloat16 [3, 4096, 8192], P(None, None, ('trow', 'tcol')), may hold values from -0.09375 to 0.09375
- filter_taps: float32 [128, 8192], P(None, ('trow', 'tcol')), may hold values from -0.5 to 0.5
- conv_skip: float32 [8192], P(('trow', 'tcol')), may hold values from -1 to 1
- out_weight: bfloat16 [8192, 4096], P(('trow', 'tcol')), may hold values from -0.09375 to 0.09375
Outputs:
- mixer_out: bfloat16 [4096, 4096], P('seq', ('trow', 'tcol'))
The draws below stay inside these ranges and needn't reach their ends.
All inputs are finite; a program needn't handle non-finite values.
Results may differ from the reference program's by a relative error of at most 0.03.
Values may be sent and summed in bfloat16 or wider, within the bound.
No kernel may reach another device: no remote copies, remote signals or barrier semaphores. Data moves between devices by JAX's collectives and lax.ppermute only.
A program may use at most 128 MiB of HBM per device.

```python
import math
import jax
import jax.numpy as jnp
from jax import lax

D = 4096
C = 8192
TAPS = 128
TOKENS = 4096
N_TROW = 2
N_TCOL = 2


def draw_tokens(key, part):
    first, second, third = jax.random.split(key, 3)
    base = jax.random.truncated_normal(first, -4.0, 4.0, (TOKENS, D), jnp.float32)
    row_scale = jnp.exp(jax.random.uniform(second, (TOKENS, 1), jnp.float32, math.log(0.5), math.log(2.0)))
    col_scale = jnp.exp(jax.random.uniform(third, (1, D), jnp.float32, math.log(0.3), math.log(3.0)))
    return (base * row_scale * col_scale).astype(jnp.bfloat16)


def spiked(values, own_key, source, target, shards_of, factor):
    def block_of(position):
        return (jnp.arange(values.shape[position]) // (values.shape[position] // shards_of)).reshape((-1,) + (1,) * (values.ndim - 1 - position))

    first = jax.random.permutation(own_key, shards_of)[block_of(target)]
    second = (block_of(target) + shards_of // 2) % shards_of
    return jnp.where((block_of(source) == first) | (block_of(source) == second), factor * values, values)


def block_scale(key, extent, shards, smallest, largest):
    factor_of = 1.0
    for axis_at, blocks in shards:
        draws = jax.random.uniform(jax.random.fold_in(jax.random.fold_in(key, 6), axis_at), (blocks,), jnp.float32, smallest / len(shards), largest / len(shards))
        factor_of = factor_of * jnp.repeat(jnp.exp(draws), extent[axis_at] // blocks).reshape((-1,) + (1,) * (len(extent) - 1 - axis_at))
    return factor_of


def normal_values(stream_key, dims, spread, most, shards=(), kind=jnp.bfloat16):
    values = spread * jax.random.normal(stream_key, dims, jnp.float32)
    if shards:
        values = values * block_scale(stream_key, dims, shards, -0.22, 0.18)
    return jnp.clip(values, -most, most).astype(kind)


def noise_with(key, dims, spread, reach, pieces, heavy, kind=jnp.bfloat16):
    values = spread * jax.random.normal(key, dims, jnp.float32)
    if pieces:
        values = values * block_scale(key, dims, pieces, -0.22, 0.18)
    return jnp.clip(spiked(values, jax.random.fold_in(key, 3), *heavy), -reach, reach).astype(kind)


def setup_inputs(seed: int = 0) -> dict:
    splits = jax.random.split(jax.random.key(seed), 7)
    tokens = draw_tokens(jax.random.fold_in(splits[6], 71), 0)
    norm_gain = jnp.clip(1.0 + 0.18 * jax.random.normal(splits[1], (D,), jnp.float32), 0.1, 1.9)
    in_weight = normal_values(splits[2], (3, D, C), D ** -0.5, 0.09375, ((2, 4),))
    filter_taps = normal_values(splits[3], (TAPS, C), TAPS ** -0.5, 0.5, ((1, 4),), jnp.float32)
    conv_skip = jnp.clip(jax.random.uniform(splits[4], (C,), jnp.float32, -1.0, 1.0) * block_scale(splits[4], (C,), ((0, 4),), -0.4, 0.0), -1.0, 1.0)
    out_weight = noise_with(splits[5], (C, D), C ** -0.5, 0.09375, ((0, 4),), (0, 1, 4, 2.0))
    return {"tokens": tokens, "norm_gain": norm_gain, "in_weight": in_weight, "filter_taps": filter_taps, "conv_skip": conv_skip, "out_weight": out_weight}


def reference(tokens, norm_gain, in_weight, filter_taps, conv_skip, out_weight):
    x = tokens.astype(jnp.float32)
    mean_square = lax.optimization_barrier(jnp.mean(x * x, axis=1, keepdims=True))
    normed = (x * lax.rsqrt(mean_square + 1e-06) * norm_gain).astype(jnp.bfloat16)
    query = jnp.dot(normed, in_weight[0], preferred_element_type=jnp.float32).astype(jnp.bfloat16)
    keys = jnp.dot(normed, in_weight[1], preferred_element_type=jnp.float32).astype(jnp.bfloat16)
    values = jnp.dot(normed, in_weight[2], preferred_element_type=jnp.float32).astype(jnp.bfloat16)
    mixed = (keys.astype(jnp.float32) * values.astype(jnp.float32)).astype(jnp.bfloat16)
    extended = jnp.concatenate([jnp.zeros((TAPS - 1, C), jnp.bfloat16), mixed], axis=0)

    def one_tap(step, total):
        index = jnp.asarray(step).astype(jnp.int32)
        window = lax.dynamic_slice_in_dim(extended, (TAPS - 1 - index).astype(jnp.int32), TOKENS, 0)
        weight = lax.dynamic_slice_in_dim(filter_taps, index, 1, 0)
        return total + window.astype(jnp.float32) * weight
    filtered = lax.fori_loop(0, TAPS, one_tap, jnp.zeros((TOKENS, C), jnp.float32))
    filtered = filtered + conv_skip * mixed.astype(jnp.float32)
    gated = (query.astype(jnp.float32) * filtered).astype(jnp.bfloat16)
    blocks = N_TROW * N_TCOL
    width = C // blocks

    def add_block(total, block):
        start = (block * width).astype(jnp.int32)
        part_gated = lax.dynamic_slice_in_dim(gated, start, width, 1)
        part_weight = lax.dynamic_slice_in_dim(out_weight, start, width, 0)
        rounded = jnp.dot(part_gated, part_weight, preferred_element_type=jnp.float32).astype(jnp.bfloat16)
        rounded = lax.optimization_barrier(rounded)
        return (total + rounded.astype(jnp.float32), None)
    total, unused = lax.scan(add_block, jnp.zeros((TOKENS, D), jnp.float32), jnp.arange(blocks, dtype=jnp.int32))
    return total.astype(jnp.bfloat16)
```

```python
import functools

import jax
import jax.numpy as jnp
import numpy as np
from jax import lax
from jax.experimental import pallas as pl
from jax.experimental.pallas import tpu as pltpu
from jax.sharding import PartitionSpec as P

BF16 = jnp.bfloat16
F32 = jnp.float32
MIB = 1024 * 1024


def dft_matrices(taps):
    size = 2 * taps
    t = np.arange(size)[None, :]
    k = np.arange(taps)[:, None]
    angle = 2.0 * np.pi * ((k * t) % size) / size
    cos, sin = np.cos(angle), np.sin(angle)
    alternating = (-1.0) ** t
    forward = np.concatenate([cos, alternating, -sin[1:]], axis=0)
    inverse = np.concatenate([cos[:1], 2.0 * cos[1:], alternating, -2.0 * sin[1:]], axis=0).T / size
    short = slice(0, taps)
    of_filter = np.concatenate(
        [cos[:, short], 0.0 * sin[:1, short], -sin[1:, short], alternating[:, short], cos[1:, short]], axis=0
    )
    of_filter = np.concatenate([of_filter, of_filter], axis=1)
    return forward.astype(BF16), inverse[taps:].astype(BF16), of_filter.astype(BF16)


def dot(a, b):
    return jnp.dot(a, b, preferred_element_type=F32)


def spectrum_kernel(taps_ref, skip_ref, of_filter_ref, spec_ref):
    h = taps_ref[...]
    first = lax.broadcasted_iota(jnp.int32, h.shape, 0) == 0
    h = h + jnp.where(first, skip_ref[...], 0.0)
    high = h.astype(BF16)
    low = (h - high.astype(F32)).astype(BF16)
    spec_ref[...] = dot(of_filter_ref[...], jnp.concatenate([high, low], axis=0))


def convolved(window, spectrum, forward, inverse):
    half = window.shape[0] // 2
    x = dot(forward, window)
    xa, xb = x[:half], x[half:]
    ha, hb, hc = spectrum[:half], spectrum[half : 2 * half], spectrum[2 * half :]
    y = jnp.concatenate([xa * ha - xb * hb, xa * hb + xb * hc], axis=0)
    return dot(inverse, y.astype(BF16))


def scaled_inputs(lhs_refs, gain_refs, xg_ref):
    total = jnp.zeros((xg_ref.shape[1], 1), F32)
    for i, (x_ref, g_ref) in enumerate(zip(lhs_refs, gain_refs)):
        x = x_ref[...].astype(F32)
        total = total + jnp.sum(x * x, axis=1, keepdims=True)
        xg_ref[i] = (x * g_ref[0]).astype(BF16)
    return jnp.broadcast_to(total, (xg_ref.shape[1], 128))


def columns(step, ct):
    return pl.ds(pl.multiple_of(step * ct, ct), ct)


def local_kernel(n_lhs, blocks_ref, *refs):
    lhs, gains, weights = refs[:n_lhs], refs[n_lhs : 2 * n_lhs], refs[2 * n_lhs : 3 * n_lhs]
    acc_ref, ssq_ref, xg_ref = refs[-3:]
    step = pl.program_id(0)

    @pl.when(step == 0)
    def _():
        ssq_ref[...] = scaled_inputs(lhs, gains, xg_ref)

    at = columns(step, weights[0].shape[2])
    for j in range(3):
        acc = dot(xg_ref[0], weights[0][j])
        for i in range(1, n_lhs):
            acc = acc + dot(xg_ref[i], weights[i][j])
        acc_ref[j, :, at] = acc


def streams(n_lhs, d_model, rows, at, lhs, gains, weights, acc_ref, ssq_ref, xg_ref, own_ssq_ref):
    @pl.when(pl.program_id(0) == 0)
    def _():
        own_ssq_ref[...] = scaled_inputs(lhs, gains, xg_ref)

    scale = lax.rsqrt((ssq_ref[rows, :1] + own_ssq_ref[:, :1]) / d_model + 1e-06)
    out = []
    for j in range(3):
        acc = acc_ref[j, rows, at]
        for i in range(n_lhs):
            acc = acc + dot(xg_ref[i], weights[i][j])
        out.append((acc * scale).astype(BF16))
    query, keys, values = out
    mixed = (keys.astype(F32) * values.astype(F32)).astype(BF16)
    return query, mixed


def gate(query, mixed, b, at, spec_ref, fwd_ref, inv_ref, taps):
    filtered = convolved(mixed[(b - 1) * taps : (b + 1) * taps], spec_ref[:, at], fwd_ref[...], inv_ref[...])
    return (query[b * taps : (b + 1) * taps].astype(F32) * filtered).astype(BF16)


def upper_kernel(n_lhs, d_model, taps, blocks_ref, *refs):
    lhs, gains, weights = refs[:n_lhs], refs[n_lhs : 2 * n_lhs], refs[2 * n_lhs : 3 * n_lhs]
    acc_ref, ssq_ref, spec_ref, fwd_ref, inv_ref = refs[3 * n_lhs : 3 * n_lhs + 5]
    tail_ref, q_ref, mixed_ref, gated_ref, xg_ref, own_ssq_ref = refs[-6:]
    at = columns(pl.program_id(0), weights[0].shape[2])
    rows = slice(2 * taps, 4 * taps)
    query, mixed = streams(n_lhs, d_model, rows, at, lhs, gains, weights, acc_ref, ssq_ref, xg_ref, own_ssq_ref)
    tail_ref[...] = mixed[taps:]
    q_ref[:, at] = query[:taps]
    mixed_ref[:, at] = mixed[:taps]
    gated_ref[:, at] = gate(query, mixed, 1, at, spec_ref, fwd_ref, inv_ref, taps)


def lower_kernel(n_lhs, d_model, taps, blocks_ref, *refs):
    lhs, gains, weights = refs[:n_lhs], refs[n_lhs : 2 * n_lhs], refs[2 * n_lhs : 3 * n_lhs]
    acc_ref, ssq_ref, spec_ref, fwd_ref, inv_ref, q_up_ref, mixed_up_ref = refs[3 * n_lhs : 3 * n_lhs + 7]
    q_ref, mixed_ref, one_ref, two_ref, xg_ref, own_ssq_ref = refs[-6:]
    at = columns(pl.program_id(0), weights[0].shape[2])
    rows = slice(0, 2 * taps)
    query, mixed = streams(n_lhs, d_model, rows, at, lhs, gains, weights, acc_ref, ssq_ref, xg_ref, own_ssq_ref)
    q_ref[:, at] = query[:taps]
    mixed_ref[:, at] = mixed[:taps]
    mixed = jnp.concatenate([mixed, mixed_up_ref[:, at]], axis=0)
    query = jnp.concatenate([query, q_up_ref[:, at]], axis=0)
    one_ref[:, at] = gate(query, mixed, 1, at, spec_ref, fwd_ref, inv_ref, taps)
    two_ref[:, at] = gate(query, mixed, 2, at, spec_ref, fwd_ref, inv_ref, taps)


def first_kernel(halo_ref, mixed_ref, q_ref, spec_ref, fwd_ref, inv_ref, gated_ref):
    ct = column_tile(q_ref.shape[1])
    for at in range(0, q_ref.shape[1], ct):
        at = slice(at, at + ct)
        window = jnp.concatenate([halo_ref[:, at], mixed_ref[:, at]], axis=0)
        filtered = convolved(window, spec_ref[:, at], fwd_ref[...], inv_ref[...])
        gated_ref[:, at] = (q_ref[:, at].astype(F32) * filtered).astype(BF16)


def params(mib, steps=1):
    return pltpu.CompilerParams(dimension_semantics=("arbitrary",) * steps, vmem_limit_bytes=mib * MIB)


def in_hbm(x):
    return pltpu.with_memory_space_constraint(x, pltpu.HBM)


def in_vmem(x):
    return pltpu.with_memory_space_constraint(x, pltpu.VMEM)


RESIDENT = pl.BlockSpec(memory_space=pltpu.VMEM)


def whole(shape):
    return pl.BlockSpec(shape, lambda ch, *_: (0,) * len(shape))


def lhs_specs(lhs, first, norm_gain, in_weight, ct):
    rows, depth = lhs[0].shape
    n = len(lhs)
    gain = norm_gain.reshape(-1, 1, depth)
    specs = [whole((rows, depth))] * n
    specs += [pl.BlockSpec((1, 1, depth), lambda ch, b, i=i: (b[first + i], 0, 0)) for i in range(n)]
    specs += [pl.BlockSpec((3, depth, ct), lambda ch, b, i=i: (0, b[first + i], ch)) for i in range(n)]
    scratch = [pltpu.VMEM((n, rows, depth), BF16)]
    return specs, scratch, [in_hbm(x) for x in lhs] + [gain] * n + [in_hbm(in_weight)] * n


def cost(rows, depth, width, extra=0):
    return pl.CostEstimate(
        flops=2 * rows * depth * width, bytes_accessed=2 * (rows * depth + depth * width) + extra, transcendentals=0
    )


def column_tile(channels, most=256):
    return most if channels % most == 0 else channels


def nothing_kernel(*refs):
    pass


def held_until(x, *others):
    return pl.pallas_call(
        nothing_kernel,
        in_specs=[pl.BlockSpec(memory_space=pl.ANY)] * (1 + len(others)),
        out_specs=pl.BlockSpec(memory_space=pl.ANY),
        out_shape=jax.ShapeDtypeStruct(x.shape, x.dtype),
        input_output_aliases={0: 0},
        compiler_params=pltpu.CompilerParams(vmem_limit_bytes=MIB),
        name="held_until",
    )(x, *others)


def filter_transform(filter_taps, conv_skip, of_filter):
    taps, channels = filter_taps.shape
    ct = column_tile(channels, 1024)
    tile = lambda r: pl.BlockSpec((r, ct), lambda ch: (0, ch))
    return pl.pallas_call(
        spectrum_kernel,
        grid=(channels // ct,),
        in_specs=[tile(taps), tile(1), whole(of_filter.shape)],
        out_specs=tile(3 * taps),
        out_shape=pltpu.VMEM((3 * taps, channels), F32),
        compiler_params=params(10),
        cost_estimate=cost(3 * taps, 2 * taps, channels),
        name="filter_transform",
    )(in_hbm(filter_taps), conv_skip.reshape(1, -1), of_filter)


def project_local(lhs, places, first, norm_gain, in_weight, waits):
    rows, depth = lhs[0].shape
    channels = in_weight.shape[2]
    ct = column_tile(channels)
    specs, scratch, operands = lhs_specs(lhs, first, norm_gain, in_weight, ct)
    return pl.pallas_call(
        functools.partial(local_kernel, len(lhs)),
        grid_spec=pltpu.PrefetchScalarGridSpec(
            num_scalar_prefetch=1,
            grid=(channels // ct,),
            in_specs=specs + [pl.BlockSpec(memory_space=pl.ANY)] * len(waits),
            out_specs=[RESIDENT, RESIDENT],
            scratch_shapes=scratch,
        ),
        out_shape=[pltpu.VMEM((3, rows, channels), F32), pltpu.VMEM((rows, 128), F32)],
        compiler_params=params(18),
        cost_estimate=cost(rows, depth * len(lhs), 3 * channels),
        name="project_local",
    )(places, *operands, *waits)


def project_rest(kernel, name, lhs, places, first, norm_gain, in_weight, resident, waits, outs, tiled, d_model, taps):
    rows, depth = lhs[0].shape
    channels = in_weight.shape[2]
    ct = column_tile(channels)
    specs, scratch, operands = lhs_specs(lhs, first, norm_gain, in_weight, ct)
    return pl.pallas_call(
        functools.partial(kernel, len(lhs), d_model, taps),
        grid_spec=pltpu.PrefetchScalarGridSpec(
            num_scalar_prefetch=1,
            grid=(channels // ct,),
            in_specs=specs + [RESIDENT] * len(resident) + [pl.BlockSpec(memory_space=pl.ANY)] * len(waits),
            out_specs=[pl.BlockSpec((taps, ct), lambda ch, b: (0, ch))] * tiled + [RESIDENT] * outs,
            scratch_shapes=scratch + [pltpu.VMEM((rows, 128), F32)],
        ),
        out_shape=[jax.ShapeDtypeStruct((taps, channels), BF16)] * tiled + [pltpu.VMEM((taps, channels), BF16)] * outs,
        compiler_params=params(18),
        cost_estimate=cost(rows, depth * len(lhs), 3 * channels),
        name=name,
    )(places, *operands, *[in_vmem(x) for x in resident], *waits)


def gate_first(halo, mixed, query, spectrum, forward, inverse):
    taps, channels = mixed.shape
    return pl.pallas_call(
        first_kernel,
        in_specs=[RESIDENT] * 6,
        out_specs=RESIDENT,
        out_shape=pltpu.VMEM((taps, channels), BF16),
        compiler_params=pltpu.CompilerParams(vmem_limit_bytes=8 * MIB),
        cost_estimate=cost(3 * taps, 2 * taps, channels),
        name="gate_first",
    )(in_hbm(halo), *[in_vmem(x) for x in (mixed, query, spectrum, forward, inverse)])


def out_kernel(n_parts, first, n_groups, has_add, groups_ref, *refs):
    parts, w_ref = refs[:n_parts], refs[n_parts]
    o_ref = refs[-1]
    width = o_ref.shape[2]
    lhs = jnp.concatenate([p[...] for p in parts], axis=0)
    for g in range(n_groups):
        at = pl.ds(pl.multiple_of(groups_ref[first + g] * width, width), width)
        product = dot(lhs, w_ref[:, at])
        if has_add:
            product = product + refs[n_parts + 1][g].astype(F32)
        o_ref[g] = product.astype(o_ref.dtype)


def project_out(parts, out_weight, places, first, n_groups, width, add, dtype, name):
    rows = sum(p.shape[0] for p in parts)
    channels = out_weight.shape[0]
    return pl.pallas_call(
        functools.partial(out_kernel, len(parts), first, n_groups, add is not None),
        in_specs=[pl.BlockSpec(memory_space=pltpu.SMEM)] + [RESIDENT] * (len(parts) + 1 + (add is not None)),
        out_specs=RESIDENT,
        out_shape=jax.ShapeDtypeStruct((n_groups, rows, width), dtype),
        compiler_params=pltpu.CompilerParams(vmem_limit_bytes=10 * MIB),
        cost_estimate=cost(rows, channels, n_groups * width),
        name=name,
    )(places, *[in_vmem(p) for p in parts], in_vmem(out_weight), *([add] if add is not None else []))


def finish_kernel(n_come, *refs):
    total = refs[0][0]
    for x in refs[1 : 1 + n_come]:
        total = total + x[...].astype(F32)
    refs[-1][...] = total.astype(refs[-1].dtype)


def finish(near, come, into, part, parts):
    rows, width = near.shape[1:]
    operands = [near, *come] + ([into] if into is not None else [])
    return pl.pallas_call(
        functools.partial(finish_kernel, len(come)),
        grid=(1,),
        in_specs=[pl.BlockSpec((1, rows, width), lambda i: (0, 0, 0))]
        + [pl.BlockSpec((rows, width), lambda i: (0, 0))] * len(come)
        + ([pl.BlockSpec(memory_space=pl.ANY)] if into is not None else []),
        out_specs=pl.BlockSpec((rows, width), lambda i: (part, 0)),
        out_shape=jax.ShapeDtypeStruct((rows * parts, width), BF16),
        input_output_aliases={len(operands) - 1: 0} if into is not None else {},
        compiler_params=params(8),
        name="finish",
    )(*operands)


def on_device(tokens, norm_gain, in_weight, filter_taps, conv_skip, out_weight):
    n_row, n_col, n_seq = lax.axis_size("trow"), lax.axis_size("tcol"), lax.axis_size("seq")
    r, c = lax.axis_index("trow"), lax.axis_index("tcol")
    rows, depth = tokens.shape
    taps = filter_taps.shape[0]
    half = 2 * taps
    d_model = depth * n_row * n_col
    assert n_row == 2 and rows == 2 * half
    forward, inverse, of_filter = (jnp.asarray(m) for m in dft_matrices(taps))

    def other_core(x):
        return lax.ppermute(x, "trow", [(0, 1), (1, 0)])

    def chips_along(x, s):
        return lax.ppermute(x, "tcol", [(i, (i + s) % n_col) for i in range(n_col)])

    def block_of(row, s):
        return row * n_col + lax.rem(c + s + n_col, n_col)

    beside = other_core(tokens)
    upper_far = [chips_along(tokens[half:], s) for s in range(1, n_col)]
    lower_far = [chips_along(tokens[:half], s) for s in range(1, n_col)]
    shifts = range(1, n_col)
    places = jnp.stack(
        [block_of(r, 0), block_of(1 - r, 0)]
        + [block_of(row, -s) for row in (r, 1 - r) for s in shifts]
        + [block_of(row, s) for row in (1 - r, r) for s in shifts]
        + [block_of(1 - r, 0), block_of(r, 0)]
    )
    far_features, theirs_far = 2, 2 * n_col
    mine_far = theirs_far + n_col - 1
    theirs_near, mine_near = mine_far + n_col - 1, mine_far + n_col
    spectrum = filter_transform(filter_taps, conv_skip, of_filter)
    acc, ssq = project_local([tokens, beside], places, 0, norm_gain, in_weight, [spectrum])
    rest = functools.partial(project_rest, places=places, first=far_features, norm_gain=norm_gain, in_weight=in_weight, d_model=d_model, taps=taps)
    upper_far = [held_until(x, ssq) for x in upper_far]
    lower_far = [held_until(x, ssq) for x in lower_far]
    resident = [acc, ssq, spectrum, forward, inverse]
    upper = upper_far + [other_core(x) for x in upper_far]
    tail, q_up, mixed_up, gated_up = rest(
        upper_kernel, "project_upper", upper, resident=resident, waits=lower_far, outs=3, tiled=1
    )
    halo = lax.ppermute(tail, "seq", [(i, i + 1) for i in range(n_seq - 1)])
    lower = lower_far + [other_core(x) for x in lower_far]
    q_low, mixed_low, gated_one, gated_two = rest(
        lower_kernel, "project_lower", lower, resident=resident + [q_up, mixed_up], waits=[], outs=4, tiled=0
    )

    def out_rows(parts, name):
        project = functools.partial(project_out, parts, out_weight, places)
        far = other_core(project(theirs_far, n_col - 1, depth, None, BF16, name + "_theirs_far"))
        near = other_core(project(theirs_near, 1, depth, None, BF16, name + "_theirs_near"))
        sent = project(mine_far, n_col - 1, depth, far, BF16, name + "_mine_far")
        come = [chips_along(sent[s - 1], s) for s in range(1, n_col)]
        return project(mine_near, 1, depth, near, F32, name + "_mine_near"), come, sent

    near_up, come_up, sent_up = out_rows([gated_two, gated_up], "out_up")
    gated_first = gate_first(halo, mixed_low, q_low, spectrum, forward, inverse)
    near_low, come_low, _ = out_rows([gated_first, gated_one], "out_low")
    out = finish(near_up, come_up, None, 1, 2)
    return finish(near_low, come_low, out, 0, 2)


def solution(mesh):
    placed = (
        P("seq", ("trow", "tcol")),
        P(),
        P(None, None, ("trow", "tcol")),
        P(None, ("trow", "tcol")),
        P(("trow", "tcol")),
        P(("trow", "tcol"), None),
    )
    return jax.shard_map(
        on_device, mesh=mesh, in_specs=placed, out_specs=P("seq", ("trow", "tcol")), check_vma=False
    )
```

```python
import functools

import jax
import jax.numpy as jnp
import numpy as np
from jax import lax
from jax.experimental import pallas as pl
from jax.experimental.pallas import tpu as pltpu
from jax.sharding import PartitionSpec as P

BF16 = jnp.bfloat16
F32 = jnp.float32
MIB = 1024 * 1024


def dft_matrices(taps):
    size = 2 * taps
    t = np.arange(size)[None, :]
    k = np.arange(taps)[:, None]
    angle = 2.0 * np.pi * ((k * t) % size) / size
    cos, sin = np.cos(angle), np.sin(angle)
    alternating = (-1.0) ** t
    forward = np.concatenate([cos, alternating, -sin[1:]], axis=0)
    inverse = np.concatenate([cos[:1], 2.0 * cos[1:], alternating, -2.0 * sin[1:]], axis=0).T / size
    short = slice(0, taps)
    of_filter = np.concatenate(
        [cos[:, short], 0.0 * sin[:1, short], -sin[1:, short], alternating[:, short], cos[1:, short]], axis=0
    )
    of_filter = np.concatenate([of_filter, of_filter], axis=1)
    return forward.astype(BF16), inverse[taps:].astype(BF16), of_filter.astype(BF16)


def dot(a, b):
    return jnp.dot(a, b, preferred_element_type=F32)


def spectrum_kernel(taps_ref, skip_ref, of_filter_ref, *refs):
    spec_ref = refs[-1]
    h = taps_ref[...]
    first = lax.broadcasted_iota(jnp.int32, h.shape, 0) == 0
    h = h + jnp.where(first, skip_ref[...], 0.0)
    high = h.astype(BF16)
    low = (h - high.astype(F32)).astype(BF16)
    spec_ref[...] = dot(of_filter_ref[...], jnp.concatenate([high, low], axis=0))


def convolved(window, spectrum, forward, inverse):
    half = window.shape[0] // 2
    x = dot(forward, window)
    xa, xb = x[:half], x[half:]
    ha, hb, hc = spectrum[:half], spectrum[half : 2 * half], spectrum[2 * half :]
    y = jnp.concatenate([xa * ha - xb * hb, xa * hb + xb * hc], axis=0)
    return dot(inverse, y.astype(BF16))


def columns(step, ct):
    return pl.ds(pl.multiple_of(step * ct, ct), ct)


def projection(first, places, tokens, gain_ref, weight_ref, xg_ref, buf, sem, use, before=None):
    slots, _, _, ct = buf.shape
    depth = tokens[0].shape[1]
    tiles = weight_ref.shape[2] // ct

    def copies(tile, slot):
        return [
            pltpu.make_async_copy(
                weight_ref.at[:, pl.ds(pl.multiple_of(places[first + i] * depth, depth), depth), columns(tile, ct)],
                buf.at[slot, :, pl.ds(i * depth, depth)],
                sem.at[slot, i],
            )
            for i in range(len(tokens))
        ]

    for tile in range(min(slots - 1, tiles)):
        for copy in copies(tile, tile):
            copy.start()
    total = jnp.zeros((xg_ref.shape[0], 1), F32)
    for i, x_ref in reversed(list(enumerate(tokens))):
        if i == 0 and before is not None:
            before.wait()
        x = x_ref[...].astype(F32)
        total = total + jnp.sum(x * x, axis=1, keepdims=True)
        xg_ref[:, i * depth : (i + 1) * depth] = (x * gain_ref[places[first + i]]).astype(BF16)

    def step(tile, _):
        slot = lax.rem(tile, slots)
        ahead = tile + slots - 1

        @pl.when(ahead < tiles)
        def _():
            for copy in copies(ahead, lax.rem(ahead, slots)):
                copy.start()

        for copy in copies(tile, slot):
            copy.wait()
        use(tile, [dot(xg_ref[...], buf[slot, j]) for j in range(3)], total)
        return 0

    lax.fori_loop(0, tiles, step, 0)
    return total


def local_kernel(first, places, own_ref, beside_ref, gain_ref, weight_ref, out_w_ref, acc_ref, ssq_ref, held_w_ref,
                 own_held, xg_ref, buf, sem, own_sem, out_sem):
    ct = buf.shape[3]
    load = pltpu.make_async_copy(own_ref, own_held, own_sem)
    load.start()
    tiles = weight_ref.shape[2] // ct
    piece = out_w_ref.shape[0] // tiles

    def piece_copy(tile):
        rows = pl.ds(pl.multiple_of(tile * piece, piece), piece)
        return pltpu.make_async_copy(out_w_ref.at[rows], held_w_ref.at[rows], out_sem.at[tile])

    def use(tile, products, total):
        piece_copy(tile).start()
        for j in range(3):
            acc_ref[j, :, columns(tile, ct)] = products[j].astype(BF16)

    total = projection(first, places, [own_held, beside_ref], gain_ref, weight_ref, xg_ref, buf, sem, use, load)
    ssq_ref[...] = jnp.broadcast_to(total, ssq_ref.shape)
    for tile in range(tiles):
        piece_copy(tile).wait()


def streams(acc_ref, rows, at, products, ssq, d_model):
    scale = lax.rsqrt(ssq / d_model + 1e-06)
    query, keys, values = [((acc_ref[j, rows, at].astype(F32) + products[j]) * scale).astype(BF16) for j in range(3)]
    mixed = (keys.astype(F32) * values.astype(F32)).astype(BF16)
    return query, mixed


def gate(before, now, query, at, spec_ref, fwd_ref, inv_ref):
    window = jnp.concatenate([before, now], axis=0)
    filtered = convolved(window, spec_ref[:, at], fwd_ref[...], inv_ref[...])
    return (query.astype(F32) * filtered).astype(BF16)


def upper_kernel(first, d_model, taps, n_lhs, places, *refs):
    tokens = refs[:n_lhs]
    gain_ref, weight_ref, acc_ref, ssq_ref, spec_ref, fwd_ref, inv_ref = refs[n_lhs : n_lhs + 7]
    tail_ref, q_ref, mixed_ref, gated_ref, q_tail, xg_ref, buf, sem = refs[-8:]
    ct = buf.shape[3]
    rows = slice(2 * taps, 4 * taps)

    def finish_tile(tile):
        at = columns(tile, ct)
        gated_ref[:, at] = gate(mixed_ref[:, at], tail_ref[:, at], q_tail[:, at], at, spec_ref, fwd_ref, inv_ref)

    def use(tile, products, total):
        at = columns(tile, ct)
        finish_tile(jnp.maximum(tile - 1, 0))
        query, mixed = streams(acc_ref, rows, at, products, ssq_ref[rows, :1] + total, d_model)
        q_ref[:, at] = query[:taps]
        q_tail[:, at] = query[taps:]
        mixed_ref[:, at] = mixed[:taps]
        tail_ref[:, at] = mixed[taps:]

    projection(first, places, tokens, gain_ref, weight_ref, xg_ref, buf, sem, use)
    finish_tile(weight_ref.shape[2] // ct - 1)


def lower_kernel(first, d_model, taps, n_lhs, places, *refs):
    tokens = refs[:n_lhs]
    gain_ref, weight_ref, acc_ref, ssq_ref, spec_ref, fwd_ref, inv_ref, q_up_ref, mixed_up_ref = refs[n_lhs : n_lhs + 9]
    q_ref, mixed_ref, one_ref, two_ref, q_one, mixed_one, xg_ref, buf, sem = refs[-9:]
    ct = buf.shape[3]
    rows = slice(0, 2 * taps)

    def finish_tile(tile):
        at = columns(tile, ct)
        one_ref[:, at] = gate(mixed_ref[:, at], mixed_one[:, at], q_one[:, at], at, spec_ref, fwd_ref, inv_ref)
        two_ref[:, at] = gate(mixed_one[:, at], mixed_up_ref[:, at], q_up_ref[:, at], at, spec_ref, fwd_ref, inv_ref)

    def use(tile, products, total):
        at = columns(tile, ct)
        finish_tile(jnp.maximum(tile - 1, 0))
        query, mixed = streams(acc_ref, rows, at, products, ssq_ref[rows, :1] + total, d_model)
        q_ref[:, at] = query[:taps]
        q_one[:, at] = query[taps:]
        mixed_ref[:, at] = mixed[:taps]
        mixed_one[:, at] = mixed[taps:]

    projection(first, places, tokens, gain_ref, weight_ref, xg_ref, buf, sem, use)
    finish_tile(weight_ref.shape[2] // ct - 1)


def first_kernel(halo_ref, mixed_ref, q_ref, spec_ref, fwd_ref, inv_ref, *refs):
    gated_ref = refs[-1]
    ct = column_tile(q_ref.shape[1], 1024)
    for at in range(0, q_ref.shape[1], ct):
        at = slice(at, at + ct)
        gated_ref[:, at] = gate(halo_ref[:, at], mixed_ref[:, at], q_ref[:, at], at, spec_ref, fwd_ref, inv_ref)


def halves_kernel(x_ref, low_ref, high_ref, sem):
    half = low_ref.shape[0]
    copies = [
        pltpu.make_async_copy(x_ref.at[pl.ds(half * i, half)], ref, sem.at[i]) for i, ref in enumerate((low_ref, high_ref))
    ]
    for copy in copies:
        copy.start()
    for copy in copies:
        copy.wait()


def params(mib, steps=1):
    return pltpu.CompilerParams(dimension_semantics=("arbitrary",) * steps, vmem_limit_bytes=mib * MIB)


def in_hbm(x):
    return pltpu.with_memory_space_constraint(x, pltpu.HBM)


def in_vmem(x):
    return pltpu.with_memory_space_constraint(x, pltpu.VMEM)


RESIDENT = pl.BlockSpec(memory_space=pltpu.VMEM)


def whole(shape):
    return pl.BlockSpec(shape, lambda ch, *_: (0,) * len(shape))


def cost(rows, depth, width, extra=0):
    return pl.CostEstimate(
        flops=2 * rows * depth * width, bytes_accessed=2 * (rows * depth + depth * width) + extra, transcendentals=0
    )


def column_tile(channels, most=256):
    return most if channels % most == 0 else channels


def nothing_kernel(*refs):
    pass


def held_until(x, *others):
    return pl.pallas_call(
        nothing_kernel,
        in_specs=[pl.BlockSpec(memory_space=pl.ANY)] * (1 + len(others)),
        out_specs=pl.BlockSpec(memory_space=pl.ANY),
        out_shape=jax.ShapeDtypeStruct(x.shape, x.dtype),
        input_output_aliases={0: 0},
        compiler_params=pltpu.CompilerParams(vmem_limit_bytes=2 * MIB),
        name="held_until",
    )(x, *others)


BRIEF = pl.CostEstimate(flops=1, bytes_accessed=1, transcendentals=0)
IN_PLACE = pl.BlockSpec(memory_space=pl.ANY)
SCALARS = pl.BlockSpec(memory_space=pltpu.SMEM)


def row_halves(x):
    rows, width = x.shape
    return pl.pallas_call(
        halves_kernel,
        in_specs=[IN_PLACE],
        out_specs=[RESIDENT] * 2,
        out_shape=[pltpu.VMEM((rows // 2, width), x.dtype)] * 2,
        scratch_shapes=[pltpu.SemaphoreType.DMA((2,))],
        compiler_params=pltpu.CompilerParams(vmem_limit_bytes=4 * MIB),
        name="row_halves",
    )(in_hbm(x))


def filter_transform(filter_taps, conv_skip, of_filter, waits):
    taps, channels = filter_taps.shape
    ct = column_tile(channels, 1024)
    tile = lambda r: pl.BlockSpec((r, ct), lambda ch: (0, ch))
    return pl.pallas_call(
        spectrum_kernel,
        grid=(channels // ct,),
        in_specs=[tile(taps), tile(1), whole(of_filter.shape)] + [IN_PLACE] * len(waits),
        out_specs=tile(3 * taps),
        out_shape=pltpu.VMEM((3 * taps, channels), F32),
        compiler_params=params(16),
        cost_estimate=cost(3 * taps, 2 * taps, channels),
        name="filter_transform",
    )(in_hbm(filter_taps), in_hbm(conv_skip.reshape(1, -1)), in_hbm(of_filter), *waits)


def weight_scratch(rows, depth, channels, n_lhs, slots=3):
    ct = column_tile(channels)
    return [
        pltpu.VMEM((rows, depth * n_lhs), BF16),
        pltpu.VMEM((slots, 3, depth * n_lhs, ct), BF16),
        pltpu.SemaphoreType.DMA((slots, n_lhs)),
    ]


def weight_limit(rows, depth, channels, n_lhs, more=0, slots=3):
    held = 2 * depth * n_lhs * (rows + slots * 3 * column_tile(channels)) + more
    return pltpu.CompilerParams(vmem_limit_bytes=held + 10 * MIB)


def gain_rows(norm_gain, depth):
    return in_hbm(norm_gain.reshape(-1, 1, depth))


def project_local(own, beside, places, first, norm_gain, in_weight, out_weight):
    rows, depth = own.shape
    channels = in_weight.shape[2]
    tiles = channels // column_tile(channels)
    return pl.pallas_call(
        functools.partial(local_kernel, first),
        in_specs=[SCALARS, IN_PLACE, RESIDENT, RESIDENT, IN_PLACE, IN_PLACE],
        out_specs=[RESIDENT] * 3,
        out_shape=[
            pltpu.VMEM((3, rows, channels), BF16),
            pltpu.VMEM((rows, 128), F32),
            pltpu.VMEM(out_weight.shape, BF16),
        ],
        scratch_shapes=[pltpu.VMEM((rows, depth), BF16)]
        + weight_scratch(rows, depth, channels, 2)
        + [pltpu.SemaphoreType.DMA, pltpu.SemaphoreType.DMA((tiles,))],
        compiler_params=weight_limit(rows, depth, channels, 2, 2 * rows * depth),
        cost_estimate=cost(rows, depth * 2, 3 * channels),
        name="project_local",
    )(places, in_hbm(own), in_vmem(beside), gain_rows(norm_gain, depth), in_hbm(in_weight), in_hbm(out_weight))


def project_rest(kernel, name, lhs, places, first, norm_gain, in_weight, resident, estimate, d_model, taps, more):
    rows, depth = lhs[0].shape
    channels = in_weight.shape[2]
    return pl.pallas_call(
        functools.partial(kernel, first, d_model, taps, len(lhs)),
        in_specs=[SCALARS]
        + [RESIDENT] * (len(lhs) + 1)
        + [IN_PLACE]
        + [RESIDENT] * len(resident),
        out_specs=[RESIDENT] * 4,
        out_shape=[pltpu.VMEM((taps, channels), BF16)] * 4,
        scratch_shapes=[pltpu.VMEM((taps, channels), BF16)] * more + weight_scratch(rows, depth, channels, len(lhs)),
        compiler_params=weight_limit(rows, depth, channels, len(lhs), more * 2 * taps * channels),
        cost_estimate=estimate,
        name=name,
    )(
        places,
        *[in_vmem(x) for x in lhs],
        gain_rows(norm_gain, depth),
        in_hbm(in_weight),
        *[in_vmem(x) for x in resident],
    )


def gate_first(halo, mixed, query, spectrum, forward, inverse, waits):
    taps, channels = mixed.shape
    return pl.pallas_call(
        first_kernel,
        in_specs=[RESIDENT] * 6 + [IN_PLACE] * len(waits),
        out_specs=RESIDENT,
        out_shape=pltpu.VMEM((taps, channels), BF16),
        compiler_params=pltpu.CompilerParams(vmem_limit_bytes=16 * MIB),
        cost_estimate=BRIEF,
        name="gate_first",
    )(*[in_vmem(x) for x in (halo, mixed, query, spectrum, forward, inverse)], *waits)


def out_kernel(n_parts, n_add, n_come, first, add_first, places, *refs):
    parts, w_ref = refs[:n_parts], refs[n_parts]
    add, come = refs[n_parts + 1 : n_parts + 1 + n_add], refs[n_parts + 1 + n_add : n_parts + 1 + n_add + n_come]
    o_ref = refs[-1]
    width = o_ref.shape[-1]
    lhs = jnp.concatenate([p[...] for p in parts], axis=0)
    for g in range(o_ref.shape[0] if len(o_ref.shape) == 3 else 1):
        at = pl.ds(pl.multiple_of(places[first + g] * width, width), width)
        product = dot(lhs, w_ref[:, at])
        for x in add:
            product = product + x[add_first + g].astype(F32)
        for x in come:
            product = product + x[...].astype(F32)
        if len(o_ref.shape) == 3:
            o_ref[g] = product.astype(o_ref.dtype)
        else:
            o_ref[...] = product.astype(o_ref.dtype)


def project_out(parts, out_weight, places, first, n_groups, width, name, add=(), add_first=0, dtype=BF16, waits=()):
    rows = sum(p.shape[0] for p in parts)
    return pl.pallas_call(
        functools.partial(out_kernel, len(parts), len(add), 0, first, add_first),
        in_specs=[SCALARS] + [RESIDENT] * (len(parts) + 1 + len(add)) + [IN_PLACE] * len(waits),
        out_specs=RESIDENT,
        out_shape=pltpu.VMEM((n_groups, rows, width), dtype),
        compiler_params=pltpu.CompilerParams(vmem_limit_bytes=16 * MIB),
        cost_estimate=BRIEF,
        name=name,
    )(places, *[in_vmem(x) for x in (*parts, out_weight, *add)], *waits)


def project_last(parts, out_weight, places, first, width, name, add, add_first, come, part, n_parts):
    rows = sum(p.shape[0] for p in parts)
    return pl.pallas_call(
        functools.partial(out_kernel, len(parts), len(add), len(come), first, add_first),
        grid=(1,),
        in_specs=[SCALARS] + [RESIDENT] * (len(parts) + 1 + len(add) + len(come)),
        out_specs=pl.BlockSpec((rows, width), lambda i: (part, 0)),
        out_shape=jax.ShapeDtypeStruct((rows * n_parts, width), BF16),
        compiler_params=params(16),
        cost_estimate=BRIEF,
        name=name,
    )(places, *[in_vmem(x) for x in (*parts, out_weight, *add, *come)])


def finish_kernel(n_come, *refs):
    total = refs[0][0]
    for x in refs[1 : 1 + n_come]:
        total = total + x[...].astype(F32)
    refs[-1][...] = total.astype(refs[-1].dtype)


def finish(near, come, into, part):
    rows, width = near.shape[1:]
    return pl.pallas_call(
        functools.partial(finish_kernel, len(come)),
        grid=(1,),
        in_specs=[RESIDENT] * (1 + len(come)) + [IN_PLACE],
        out_specs=pl.BlockSpec((rows, width), lambda i: (part, 0)),
        out_shape=jax.ShapeDtypeStruct(into.shape, BF16),
        input_output_aliases={1 + len(come): 0},
        compiler_params=params(16),
        cost_estimate=BRIEF,
        name="finish",
    )(in_vmem(near), *[in_vmem(x) for x in come], into)


def on_device(tokens, norm_gain, in_weight, filter_taps, conv_skip, out_weight):
    n_row, n_col, n_seq = lax.axis_size("trow"), lax.axis_size("tcol"), lax.axis_size("seq")
    r, c = lax.axis_index("trow"), lax.axis_index("tcol")
    rows, depth = tokens.shape
    taps = filter_taps.shape[0]
    half = 2 * taps
    d_model = depth * n_row * n_col
    assert n_row == 2 and rows == 2 * half
    forward, inverse, of_filter = (jnp.asarray(m) for m in dft_matrices(taps))

    def other_core(x):
        return lax.ppermute(x, "trow", [(0, 1), (1, 0)])

    def chips_along(x, s):
        return lax.ppermute(x, "tcol", [(i, (i + s) % n_col) for i in range(n_col)])

    def block_of(row, s):
        return row * n_col + lax.rem(c + s + n_col, n_col)

    beside = other_core(tokens)
    low_rows, high_rows = row_halves(tokens)
    upper_far = [chips_along(high_rows, s) for s in range(1, n_col)]
    lower_far = [chips_along(low_rows, s) for s in range(1, n_col)]
    shifts = range(1, n_col)
    places = jnp.stack(
        [block_of(r, 0), block_of(1 - r, 0)]
        + [block_of(row, -s) for row in (r, 1 - r) for s in shifts]
        + [block_of(row, s) for row in (1 - r, r) for s in (*shifts, 0)]
    )
    n_far = n_col - 1
    far_features, theirs_far = 2, 2 * n_col
    theirs_near, mine_far = theirs_far + n_far, theirs_far + n_col
    mine_near = mine_far + n_far
    acc, ssq, held_weight = project_local(tokens, beside, places, 0, norm_gain, in_weight, out_weight)
    spectrum = filter_transform(filter_taps, conv_skip, of_filter, [ssq])
    rest = functools.partial(
        project_rest, places=places, first=far_features, norm_gain=norm_gain, in_weight=in_weight, d_model=d_model, taps=taps
    )
    upper_far = [held_until(x, ssq) for x in upper_far]
    resident = [acc, ssq, spectrum, forward, inverse]
    upper = upper_far + [other_core(x) for x in upper_far]
    tail, q_up, mixed_up, gated_up = rest(
        upper_kernel, "project_upper", upper, resident=resident, estimate=BRIEF, more=1
    )
    halo = lax.ppermute(tail, "seq", [(i, i + 1) for i in range(n_seq - 1)])
    lower_far = [held_until(x, tail) for x in lower_far]
    lower = lower_far + [other_core(x) for x in lower_far]
    q_low, mixed_low, gated_one, gated_two = rest(
        lower_kernel, "project_lower", lower, resident=resident + [q_up, mixed_up], estimate=cost(2 * taps, d_model, 3 * in_weight.shape[2]), more=2
    )
    gated_first = gate_first(halo, mixed_low, q_low, spectrum, forward, inverse, [])

    project = functools.partial(project_out, [gated_two, gated_up], held_weight, places, width=depth)
    far = other_core(project(theirs_far, n_far, name="up_theirs_far", waits=[gated_first]))
    near = project(theirs_near, 1, name="up_theirs_near")
    sent_up = project(mine_far, n_far, name="up_mine_far", add=[far], waits=[near])
    near = other_core(near)
    come_up = [chips_along(sent_up[s - 1], s) for s in shifts]

    low = [gated_first, gated_one]
    project = functools.partial(project_out, low, held_weight, places, width=depth)
    theirs = other_core(project(theirs_far, n_col, name="low_theirs", waits=[sent_up]))
    sent_low = project(mine_far, n_far, name="low_mine_far", add=[theirs])
    come_low = [chips_along(sent_low[s - 1], s) for s in shifts]

    out = project_last(
        [gated_two, gated_up], held_weight, places, mine_near, depth, "up_mine_near", [near], 0, come_up, 1, 2
    )
    near_low = project(mine_near, 1, name="low_mine_near", add=[theirs], add_first=n_far, dtype=F32, waits=come_up)
    return finish(near_low, come_low, out, 0)


def solution(mesh):
    placed = (
        P("seq", ("trow", "tcol")),
        P(),
        P(None, None, ("trow", "tcol")),
        P(None, ("trow", "tcol")),
        P(("trow", "tcol")),
        P(("trow", "tcol"), None),
    )
    return jax.shard_map(
        on_device, mesh=mesh, in_specs=placed, out_specs=P("seq", ("trow", "tcol")), check_vma=False
    )
```

```python
import functools

import jax
import jax.numpy as jnp
import numpy as np
from jax import lax
from jax.experimental import pallas as pl
from jax.experimental.pallas import tpu as pltpu
from jax.sharding import PartitionSpec as P

BF16 = jnp.bfloat16
F32 = jnp.float32
MIB = 1024 * 1024


def dft_matrices(taps):
    size = 2 * taps
    t = np.arange(size)[None, :]
    k = np.arange(taps)[:, None]
    angle = 2.0 * np.pi * ((k * t) % size) / size
    cos, sin = np.cos(angle), np.sin(angle)
    alternating = (-1.0) ** t
    forward = np.concatenate([cos, alternating, -sin[1:]], axis=0)
    inverse = np.concatenate([cos[:1], 2.0 * cos[1:], alternating, -2.0 * sin[1:]], axis=0).T / size
    short = slice(0, taps)
    of_filter = np.concatenate(
        [cos[:, short], 0.0 * sin[:1, short], -sin[1:, short], alternating[:, short], cos[1:, short]], axis=0
    )
    of_filter = np.concatenate([of_filter, of_filter], axis=1)
    return forward.astype(BF16), inverse[taps:].astype(BF16), of_filter.astype(BF16)


def dot(a, b):
    return jnp.dot(a, b, preferred_element_type=F32)


def spectrum_kernel(taps_ref, skip_ref, of_filter_ref, *refs):
    spec_ref = refs[-1]
    h = taps_ref[...]
    first = lax.broadcasted_iota(jnp.int32, h.shape, 0) == 0
    h = h + jnp.where(first, skip_ref[...], 0.0)
    high = h.astype(BF16)
    low = (h - high.astype(F32)).astype(BF16)
    spec_ref[...] = dot(of_filter_ref[...], jnp.concatenate([high, low], axis=0))


def convolved(window, spectrum, forward, inverse):
    half = window.shape[0] // 2
    x = dot(forward, window)
    xa, xb = x[:half], x[half:]
    ha, hb, hc = spectrum[:half], spectrum[half : 2 * half], spectrum[2 * half :]
    y = jnp.concatenate([xa * ha - xb * hb, xa * hb + xb * hc], axis=0)
    return dot(inverse, y.astype(BF16))


def columns(step, ct):
    return pl.ds(pl.multiple_of(step * ct, ct), ct)


def projection(first, places, tokens, gain_ref, weight_ref, xg_ref, buf, sem, use, before=None):
    slots, _, _, ct = buf.shape
    depth = tokens[0].shape[1]
    tiles = weight_ref.shape[2] // ct

    def copies(tile, slot):
        return [
            pltpu.make_async_copy(
                weight_ref.at[:, pl.ds(pl.multiple_of(places[first + i] * depth, depth), depth), columns(tile, ct)],
                buf.at[slot, :, pl.ds(i * depth, depth)],
                sem.at[slot, i],
            )
            for i in range(len(tokens))
        ]

    for tile in range(min(slots - 1, tiles)):
        for copy in copies(tile, tile):
            copy.start()
    total = jnp.zeros((xg_ref.shape[0], 1), F32)
    for i, x_ref in reversed(list(enumerate(tokens))):
        if i == 0 and before is not None:
            before.wait()
        x = x_ref[...].astype(F32)
        total = total + jnp.sum(x * x, axis=1, keepdims=True)
        xg_ref[:, i * depth : (i + 1) * depth] = (x * gain_ref[places[first + i]]).astype(BF16)

    def step(tile, _):
        slot = lax.rem(tile, slots)
        ahead = tile + slots - 1

        @pl.when(ahead < tiles)
        def _():
            for copy in copies(ahead, lax.rem(ahead, slots)):
                copy.start()

        for copy in copies(tile, slot):
            copy.wait()
        use(tile, [dot(xg_ref[...], buf[slot, j]) for j in range(3)], total)
        return 0

    lax.fori_loop(0, tiles, step, 0)
    return total


def local_kernel(first, places, own_ref, beside_ref, gain_ref, weight_ref, out_w_ref, acc_ref, ssq_ref, held_w_ref,
                 own_held, xg_ref, buf, sem, own_sem, out_sem):
    ct = buf.shape[3]
    load = pltpu.make_async_copy(own_ref, own_held, own_sem)
    load.start()
    tiles = weight_ref.shape[2] // ct
    piece = out_w_ref.shape[0] // tiles

    def piece_copy(tile):
        rows = pl.ds(pl.multiple_of(tile * piece, piece), piece)
        return pltpu.make_async_copy(out_w_ref.at[rows], held_w_ref.at[rows], out_sem.at[tile])

    def use(tile, products, total):
        piece_copy(tile).start()
        for j in range(3):
            acc_ref[j, :, columns(tile, ct)] = products[j].astype(BF16)

    total = projection(first, places, [own_held, beside_ref], gain_ref, weight_ref, xg_ref, buf, sem, use, load)
    ssq_ref[...] = jnp.broadcast_to(total, ssq_ref.shape)
    for tile in range(tiles):
        piece_copy(tile).wait()


def gate(before, now, query, at, spec_ref, fwd_ref, inv_ref):
    window = jnp.concatenate([before, now], axis=0)
    filtered = convolved(window, spec_ref[:, at], fwd_ref[...], inv_ref[...])
    return (query.astype(F32) * filtered).astype(BF16)


def last_kernel(first, d_model, taps, n_lhs, places, *refs):
    tokens = refs[:n_lhs]
    gain_ref, weight_ref, acc_ref, ssq_ref, spec_ref, fwd_ref, inv_ref = refs[n_lhs : n_lhs + 7]
    tail_ref, q_ref, mixed_ref, gated_ref, q_rest, mixed_rest, xg_ref, buf, sem = refs[-9:]
    channels, ct = weight_ref.shape[2], buf.shape[3]

    def use(tile, products, total):
        at = columns(tile, ct)
        scale = lax.rsqrt((ssq_ref[:, :1] + total) / d_model + 1e-06)
        query, keys, values = [((acc_ref[j, :, at].astype(F32) + products[j]) * scale).astype(BF16) for j in range(3)]
        mixed = (keys.astype(F32) * values.astype(F32)).astype(BF16)
        q_ref[:, at] = query[:taps]
        q_rest[:, at] = query[taps:]
        mixed_ref[:, at] = mixed[:taps]
        mixed_rest[:, at] = mixed[taps:]
        tail_ref[:, at] = mixed[mixed.shape[0] - taps :]

    projection(first, places, tokens, gain_ref, weight_ref, xg_ref, buf, sem, use)
    wide = column_tile(channels, 1024)
    for at in range(0, channels, wide):
        at = slice(at, at + wide)
        before = mixed_ref[:, at]
        for row in range(0, mixed_rest.shape[0], taps):
            rows = slice(row, row + taps)
            now = mixed_rest[rows, at]
            gated_ref[rows, at] = gate(before, now, q_rest[rows, at], at, spec_ref, fwd_ref, inv_ref)
            before = now


def first_kernel(halo_ref, mixed_ref, q_ref, spec_ref, fwd_ref, inv_ref, *refs):
    gated_ref = refs[-1]
    ct = column_tile(q_ref.shape[1], 1024)
    for at in range(0, q_ref.shape[1], ct):
        at = slice(at, at + ct)
        gated_ref[:, at] = gate(halo_ref[:, at], mixed_ref[:, at], q_ref[:, at], at, spec_ref, fwd_ref, inv_ref)


def params(mib, steps=1):
    return pltpu.CompilerParams(dimension_semantics=("arbitrary",) * steps, vmem_limit_bytes=mib * MIB)


def in_hbm(x):
    return pltpu.with_memory_space_constraint(x, pltpu.HBM)


def in_vmem(x):
    return pltpu.with_memory_space_constraint(x, pltpu.VMEM)


RESIDENT = pl.BlockSpec(memory_space=pltpu.VMEM)


def whole(shape):
    return pl.BlockSpec(shape, lambda ch, *_: (0,) * len(shape))


def cost(rows, depth, width, extra=0):
    return pl.CostEstimate(
        flops=2 * rows * depth * width, bytes_accessed=2 * (rows * depth + depth * width) + extra, transcendentals=0
    )


def column_tile(channels, most=256):
    return most if channels % most == 0 else channels


def nothing_kernel(*refs):
    pass


def held_until(x, *others):
    return pl.pallas_call(
        nothing_kernel,
        in_specs=[pl.BlockSpec(memory_space=pl.ANY)] * (1 + len(others)),
        out_specs=pl.BlockSpec(memory_space=pl.ANY),
        out_shape=jax.ShapeDtypeStruct(x.shape, x.dtype),
        input_output_aliases={0: 0},
        compiler_params=pltpu.CompilerParams(vmem_limit_bytes=2 * MIB),
        name="held_until",
    )(x, *others)


BRIEF = pl.CostEstimate(flops=1, bytes_accessed=1, transcendentals=0)
IN_PLACE = pl.BlockSpec(memory_space=pl.ANY)
SCALARS = pl.BlockSpec(memory_space=pltpu.SMEM)


def filter_transform(filter_taps, conv_skip, of_filter, waits):
    taps, channels = filter_taps.shape
    ct = column_tile(channels, 1024)
    tile = lambda r: pl.BlockSpec((r, ct), lambda ch: (0, ch))
    return pl.pallas_call(
        spectrum_kernel,
        grid=(channels // ct,),
        in_specs=[tile(taps), tile(1), whole(of_filter.shape)] + [IN_PLACE] * len(waits),
        out_specs=tile(3 * taps),
        out_shape=pltpu.VMEM((3 * taps, channels), F32),
        compiler_params=params(16),
        cost_estimate=cost(3 * taps, 2 * taps, channels),
        name="filter_transform",
    )(in_hbm(filter_taps), in_hbm(conv_skip.reshape(1, -1)), in_hbm(of_filter), *waits)


def weight_scratch(rows, depth, channels, n_lhs, slots=3):
    ct = column_tile(channels)
    return [
        pltpu.VMEM((rows, depth * n_lhs), BF16),
        pltpu.VMEM((slots, 3, depth * n_lhs, ct), BF16),
        pltpu.SemaphoreType.DMA((slots, n_lhs)),
    ]


def weight_limit(rows, depth, channels, n_lhs, more=0, slots=3):
    held = 2 * depth * n_lhs * (rows + slots * 3 * column_tile(channels)) + more
    return pltpu.CompilerParams(vmem_limit_bytes=held + 10 * MIB)


def gain_rows(norm_gain, depth):
    return in_hbm(norm_gain.reshape(-1, 1, depth))


def project_local(own, beside, places, first, norm_gain, in_weight, out_weight):
    rows, depth = own.shape
    channels = in_weight.shape[2]
    tiles = channels // column_tile(channels)
    return pl.pallas_call(
        functools.partial(local_kernel, first),
        in_specs=[SCALARS, IN_PLACE, RESIDENT, RESIDENT, IN_PLACE, IN_PLACE],
        out_specs=[RESIDENT] * 3,
        out_shape=[
            pltpu.VMEM((3, rows, channels), BF16),
            pltpu.VMEM((rows, 128), F32),
            pltpu.VMEM(out_weight.shape, BF16),
        ],
        scratch_shapes=[pltpu.VMEM((rows, depth), BF16)]
        + weight_scratch(rows, depth, channels, 2)
        + [pltpu.SemaphoreType.DMA, pltpu.SemaphoreType.DMA((tiles,))],
        compiler_params=weight_limit(rows, depth, channels, 2, 2 * rows * depth),
        cost_estimate=cost(rows, depth * 2, 3 * channels),
        name="project_local",
    )(places, in_hbm(own), in_vmem(beside), gain_rows(norm_gain, depth), in_hbm(in_weight), in_hbm(out_weight))


def project_last_part(lhs, places, first, norm_gain, in_weight, resident, d_model, taps):
    rows, depth = lhs[0].shape
    channels = in_weight.shape[2]
    n = len(lhs)
    rest = rows - taps
    return pl.pallas_call(
        functools.partial(last_kernel, first, d_model, taps, n),
        in_specs=[SCALARS] + [RESIDENT] * (n + 1) + [IN_PLACE] + [RESIDENT] * len(resident),
        out_specs=[RESIDENT] * 4,
        out_shape=[pltpu.VMEM((r, channels), BF16) for r in (taps, taps, taps, rest)],
        scratch_shapes=[pltpu.VMEM((rest, channels), BF16)] * 2 + weight_scratch(rows, depth, channels, n),
        compiler_params=weight_limit(rows, depth, channels, n, 4 * rest * channels),
        cost_estimate=cost(rows, depth * n, 3 * channels),
        name="project_last_part",
    )(
        places,
        *[in_vmem(x) for x in lhs],
        gain_rows(norm_gain, depth),
        in_hbm(in_weight),
        *[in_vmem(x) for x in resident],
    )


def gate_first(halo, mixed, query, spectrum, forward, inverse, waits):
    taps, channels = mixed.shape
    return pl.pallas_call(
        first_kernel,
        in_specs=[RESIDENT] * 6 + [IN_PLACE] * len(waits),
        out_specs=RESIDENT,
        out_shape=pltpu.VMEM((taps, channels), BF16),
        compiler_params=pltpu.CompilerParams(vmem_limit_bytes=16 * MIB),
        cost_estimate=BRIEF,
        name="gate_first",
    )(*[in_vmem(x) for x in (halo, mixed, query, spectrum, forward, inverse)], *waits)


def out_kernel(slices, n_add, first, add_first, places, *refs):
    n = len(slices)
    w_ref, add, o_ref = refs[n], refs[n + 1 : n + 1 + n_add], refs[-1]
    width = o_ref.shape[-1]
    lhs = [ref[part] for ref, part in zip(refs[:n], slices)]
    lhs = lhs[0] if n == 1 else jnp.concatenate(lhs, axis=0)
    for g in range(o_ref.shape[0]):
        at = pl.ds(pl.multiple_of(places[first + g] * width, width), width)
        product = dot(lhs, w_ref[:, at])
        for x in add:
            product = product + x[add_first + g].astype(F32)
        o_ref[g] = product.astype(o_ref.dtype)


def project_out(parts, out_weight, places, first, n_groups, width, name, add=(), add_first=0, dtype=BF16, waits=()):
    arrays, slices = zip(*parts)
    rows = sum(part.stop - part.start for part in slices)
    return pl.pallas_call(
        functools.partial(out_kernel, slices, len(add), first, add_first),
        in_specs=[SCALARS] + [RESIDENT] * (len(parts) + 1 + len(add)) + [IN_PLACE] * len(waits),
        out_specs=RESIDENT,
        out_shape=pltpu.VMEM((n_groups, rows, width), dtype),
        compiler_params=pltpu.CompilerParams(vmem_limit_bytes=16 * MIB),
        cost_estimate=BRIEF,
        name=name,
    )(places, *[in_vmem(x) for x in (*arrays, out_weight, *add)], *waits)


def total_kernel(slices, n_come, first_row, *refs):
    near, come = refs[: len(slices)], refs[len(slices) : len(slices) + n_come]
    out_ref, held, sem = refs[-3:]
    row = 0
    for ref, part in zip(near, slices):
        rows = slice(row, row + part.stop - part.start)
        total = ref[0, part]
        for x in come:
            total = total + x[rows].astype(F32)
        held[rows] = total.astype(BF16)
        row = rows.stop
    copy = pltpu.make_async_copy(held, out_ref.at[pl.ds(first_row, held.shape[0])], sem)
    copy.start()
    copy.wait()


def total_rows(near, come, first_row, rows, into):
    arrays, slices = zip(*near)
    part, width = come[0].shape
    given = [] if into is None else [into]
    n = len(near) + len(come)
    return pl.pallas_call(
        functools.partial(total_kernel, slices, len(come), first_row),
        in_specs=[RESIDENT] * n + [IN_PLACE] * len(given),
        out_specs=IN_PLACE,
        out_shape=jax.ShapeDtypeStruct((rows, width), BF16),
        input_output_aliases={n: 0} if given else {},
        scratch_shapes=[pltpu.VMEM((part, width), BF16), pltpu.SemaphoreType.DMA],
        compiler_params=pltpu.CompilerParams(vmem_limit_bytes=8 * MIB),
        cost_estimate=BRIEF,
        name="total_rows",
    )(*[in_vmem(x) for x in (*arrays, *come)], *given)


def on_device(tokens, norm_gain, in_weight, filter_taps, conv_skip, out_weight):
    n_row, n_col, n_seq = lax.axis_size("trow"), lax.axis_size("tcol"), lax.axis_size("seq")
    r, c = lax.axis_index("trow"), lax.axis_index("tcol")
    rows, depth = tokens.shape
    taps = filter_taps.shape[0]
    d_model = depth * n_row * n_col
    assert n_row == 2 and rows % taps == 0
    forward, inverse, of_filter = (jnp.asarray(m) for m in dft_matrices(taps))

    def other_core(x):
        return lax.ppermute(x, "trow", [(0, 1), (1, 0)])

    def chips_along(x, s):
        return lax.ppermute(x, "tcol", [(i, (i + s) % n_col) for i in range(n_col)])

    def block_of(row, s):
        return row * n_col + lax.rem(c + s + n_col, n_col)

    shifts = range(1, n_col)
    n_far = n_col - 1
    beside = other_core(tokens)
    far = [chips_along(tokens, s) for s in shifts]
    places = jnp.stack(
        [block_of(r, 0), block_of(1 - r, 0)]
        + [block_of(row, -s) for row in (r, 1 - r) for s in shifts]
        + [block_of(row, s) for row in (1 - r, r) for s in (*shifts, 0)]
    )
    theirs_far = 2 + 2 * n_far
    theirs_near, mine_far = theirs_far + n_far, theirs_far + n_col
    mine_near = mine_far + n_far
    acc, ssq, held_weight = project_local(tokens, beside, places, 0, norm_gain, in_weight, out_weight)
    spectrum = filter_transform(filter_taps, conv_skip, of_filter, [ssq])
    far = [held_until(x, ssq) for x in far]
    far = far + [other_core(x) for x in far]
    tail, q_low, mixed_low, gated_rest = project_last_part(
        far, places, 2, norm_gain, in_weight, [acc, ssq, spectrum, forward, inverse], d_model, taps
    )
    halo = lax.ppermute(tail, "seq", [(i, i + 1) for i in range(n_seq - 1)])

    project = functools.partial(project_out, out_weight=held_weight, places=places, width=depth)

    half = rows // 2
    rest = [(gated_rest, slice(0, rows - taps))]
    theirs = other_core(project(rest, first=theirs_far, n_groups=n_far, name="rest_theirs_far"))
    sent = project(rest, first=mine_far, n_groups=n_far, name="rest_mine_far", add=[theirs])
    come = [chips_along(sent[s - 1], s) for s in shifts]

    gated_first = gate_first(halo, mixed_low, q_low, spectrum, forward, inverse, [sent])
    only = [(gated_first, slice(0, taps))]
    theirs = other_core(project(only, first=theirs_far, n_groups=n_far, name="first_theirs_far"))
    sent_first = project(only, first=mine_far, n_groups=n_far, name="first_mine_far", add=[theirs])
    come_first = [chips_along(sent_first[s - 1], s) for s in shifts]

    upper = [(gated_rest, slice(half - taps, rows - taps))]
    lower = only + [(gated_rest, slice(0, half - taps))]
    near = []
    for part, name in ((lower, "lower"), (upper, "upper")):
        theirs = other_core(project(part, first=theirs_near, n_groups=1, name=name + "_theirs_near"))
        near.append(project(part, first=mine_near, n_groups=1, name=name + "_mine_near", add=[theirs], dtype=F32))

    out = total_rows([(near[0], slice(taps, half)), (near[1], slice(0, rows - half))], come, taps, rows, None)
    return total_rows([(near[0], slice(0, taps))], come_first, 0, rows, out)


def solution(mesh):
    placed = (
        P("seq", ("trow", "tcol")),
        P(),
        P(None, None, ("trow", "tcol")),
        P(None, ("trow", "tcol")),
        P(("trow", "tcol")),
        P(("trow", "tcol"), None),
    )
    return jax.shard_map(
        on_device, mesh=mesh, in_specs=placed, out_specs=P("seq", ("trow", "tcol")), check_vma=False
    )
```

```python
import functools

import jax
import jax.numpy as jnp
import numpy as np
from jax import lax
from jax.experimental import pallas as pl
from jax.experimental.pallas import tpu as pltpu
from jax.sharding import PartitionSpec as P

BF16 = jnp.bfloat16
F32 = jnp.float32
MIB = 1024 * 1024


def dft_matrices(taps):
    size = 2 * taps
    t = np.arange(size)[None, :]
    k = np.arange(taps)[:, None]
    angle = 2.0 * np.pi * ((k * t) % size) / size
    cos, sin = np.cos(angle), np.sin(angle)
    alternating = (-1.0) ** t
    forward = np.concatenate([cos, alternating, -sin[1:]], axis=0)
    inverse = np.concatenate([cos[:1], 2.0 * cos[1:], alternating, -2.0 * sin[1:]], axis=0).T / size
    short = slice(0, taps)
    of_filter = np.concatenate(
        [cos[:, short], 0.0 * sin[:1, short], -sin[1:, short], alternating[:, short], cos[1:, short]], axis=0
    )
    of_filter = np.concatenate([of_filter, of_filter], axis=1)
    return forward.astype(BF16), inverse[taps:].astype(BF16), of_filter.astype(BF16)


def dot(a, b):
    return jnp.dot(a, b, preferred_element_type=F32)


def convolved(window, spectrum, forward, inverse):
    half = window.shape[0] // 2
    x = dot(forward, window)
    xa, xb = x[:half], x[half:]
    ha, hb, hc = spectrum[:half], spectrum[half : 2 * half], spectrum[2 * half :]
    y = jnp.concatenate([xa * ha - xb * hb, xa * hb + xb * hc], axis=0)
    return dot(inverse, y.astype(BF16))


def columns(step, ct):
    return pl.ds(pl.multiple_of(step * ct, ct), ct)


SLOTS = 3


def weight_copies(first, depth, count, places, weight_ref, ring_ref, sem, tile):
    ct = ring_ref.shape[3]
    slot = lax.rem(tile, SLOTS)
    return [
        pltpu.make_async_copy(
            weight_ref.at[:, pl.ds(pl.multiple_of(places[first + i] * depth, depth), depth), columns(tile, ct)],
            ring_ref.at[slot, :, pl.ds(i * depth, depth)],
            sem.at[slot, i],
        )
        for i in range(count)
    ]


def scaled(x_ref, gain, xg_ref, at):
    x = x_ref[...].astype(F32)
    xg_ref[:, at] = (x * gain).astype(BF16)
    return jnp.sum(x * x, axis=1, keepdims=True)


def products(copies, tiles, xg_ref, ring_ref, loaded, use):
    ahead = min(SLOTS - 1, tiles)

    def step(tile, _):
        @pl.when(tile + ahead < tiles)
        def _():
            for copy in copies(tile + ahead):
                copy.start()

        @pl.when(tile >= loaded)
        def _():
            for copy in copies(tile):
                copy.wait()

        slot = lax.rem(tile, SLOTS)
        use(tile, [dot(xg_ref[...], ring_ref[slot, j]) for j in range(3)])
        return 0

    lax.fori_loop(0, tiles, step, 0)


def local_kernel(first, places, own_ref, beside_ref, gain_ref, weight_ref, out_w_ref, acc_ref, ssq_ref, held_w_ref,
                 own_held, xg_ref, ring_ref, sem, own_sem, out_sem):
    ct, depth = ring_ref.shape[3], own_ref.shape[1]
    tiles = weight_ref.shape[2] // ct
    piece = out_w_ref.shape[0] // tiles
    copies = functools.partial(weight_copies, first, depth, 2, places, weight_ref, ring_ref, sem)

    def piece_copy(tile):
        rows = pl.ds(pl.multiple_of(tile * piece, piece), piece)
        return pltpu.make_async_copy(out_w_ref.at[rows], held_w_ref.at[rows], out_sem.at[tile])

    def use(tile, streams):
        piece_copy(tile).start()
        for j in range(3):
            acc_ref[j, :, columns(tile, ct)] = streams[j].astype(BF16)

    load = pltpu.make_async_copy(own_ref, own_held, own_sem)
    load.start()
    for tile in range(min(SLOTS - 1, tiles)):
        for copy in copies(tile):
            copy.start()
    total = scaled(beside_ref, gain_ref[places[first + 1]], xg_ref, slice(depth, 2 * depth))
    load.wait()
    total = total + scaled(own_held, gain_ref[places[first]], xg_ref, slice(0, depth))
    ssq_ref[...] = jnp.broadcast_to(total, ssq_ref.shape)
    products(copies, tiles, xg_ref, ring_ref, 0, use)
    for tile in range(tiles):
        piece_copy(tile).wait()


def ready_kernel(first, depth, count, places, taps_ref, skip_ref, of_filter_ref, weight_ref, _, spec_ref, ring_ref,
                 taps_held, taps_sem, sem):
    load = pltpu.make_async_copy(taps_ref, taps_held, taps_sem)
    load.start()
    tiles = weight_ref.shape[2] // ring_ref.shape[3]
    copies = functools.partial(weight_copies, first, depth, count, places, weight_ref, ring_ref, sem)
    ahead = min(SLOTS - 1, tiles)
    for tile in range(ahead):
        for copy in copies(tile):
            copy.start()
    load.wait()
    channels = taps_ref.shape[1]
    wide = column_tile(channels, 512)
    for at in range(0, channels, wide):
        at = slice(at, at + wide)
        h = taps_held[:, at]
        at_first = lax.broadcasted_iota(jnp.int32, h.shape, 0) == 0
        h = h + jnp.where(at_first, skip_ref[:, at], 0.0)
        high = h.astype(BF16)
        low = (h - high.astype(F32)).astype(BF16)
        spec_ref[:, at] = dot(of_filter_ref[...], jnp.concatenate([high, low], axis=0))
    for tile in range(ahead):
        for copy in copies(tile):
            copy.wait()


def scaled_kernel(first, n_lhs, places, *refs):
    tokens = refs[:n_lhs]
    gain_ref, ssq_in_ref, xg_ref, ssq_ref = refs[n_lhs:]
    depth = tokens[0].shape[1]
    total = ssq_in_ref[...]
    for i, x_ref in enumerate(tokens):
        total = total + scaled(x_ref, gain_ref[places[first + i]], xg_ref, slice(i * depth, (i + 1) * depth))
    ssq_ref[...] = total


def gate(before, now, query, at, spec_ref, fwd_ref, inv_ref):
    window = jnp.concatenate([before, now], axis=0)
    filtered = convolved(window, spec_ref[:, at], fwd_ref[...], inv_ref[...])
    return (query.astype(F32) * filtered).astype(BF16)


def last_kernel(first, d_model, taps, n_lhs, places, *refs):
    tokens = refs[:n_lhs]
    gain_ref, weight_ref, acc_ref, ssq_ref, spec_ref, fwd_ref, inv_ref, _, _ = refs[n_lhs : n_lhs + 9]
    tail_ref, q_ref, mixed_ref, gated_ref, xg_ref, ring_ref, q_rest, mixed_rest, sem = refs[n_lhs + 9 :]
    channels, ct = weight_ref.shape[2], ring_ref.shape[3]
    tiles = channels // ct
    depth = tokens[0].shape[1]
    copies = functools.partial(weight_copies, first, depth, 2 * n_lhs, places, weight_ref, ring_ref, sem)

    total = ssq_ref[:, :1]
    for i, x_ref in enumerate(tokens, n_lhs):
        total = total + scaled(x_ref, gain_ref[places[first + i]], xg_ref, slice(i * depth, (i + 1) * depth))
    scale = lax.rsqrt(total / d_model + 1e-06)

    def use(tile, streams):
        at = columns(tile, ct)
        query, keys, values = [((acc_ref[j, :, at].astype(F32) + streams[j]) * scale).astype(BF16) for j in range(3)]
        mixed = (keys.astype(F32) * values.astype(F32)).astype(BF16)
        q_ref[:, at] = query[:taps]
        q_rest[:, at] = query[taps:]
        mixed_ref[:, at] = mixed[:taps]
        mixed_rest[:, at] = mixed[taps:]
        tail_ref[:, at] = mixed[mixed.shape[0] - taps :]

    products(copies, tiles, xg_ref, ring_ref, min(SLOTS - 1, tiles), use)
    wide = column_tile(channels, 1024)
    for at in range(0, channels, wide):
        at = slice(at, at + wide)
        before = mixed_ref[:, at]
        for row in range(0, mixed_rest.shape[0], taps):
            rows = slice(row, row + taps)
            now = mixed_rest[rows, at]
            gated_ref[rows, at] = gate(before, now, q_rest[rows, at], at, spec_ref, fwd_ref, inv_ref)
            before = now


def block_columns(places, first, group, width, piece=0, pieces=1):
    return pl.ds(pl.multiple_of((places[first + group] * pieces + piece) * width, width), width)


def first_kernel(has_before, first, places, halo_ref, mixed_ref, q_ref, spec_ref, fwd_ref, inv_ref, w_ref, *refs):
    gated_ref, far_ref = refs[-2:]
    channels = q_ref.shape[1]
    ct = column_tile(channels, 1024)
    for at in range(0, channels, ct):
        at = slice(at, at + ct)
        before = jnp.where(places[has_before] > 0, halo_ref[:, at].astype(F32), 0.0).astype(BF16)
        gated_ref[:, at] = gate(before, mixed_ref[:, at], q_ref[:, at], at, spec_ref, fwd_ref, inv_ref)
    n_far, _, width = far_ref.shape
    for g in range(n_far):
        far_ref[g] = dot(gated_ref[...], w_ref[:, block_columns(places, first, g, width)]).astype(BF16)


def params(mib, steps=1):
    return pltpu.CompilerParams(dimension_semantics=("arbitrary",) * steps, vmem_limit_bytes=mib * MIB)


def in_hbm(x):
    return pltpu.with_memory_space_constraint(x, pltpu.HBM)


def in_vmem(x):
    return pltpu.with_memory_space_constraint(x, pltpu.VMEM)


RESIDENT = pl.BlockSpec(memory_space=pltpu.VMEM)


def whole(shape):
    return pl.BlockSpec(shape, lambda ch, *_: (0,) * len(shape))


def cost(rows, depth, width, extra=0):
    return pl.CostEstimate(
        flops=2 * rows * depth * width, bytes_accessed=2 * (rows * depth + depth * width) + extra, transcendentals=0
    )


def column_tile(channels, most=256):
    return most if channels % most == 0 else channels


def nothing_kernel(*refs):
    pass


def held_until(x, *others):
    return pl.pallas_call(
        nothing_kernel,
        in_specs=[pl.BlockSpec(memory_space=pl.ANY)] * (1 + len(others)),
        out_specs=pl.BlockSpec(memory_space=pl.ANY),
        out_shape=jax.ShapeDtypeStruct(x.shape, x.dtype),
        input_output_aliases={0: 0},
        compiler_params=pltpu.CompilerParams(vmem_limit_bytes=2 * MIB),
        name="held_until",
    )(x, *others)


BRIEF = pl.CostEstimate(flops=1, bytes_accessed=1, transcendentals=0)
IN_PLACE = pl.BlockSpec(memory_space=pl.ANY)
SCALARS = pl.BlockSpec(memory_space=pltpu.SMEM)


def ring_of(depth, channels):
    return pltpu.VMEM((SLOTS, 3, depth, column_tile(channels)), BF16)


def gain_rows(norm_gain, depth):
    return in_hbm(norm_gain.reshape(-1, 1, depth))


def project_local(own, beside, places, first, norm_gain, in_weight, out_weight):
    rows, depth = own.shape
    channels = in_weight.shape[2]
    ct = column_tile(channels)
    held = 2 * (rows * depth * 3 + SLOTS * 3 * 2 * depth * ct)
    return pl.pallas_call(
        functools.partial(local_kernel, first),
        in_specs=[SCALARS, IN_PLACE, RESIDENT, RESIDENT, IN_PLACE, IN_PLACE],
        out_specs=[RESIDENT] * 3,
        out_shape=[
            pltpu.VMEM((3, rows, channels), BF16),
            pltpu.VMEM((rows, 128), F32),
            pltpu.VMEM(out_weight.shape, BF16),
        ],
        scratch_shapes=[
            pltpu.VMEM((rows, depth), BF16),
            pltpu.VMEM((rows, 2 * depth), BF16),
            ring_of(2 * depth, channels),
            pltpu.SemaphoreType.DMA((SLOTS, 2)),
            pltpu.SemaphoreType.DMA,
            pltpu.SemaphoreType.DMA((channels // ct,)),
        ],
        compiler_params=pltpu.CompilerParams(vmem_limit_bytes=held + 10 * MIB),
        cost_estimate=cost(rows, depth * 2, 3 * channels),
        name="project_local",
    )(places, in_hbm(own), in_vmem(beside), gain_rows(norm_gain, depth), in_hbm(in_weight), in_hbm(out_weight))


def get_ready(places, first, depth, count, filter_taps, conv_skip, of_filter, in_weight, wait):
    taps, channels = filter_taps.shape
    return pl.pallas_call(
        functools.partial(ready_kernel, first, depth, count),
        in_specs=[SCALARS, IN_PLACE, RESIDENT, RESIDENT, IN_PLACE, IN_PLACE],
        out_specs=[RESIDENT] * 2,
        out_shape=[pltpu.VMEM((3 * taps, channels), F32), ring_of(depth * count, channels)],
        scratch_shapes=[
            pltpu.VMEM((taps, channels), F32),
            pltpu.SemaphoreType.DMA,
            pltpu.SemaphoreType.DMA((SLOTS, count)),
        ],
        compiler_params=pltpu.CompilerParams(vmem_limit_bytes=8 * MIB),
        cost_estimate=BRIEF,
        name="get_ready",
    )(places, in_hbm(filter_taps), conv_skip.reshape(1, -1), of_filter, in_hbm(in_weight), wait)


def scale_far(far, places, first, norm_gain, ssq):
    n, (rows, depth) = len(far), far[0].shape
    return pl.pallas_call(
        functools.partial(scaled_kernel, first, n),
        in_specs=[SCALARS] + [RESIDENT] * (n + 2),
        out_specs=[RESIDENT] * 2,
        out_shape=[pltpu.VMEM((rows, 2 * n * depth), BF16), pltpu.VMEM(ssq.shape, F32)],
        compiler_params=pltpu.CompilerParams(vmem_limit_bytes=8 * MIB),
        cost_estimate=BRIEF,
        name="scale_far",
    )(places, *[in_vmem(x) for x in far], gain_rows(norm_gain, depth), in_vmem(ssq))


def project_rest(lhs, places, first, norm_gain, in_weight, resident, xg, ring, d_model, taps):
    n, (rows, depth) = len(lhs), lhs[0].shape
    channels = in_weight.shape[2]
    rest = rows - taps
    at = n + 3 + len(resident)
    out = pl.pallas_call(
        functools.partial(last_kernel, first, d_model, taps, n),
        in_specs=[SCALARS] + [RESIDENT] * (n + 1) + [IN_PLACE] + [RESIDENT] * (len(resident) + 2),
        out_specs=[RESIDENT] * 6,
        out_shape=[pltpu.VMEM((r, channels), BF16) for r in (taps, taps, taps, rest)]
        + [pltpu.VMEM(x.shape, BF16) for x in (xg, ring)],
        input_output_aliases={at: 4, at + 1: 5},
        scratch_shapes=[pltpu.VMEM((rest, channels), BF16)] * 2 + [pltpu.SemaphoreType.DMA((SLOTS, 2 * n))],
        compiler_params=pltpu.CompilerParams(vmem_limit_bytes=4 * rest * channels + 10 * MIB),
        cost_estimate=cost(rows, d_model // 2, 3 * channels),
        name="project_rest",
    )(
        places,
        *[in_vmem(x) for x in lhs],
        gain_rows(norm_gain, depth),
        in_hbm(in_weight),
        *[in_vmem(x) for x in (*resident, xg, ring)],
    )
    return out[:4]


def gate_first(halo, mixed, query, spectrum, forward, inverse, out_weight, places, has_before, first, n_far, width, waits):
    taps, channels = mixed.shape
    resident = (halo, mixed, query, spectrum, forward, inverse, out_weight)
    return pl.pallas_call(
        functools.partial(first_kernel, has_before, first),
        in_specs=[SCALARS] + [RESIDENT] * len(resident) + [IN_PLACE] * len(waits),
        out_specs=[RESIDENT] * 2,
        out_shape=[pltpu.VMEM((taps, channels), BF16), pltpu.VMEM((n_far, taps, width), BF16)],
        compiler_params=pltpu.CompilerParams(vmem_limit_bytes=12 * MIB),
        cost_estimate=BRIEF,
        name="gate_first",
    )(places, *[in_vmem(x) for x in resident], *waits)


def out_kernel(n_add, first, piece, pieces, places, *refs):
    part_ref, w_ref, add, o_ref = refs[0], refs[1], refs[2 : 2 + n_add], refs[-1]
    width = o_ref.shape[-1]
    for g in range(o_ref.shape[0]):
        at = block_columns(places, first, g, width, piece, pieces)
        product = dot(part_ref[...], w_ref[:, at])
        for x in add:
            product = product + x[g].astype(F32)
        o_ref[g] = product.astype(o_ref.dtype)


def project_out(part, out_weight, places, first, n_groups, width, name, add=(), dtype=BF16, waits=(), piece=0, pieces=1):
    rows = part.shape[0]
    return pl.pallas_call(
        functools.partial(out_kernel, len(add), first, piece, pieces),
        in_specs=[SCALARS] + [RESIDENT] * (2 + len(add)) + [IN_PLACE] * len(waits),
        out_specs=RESIDENT,
        out_shape=pltpu.VMEM((n_groups, rows, width // pieces), dtype),
        compiler_params=pltpu.CompilerParams(vmem_limit_bytes=12 * MIB),
        cost_estimate=BRIEF,
        name=name,
    )(places, *[in_vmem(x) for x in (part, out_weight, *add)], *waits)


def total_kernel(n_near, n_come, first_row, *refs):
    near, come = refs[:n_near], refs[n_near : n_near + n_come]
    out_ref, held, sem = refs[-3:]
    width = held.shape[1] // n_near
    for i, x_ref in enumerate(near):
        at = slice(i * width, (i + 1) * width)
        total = x_ref[0]
        for x in come:
            total = total + x[:, at].astype(F32)
        held[:, at] = total.astype(BF16)
    copy = pltpu.make_async_copy(held, out_ref.at[pl.ds(first_row, held.shape[0])], sem)
    copy.start()
    copy.wait()


def total_rows(near, come, first_row, rows, into):
    part, width = come[0].shape
    given = [] if into is None else [into]
    n = len(near) + len(come)
    return pl.pallas_call(
        functools.partial(total_kernel, len(near), len(come), first_row),
        in_specs=[RESIDENT] * n + [IN_PLACE] * len(given),
        out_specs=IN_PLACE,
        out_shape=jax.ShapeDtypeStruct((rows, width), BF16),
        input_output_aliases={n: 0} if given else {},
        scratch_shapes=[pltpu.VMEM((part, width), BF16), pltpu.SemaphoreType.DMA],
        compiler_params=pltpu.CompilerParams(vmem_limit_bytes=8 * MIB),
        cost_estimate=BRIEF,
        name="total_rows",
    )(*[in_vmem(x) for x in (*near, *come)], *given)


def on_device(tokens, norm_gain, in_weight, filter_taps, conv_skip, out_weight):
    n_row, n_col, n_seq = lax.axis_size("trow"), lax.axis_size("tcol"), lax.axis_size("seq")
    r, c = lax.axis_index("trow"), lax.axis_index("tcol")
    rows, depth = tokens.shape
    taps = filter_taps.shape[0]
    d_model = depth * n_row * n_col
    assert n_row == 2 and rows % taps == 0
    forward, inverse, of_filter = (jnp.asarray(m) for m in dft_matrices(taps))

    def other_core(x):
        return lax.ppermute(x, "trow", [(0, 1), (1, 0)])

    def chips_along(x, s):
        return lax.ppermute(x, "tcol", [(i, (i + s) % n_col) for i in range(n_col)])

    def block_of(row, s):
        return row * n_col + lax.rem(c + s + n_col, n_col)

    shifts = range(1, n_col)
    n_far = n_col - 1
    beside = other_core(tokens)
    far = [chips_along(tokens, s) for s in shifts]
    places = jnp.stack(
        [block_of(r, 0), block_of(1 - r, 0)]
        + [block_of(row, -s) for row in (r, 1 - r) for s in shifts]
        + [block_of(row, s) for row in (1 - r, r) for s in (*shifts, 0)]
        + [jnp.minimum(lax.axis_index("seq"), 1)]
    )
    has_before = 2 + 4 * n_far + 2
    theirs_far = 2 + 2 * n_far
    theirs_near, mine_far = theirs_far + n_far, theirs_far + n_col
    mine_near = mine_far + n_far
    acc, ssq, held_weight = project_local(tokens, beside, places, 0, norm_gain, in_weight, out_weight)
    spectrum, ring = get_ready(places, 2, depth, 2 * n_far, filter_taps, conv_skip, of_filter, in_weight, ssq)
    far = [held_until(x, spectrum) for x in far]
    lhs = [other_core(x) for x in far]
    xg, ssq = scale_far(far, places, 2, norm_gain, ssq)
    resident = [acc, ssq, spectrum, forward, inverse]
    tail, q_low, mixed_low, gated_rest = project_rest(
        lhs, places, 2, norm_gain, in_weight, resident, xg, ring, d_model, taps
    )
    halo = lax.ppermute(tail, "seq", [(i, (i + 1) % n_seq) for i in range(n_seq)])

    project = functools.partial(project_out, out_weight=held_weight, places=places, width=depth)

    theirs = other_core(project(gated_rest, first=theirs_far, n_groups=n_far, name="rest_theirs_far"))
    sent = project(gated_rest, first=mine_far, n_groups=n_far, name="rest_mine_far", add=[theirs])
    come = [chips_along(sent[s - 1], s) for s in shifts]
    halves = [
        project(gated_rest, first=theirs_near, n_groups=1, name="rest_theirs_near", piece=i, pieces=2, waits=[sent])
        for i in range(2)
    ]

    gated_first, theirs = gate_first(
        halo, mixed_low, q_low, spectrum, forward, inverse, held_weight, places, has_before, theirs_far, n_far, depth, halves
    )
    sent_first = project(gated_first, first=mine_far, n_groups=n_far, name="first_mine_far", add=[other_core(theirs)])
    come_first = [chips_along(sent_first[s - 1], s) for s in shifts]

    near = [
        project(gated_rest, first=mine_near, n_groups=1, name="rest_mine_near", piece=i, pieces=2, add=[other_core(x)], dtype=F32)
        for i, x in enumerate(halves)
    ]
    theirs = other_core(project(gated_first, first=theirs_near, n_groups=1, name="first_theirs_near"))
    near_first = project(
        gated_first, first=mine_near, n_groups=1, name="first_mine_near", add=[theirs], dtype=F32
    )
    out = total_rows(near, come, taps, rows, None)
    return total_rows([near_first], come_first, 0, rows, out)


def solution(mesh):
    placed = (
        P("seq", ("trow", "tcol")),
        P(),
        P(None, None, ("trow", "tcol")),
        P(None, ("trow", "tcol")),
        P(("trow", "tcol")),
        P(("trow", "tcol"), None),
    )
    return jax.shard_map(
        on_device, mesh=mesh, in_specs=placed, out_specs=P("seq", ("trow", "tcol")), check_vma=False
    )
```

```python
import functools

import jax
import jax.numpy as jnp
import numpy as np
from jax import lax
from jax.experimental import pallas as pl
from jax.experimental.pallas import tpu as pltpu
from jax.sharding import PartitionSpec as P

BF16 = jnp.bfloat16
F32 = jnp.float32
MIB = 1024 * 1024


def dft_matrices(taps):
    size = 2 * taps
    t = np.arange(size)[None, :]
    k = np.arange(taps)[:, None]
    angle = 2.0 * np.pi * ((k * t) % size) / size
    cos, sin = np.cos(angle), np.sin(angle)
    alternating = (-1.0) ** t
    forward = np.concatenate([cos, alternating, -sin[1:]], axis=0)
    inverse = np.concatenate([cos[:1], 2.0 * cos[1:], alternating, -2.0 * sin[1:]], axis=0).T / size
    short = slice(0, taps)
    of_filter = np.concatenate(
        [cos[:, short], 0.0 * sin[:1, short], -sin[1:, short], alternating[:, short], cos[1:, short]], axis=0
    )
    of_filter = np.concatenate([of_filter, of_filter], axis=1)
    return forward.astype(BF16), inverse[taps:].astype(BF16), of_filter.astype(BF16)


def dot(a, b):
    return jnp.dot(a, b, preferred_element_type=F32)


def convolved(window, spectrum, forward, inverse):
    half = window.shape[0] // 2
    x = dot(forward, window)
    xa, xb = x[:half], x[half:]
    ha, hb, hc = spectrum[:half], spectrum[half : 2 * half], spectrum[2 * half :]
    y = jnp.concatenate([xa * ha - xb * hb, xa * hb + xb * hc], axis=0)
    return dot(inverse, y.astype(BF16))


def columns(step, ct):
    return pl.ds(pl.multiple_of(step * ct, ct), ct)


SLOTS = 3


def weight_copies(first, depth, count, places, weight_ref, ring_ref, sem, tile):
    ct = ring_ref.shape[3]
    slot = lax.rem(tile, SLOTS)
    return [
        pltpu.make_async_copy(
            weight_ref.at[:, pl.ds(pl.multiple_of(places[first + i] * depth, depth), depth), columns(tile, ct)],
            ring_ref.at[slot, :, pl.ds(i * depth, depth)],
            sem.at[slot, i],
        )
        for i in range(count)
    ]


def scaled(x_ref, gain, xg_ref, at):
    x = x_ref[...].astype(F32)
    xg_ref[:, at] = (x * gain).astype(BF16)
    return jnp.sum(x * x, axis=1, keepdims=True)


def products(copies, tiles, xg_ref, ring_ref, loaded, use):
    ahead = min(SLOTS - 1, tiles)

    def step(tile, _):
        @pl.when(tile + ahead < tiles)
        def _():
            for copy in copies(tile + ahead):
                copy.start()

        @pl.when(tile >= loaded)
        def _():
            for copy in copies(tile):
                copy.wait()

        slot = lax.rem(tile, SLOTS)
        use(tile, [dot(xg_ref[...], ring_ref[slot, j]) for j in range(3)])
        return 0

    lax.fori_loop(0, tiles, step, 0)


def local_kernel(first, places, own_ref, beside_ref, gain_ref, weight_ref, out_w_ref, acc_ref, ssq_ref, held_w_ref,
                 own_held, xg_ref, ring_ref, sem, own_sem, out_sem):
    ct, depth = ring_ref.shape[3], own_ref.shape[1]
    tiles = weight_ref.shape[2] // ct
    piece = out_w_ref.shape[0] // tiles
    copies = functools.partial(weight_copies, first, depth, 2, places, weight_ref, ring_ref, sem)

    def piece_copy(tile):
        rows = pl.ds(pl.multiple_of(tile * piece, piece), piece)
        return pltpu.make_async_copy(out_w_ref.at[rows], held_w_ref.at[rows], out_sem.at[tile])

    def use(tile, streams):
        piece_copy(tile).start()
        for j in range(3):
            acc_ref[j, :, columns(tile, ct)] = streams[j].astype(BF16)

    load = pltpu.make_async_copy(own_ref, own_held, own_sem)
    load.start()
    for tile in range(min(SLOTS - 1, tiles)):
        for copy in copies(tile):
            copy.start()
    total = scaled(beside_ref, gain_ref[places[first + 1]], xg_ref, slice(depth, 2 * depth))
    load.wait()
    total = total + scaled(own_held, gain_ref[places[first]], xg_ref, slice(0, depth))
    ssq_ref[...] = jnp.broadcast_to(total, ssq_ref.shape)
    products(copies, tiles, xg_ref, ring_ref, 0, use)
    for tile in range(tiles):
        piece_copy(tile).wait()


def ready_kernel(first, depth, count, places, taps_ref, skip_ref, of_filter_ref, weight_ref, _, spec_ref, ring_ref,
                 taps_held, taps_sem, sem):
    load = pltpu.make_async_copy(taps_ref, taps_held, taps_sem)
    load.start()
    tiles = weight_ref.shape[2] // ring_ref.shape[3]
    copies = functools.partial(weight_copies, first, depth, count, places, weight_ref, ring_ref, sem)
    ahead = min(SLOTS - 1, tiles)
    for tile in range(ahead):
        for copy in copies(tile):
            copy.start()
    load.wait()
    channels = taps_ref.shape[1]
    wide = column_tile(channels, 512)
    for at in range(0, channels, wide):
        at = slice(at, at + wide)
        h = taps_held[:, at]
        at_first = lax.broadcasted_iota(jnp.int32, h.shape, 0) == 0
        h = h + jnp.where(at_first, skip_ref[:, at], 0.0)
        high = h.astype(BF16)
        low = (h - high.astype(F32)).astype(BF16)
        spec_ref[:, at] = dot(of_filter_ref[...], jnp.concatenate([high, low], axis=0))
    for tile in range(ahead):
        for copy in copies(tile):
            copy.wait()


def scaled_kernel(first, n_lhs, places, *refs):
    tokens = refs[:n_lhs]
    gain_ref, ssq_in_ref, xg_ref, ssq_ref = refs[n_lhs:]
    depth = tokens[0].shape[1]
    total = ssq_in_ref[...]
    for i, x_ref in enumerate(tokens):
        total = total + scaled(x_ref, gain_ref[places[first + i]], xg_ref, slice(i * depth, (i + 1) * depth))
    ssq_ref[...] = total


def gate(before, now, query, at, spec_ref, fwd_ref, inv_ref):
    window = jnp.concatenate([before, now], axis=0)
    filtered = convolved(window, spec_ref[:, at], fwd_ref[...], inv_ref[...])
    return (query.astype(F32) * filtered).astype(BF16)


def last_kernel(first, d_model, taps, n_lhs, places, *refs):
    tokens = refs[:n_lhs]
    gain_ref, weight_ref, acc_ref, ssq_ref, spec_ref, fwd_ref, inv_ref, _, _ = refs[n_lhs : n_lhs + 9]
    tail_ref, q_ref, mixed_ref, gated_ref, xg_ref, ring_ref, q_rest, mixed_rest, sem = refs[n_lhs + 9 :]
    channels, ct = weight_ref.shape[2], ring_ref.shape[3]
    tiles = channels // ct
    depth = tokens[0].shape[1]
    copies = functools.partial(weight_copies, first, depth, 2 * n_lhs, places, weight_ref, ring_ref, sem)

    total = ssq_ref[:, :1]
    for i, x_ref in enumerate(tokens, n_lhs):
        total = total + scaled(x_ref, gain_ref[places[first + i]], xg_ref, slice(i * depth, (i + 1) * depth))
    scale = lax.rsqrt(total / d_model + 1e-06)

    def use(tile, streams):
        at = columns(tile, ct)
        query, keys, values = [((acc_ref[j, :, at].astype(F32) + streams[j]) * scale).astype(BF16) for j in range(3)]
        mixed = (keys.astype(F32) * values.astype(F32)).astype(BF16)
        q_ref[:, at] = query[:taps]
        q_rest[:, at] = query[taps:]
        mixed_ref[:, at] = mixed[:taps]
        mixed_rest[:, at] = mixed[taps:]
        tail_ref[:, at] = mixed[mixed.shape[0] - taps :]

    products(copies, tiles, xg_ref, ring_ref, min(SLOTS - 1, tiles), use)
    wide = column_tile(channels, 1024)
    for at in range(0, channels, wide):
        at = slice(at, at + wide)
        before = mixed_ref[:, at]
        for row in range(0, mixed_rest.shape[0], taps):
            rows = slice(row, row + taps)
            now = mixed_rest[rows, at]
            gated_ref[rows, at] = gate(before, now, q_rest[rows, at], at, spec_ref, fwd_ref, inv_ref)
            before = now


def block_columns(places, first, group, width, piece=0, pieces=1):
    return pl.ds(pl.multiple_of((places[first + group] * pieces + piece) * width, width), width)


def first_kernel(has_before, first, places, halo_ref, mixed_ref, q_ref, spec_ref, fwd_ref, inv_ref, w_ref, *refs):
    gated_ref, far_ref = refs[-2:]
    channels = q_ref.shape[1]
    ct = column_tile(channels, 1024)
    for at in range(0, channels, ct):
        at = slice(at, at + ct)
        before = jnp.where(places[has_before] > 0, halo_ref[:, at].astype(F32), 0.0).astype(BF16)
        gated_ref[:, at] = gate(before, mixed_ref[:, at], q_ref[:, at], at, spec_ref, fwd_ref, inv_ref)
    n_far, _, width = far_ref.shape
    for g in range(n_far):
        far_ref[g] = dot(gated_ref[...], w_ref[:, block_columns(places, first, g, width)]).astype(BF16)


def params(mib, steps=1):
    return pltpu.CompilerParams(dimension_semantics=("arbitrary",) * steps, vmem_limit_bytes=mib * MIB)


def in_hbm(x):
    return pltpu.with_memory_space_constraint(x, pltpu.HBM)


def in_vmem(x):
    return pltpu.with_memory_space_constraint(x, pltpu.VMEM)


RESIDENT = pl.BlockSpec(memory_space=pltpu.VMEM)


def whole(shape):
    return pl.BlockSpec(shape, lambda ch, *_: (0,) * len(shape))


def cost(rows, depth, width, extra=0):
    return pl.CostEstimate(
        flops=2 * rows * depth * width, bytes_accessed=2 * (rows * depth + depth * width) + extra, transcendentals=0
    )


def column_tile(channels, most=256):
    return most if channels % most == 0 else channels


def nothing_kernel(*refs):
    pass


def held_until(x, *others):
    return pl.pallas_call(
        nothing_kernel,
        in_specs=[pl.BlockSpec(memory_space=pl.ANY)] * (1 + len(others)),
        out_specs=pl.BlockSpec(memory_space=pl.ANY),
        out_shape=jax.ShapeDtypeStruct(x.shape, x.dtype),
        input_output_aliases={0: 0},
        compiler_params=pltpu.CompilerParams(vmem_limit_bytes=2 * MIB),
        name="held_until",
    )(x, *others)


BRIEF = pl.CostEstimate(flops=1, bytes_accessed=1, transcendentals=0)
IN_PLACE = pl.BlockSpec(memory_space=pl.ANY)
SCALARS = pl.BlockSpec(memory_space=pltpu.SMEM)


def ring_of(depth, channels):
    return pltpu.VMEM((SLOTS, 3, depth, column_tile(channels)), BF16)


def gain_rows(norm_gain, depth):
    return in_hbm(norm_gain.reshape(-1, 1, depth))


def project_local(own, beside, places, first, norm_gain, in_weight, out_weight):
    rows, depth = own.shape
    channels = in_weight.shape[2]
    ct = column_tile(channels)
    held = 2 * (rows * depth * 3 + SLOTS * 3 * 2 * depth * ct)
    return pl.pallas_call(
        functools.partial(local_kernel, first),
        in_specs=[SCALARS, IN_PLACE, RESIDENT, RESIDENT, IN_PLACE, IN_PLACE],
        out_specs=[RESIDENT] * 3,
        out_shape=[
            pltpu.VMEM((3, rows, channels), BF16),
            pltpu.VMEM((rows, 128), F32),
            pltpu.VMEM(out_weight.shape, BF16),
        ],
        scratch_shapes=[
            pltpu.VMEM((rows, depth), BF16),
            pltpu.VMEM((rows, 2 * depth), BF16),
            ring_of(2 * depth, channels),
            pltpu.SemaphoreType.DMA((SLOTS, 2)),
            pltpu.SemaphoreType.DMA,
            pltpu.SemaphoreType.DMA((channels // ct,)),
        ],
        compiler_params=pltpu.CompilerParams(vmem_limit_bytes=held + 10 * MIB),
        cost_estimate=cost(rows, depth * 2, 3 * channels),
        name="project_local",
    )(places, in_hbm(own), in_vmem(beside), gain_rows(norm_gain, depth), in_hbm(in_weight), in_hbm(out_weight))


def get_ready(places, first, depth, count, filter_taps, conv_skip, of_filter, in_weight, wait):
    taps, channels = filter_taps.shape
    return pl.pallas_call(
        functools.partial(ready_kernel, first, depth, count),
        in_specs=[SCALARS, IN_PLACE, RESIDENT, RESIDENT, IN_PLACE, IN_PLACE],
        out_specs=[RESIDENT] * 2,
        out_shape=[pltpu.VMEM((3 * taps, channels), F32), ring_of(depth * count, channels)],
        scratch_shapes=[
            pltpu.VMEM((taps, channels), F32),
            pltpu.SemaphoreType.DMA,
            pltpu.SemaphoreType.DMA((SLOTS, count)),
        ],
        compiler_params=pltpu.CompilerParams(vmem_limit_bytes=8 * MIB),
        cost_estimate=BRIEF,
        name="get_ready",
    )(places, in_hbm(filter_taps), conv_skip.reshape(1, -1), of_filter, in_hbm(in_weight), wait)


def scale_far(far, places, first, norm_gain, ssq):
    n, (rows, depth) = len(far), far[0].shape
    return pl.pallas_call(
        functools.partial(scaled_kernel, first, n),
        in_specs=[SCALARS] + [RESIDENT] * (n + 2),
        out_specs=[RESIDENT] * 2,
        out_shape=[pltpu.VMEM((rows, 2 * n * depth), BF16), pltpu.VMEM(ssq.shape, F32)],
        compiler_params=pltpu.CompilerParams(vmem_limit_bytes=8 * MIB),
        cost_estimate=BRIEF,
        name="scale_far",
    )(places, *[in_vmem(x) for x in far], gain_rows(norm_gain, depth), in_vmem(ssq))


def project_rest(lhs, places, first, norm_gain, in_weight, resident, xg, ring, d_model, taps):
    n, (rows, depth) = len(lhs), lhs[0].shape
    channels = in_weight.shape[2]
    rest = rows - taps
    at = n + 3 + len(resident)
    out = pl.pallas_call(
        functools.partial(last_kernel, first, d_model, taps, n),
        in_specs=[SCALARS] + [RESIDENT] * (n + 1) + [IN_PLACE] + [RESIDENT] * (len(resident) + 2),
        out_specs=[RESIDENT] * 6,
        out_shape=[pltpu.VMEM((r, channels), BF16) for r in (taps, taps, taps, rest)]
        + [pltpu.VMEM(x.shape, BF16) for x in (xg, ring)],
        input_output_aliases={at: 4, at + 1: 5},
        scratch_shapes=[pltpu.VMEM((rest, channels), BF16)] * 2 + [pltpu.SemaphoreType.DMA((SLOTS, 2 * n))],
        compiler_params=pltpu.CompilerParams(vmem_limit_bytes=4 * rest * channels + 10 * MIB),
        cost_estimate=cost(rows, d_model // 2, 3 * channels),
        name="project_rest",
    )(
        places,
        *[in_vmem(x) for x in lhs],
        gain_rows(norm_gain, depth),
        in_hbm(in_weight),
        *[in_vmem(x) for x in (*resident, xg, ring)],
    )
    return out[:4]


def gate_first(halo, mixed, query, spectrum, forward, inverse, out_weight, places, has_before, first, n_far, width, waits):
    taps, channels = mixed.shape
    resident = (halo, mixed, query, spectrum, forward, inverse, out_weight)
    return pl.pallas_call(
        functools.partial(first_kernel, has_before, first),
        in_specs=[SCALARS] + [RESIDENT] * len(resident) + [IN_PLACE] * len(waits),
        out_specs=[RESIDENT] * 2,
        out_shape=[pltpu.VMEM((taps, channels), BF16), pltpu.VMEM((n_far, taps, width), BF16)],
        compiler_params=pltpu.CompilerParams(vmem_limit_bytes=12 * MIB),
        cost_estimate=BRIEF,
        name="gate_first",
    )(places, *[in_vmem(x) for x in resident], *waits)


def out_kernel(n_add, first, piece, pieces, places, *refs):
    part_ref, w_ref, add, o_ref = refs[0], refs[1], refs[2 : 2 + n_add], refs[-1]
    width = o_ref.shape[-1]
    for g in range(o_ref.shape[0]):
        at = block_columns(places, first, g, width, piece, pieces)
        product = dot(part_ref[...], w_ref[:, at])
        if not add:
            o_ref[g] = product.astype(o_ref.dtype)
        for i, x in enumerate(add):
            at = slice(i * width // n_add, (i + 1) * width // n_add)
            o_ref[g, :, at] = (product[:, at] + x[g].astype(F32)).astype(o_ref.dtype)


def add_kernel(a_ref, b_ref, o_ref):
    o_ref[...] = (a_ref[...] + b_ref[...].astype(F32)).astype(o_ref.dtype)


def added(a, b):
    return pl.pallas_call(
        add_kernel,
        in_specs=[RESIDENT] * 2,
        out_specs=RESIDENT,
        out_shape=pltpu.VMEM(b.shape, b.dtype),
        compiler_params=pltpu.CompilerParams(vmem_limit_bytes=8 * MIB),
        cost_estimate=BRIEF,
        name="added",
    )(in_vmem(a), in_vmem(b))


def project_out(part, out_weight, places, first, n_groups, width, name, add=(), dtype=BF16, waits=(), piece=0, pieces=1):
    rows = part.shape[0]
    return pl.pallas_call(
        functools.partial(out_kernel, len(add), first, piece, pieces),
        in_specs=[SCALARS] + [RESIDENT] * (2 + len(add)) + [IN_PLACE] * len(waits),
        out_specs=RESIDENT,
        out_shape=pltpu.VMEM((n_groups, rows, width // pieces), dtype),
        compiler_params=pltpu.CompilerParams(vmem_limit_bytes=12 * MIB),
        cost_estimate=BRIEF,
        name=name,
    )(places, *[in_vmem(x) for x in (part, out_weight, *add)], *waits)


def total_kernel(n_come, first_row, *refs):
    near_ref, come = refs[0], refs[1 : 1 + n_come]
    out_ref, held, sem = refs[-3:]
    total = near_ref[0]
    for x in come:
        total = total + x[...].astype(F32)
    held[...] = total.astype(BF16)
    copy = pltpu.make_async_copy(held, out_ref.at[pl.ds(first_row, held.shape[0])], sem)
    copy.start()
    copy.wait()


def total_rows(near, come, first_row, rows, into):
    part, width = come[0].shape
    given = [] if into is None else [into]
    n = 1 + len(come)
    return pl.pallas_call(
        functools.partial(total_kernel, len(come), first_row),
        in_specs=[RESIDENT] * n + [IN_PLACE] * len(given),
        out_specs=IN_PLACE,
        out_shape=jax.ShapeDtypeStruct((rows, width), BF16),
        input_output_aliases={n: 0} if given else {},
        scratch_shapes=[pltpu.VMEM((part, width), BF16), pltpu.SemaphoreType.DMA],
        compiler_params=pltpu.CompilerParams(vmem_limit_bytes=8 * MIB),
        cost_estimate=BRIEF,
        name="total_rows",
    )(*[in_vmem(x) for x in (near, *come)], *given)


def on_device(tokens, norm_gain, in_weight, filter_taps, conv_skip, out_weight):
    n_row, n_col, n_seq = lax.axis_size("trow"), lax.axis_size("tcol"), lax.axis_size("seq")
    r, c = lax.axis_index("trow"), lax.axis_index("tcol")
    rows, depth = tokens.shape
    taps = filter_taps.shape[0]
    d_model = depth * n_row * n_col
    assert n_row == 2 and rows % taps == 0
    forward, inverse, of_filter = (jnp.asarray(m) for m in dft_matrices(taps))

    def other_core(x):
        return lax.ppermute(x, "trow", [(0, 1), (1, 0)])

    def chips_along(x, s):
        return lax.ppermute(x, "tcol", [(i, (i + s) % n_col) for i in range(n_col)])

    def block_of(row, s):
        return row * n_col + lax.rem(c + s + n_col, n_col)

    shifts = range(1, n_col)
    n_far = n_col - 1
    beside = other_core(tokens)
    far = [chips_along(tokens, s) for s in shifts]
    places = jnp.stack(
        [block_of(r, 0), block_of(1 - r, 0)]
        + [block_of(row, -s) for row in (r, 1 - r) for s in shifts]
        + [block_of(row, s) for row in (1 - r, r) for s in (*shifts, 0)]
        + [jnp.minimum(lax.axis_index("seq"), 1)]
    )
    has_before = 2 + 4 * n_far + 2
    theirs_far = 2 + 2 * n_far
    theirs_near, mine_far = theirs_far + n_far, theirs_far + n_col
    mine_near = mine_far + n_far
    acc, ssq, held_weight = project_local(tokens, beside, places, 0, norm_gain, in_weight, out_weight)
    spectrum, ring = get_ready(places, 2, depth, 2 * n_far, filter_taps, conv_skip, of_filter, in_weight, ssq)
    far = [held_until(x, spectrum) for x in far]
    lhs = [other_core(x) for x in far]
    xg, ssq = scale_far(far, places, 2, norm_gain, ssq)
    resident = [acc, ssq, spectrum, forward, inverse]
    tail, q_low, mixed_low, gated_rest = project_rest(
        lhs, places, 2, norm_gain, in_weight, resident, xg, ring, d_model, taps
    )
    halo = lax.ppermute(tail, "seq", [(i, (i + 1) % n_seq) for i in range(n_seq)])

    project = functools.partial(project_out, out_weight=held_weight, places=places, width=depth)

    theirs = other_core(project(gated_rest, first=theirs_far, n_groups=n_far, name="rest_theirs_far"))
    sent = project(gated_rest, first=mine_far, n_groups=n_far, name="rest_mine_far", add=[theirs])
    come = [chips_along(sent[s - 1], s) for s in shifts]
    halves = [
        project(gated_rest, first=theirs_near, n_groups=1, name="rest_theirs_near", piece=i, pieces=2, waits=[sent])
        for i in range(2)
    ]

    gated_first, theirs = gate_first(
        halo, mixed_low, q_low, spectrum, forward, inverse, held_weight, places, has_before, theirs_far, n_far, depth, halves
    )
    mine = project(gated_first, first=mine_far, n_groups=n_far, name="first_mine_far", dtype=F32)
    sent_first = added(mine, other_core(theirs))
    come_first = [chips_along(sent_first[s - 1], s) for s in shifts]
    halves_first = [
        project(gated_first, first=theirs_near, n_groups=1, name="first_theirs_near", piece=i, pieces=2, waits=[sent_first])
        for i in range(2)
    ]

    near, near_first = [
        project(part, first=mine_near, n_groups=1, name=name, add=[other_core(x) for x in pieces], dtype=F32)
        for part, name, pieces in (
            (gated_rest, "rest_mine_near", halves),
            (gated_first, "first_mine_near", halves_first),
        )
    ]
    out = total_rows(near, come, taps, rows, None)
    return total_rows(near_first, come_first, 0, rows, out)


def solution(mesh):
    placed = (
        P("seq", ("trow", "tcol")),
        P(),
        P(None, None, ("trow", "tcol")),
        P(None, ("trow", "tcol")),
        P(("trow", "tcol")),
        P(("trow", "tcol"), None),
    )
    return jax.shard_map(
        on_device, mesh=mesh, in_specs=placed, out_specs=P("seq", ("trow", "tcol")), check_vma=False
    )
```

```python
import functools

import jax
import jax.numpy as jnp
import numpy as np
from jax import lax
from jax.experimental import pallas as pl
from jax.experimental.pallas import tpu as pltpu
from jax.sharding import PartitionSpec as P

BF16 = jnp.bfloat16
F32 = jnp.float32
MIB = 1024 * 1024


def dft_matrices(taps):
    size = 2 * taps
    t = np.arange(size)[None, :]
    k = np.arange(taps)[:, None]
    angle = 2.0 * np.pi * ((k * t) % size) / size
    cos, sin = np.cos(angle), np.sin(angle)
    alternating = (-1.0) ** t
    forward = np.concatenate([cos, alternating, -sin[1:]], axis=0)
    inverse = np.concatenate([cos[:1], 2.0 * cos[1:], alternating, -2.0 * sin[1:]], axis=0).T / size
    short = slice(0, taps)
    of_filter = np.concatenate(
        [cos[:, short], 0.0 * sin[:1, short], -sin[1:, short], alternating[:, short], cos[1:, short]], axis=0
    )
    of_filter = np.concatenate([of_filter, of_filter], axis=1)
    return forward.astype(BF16), inverse[taps:].astype(BF16), of_filter.astype(BF16)


def dot(a, b):
    return jnp.dot(a, b, preferred_element_type=F32)


def convolved(window, spectrum, forward, inverse):
    half = window.shape[0] // 2
    x = dot(forward, window)
    xa, xb = x[:half], x[half:]
    ha, hb, hc = spectrum[:half], spectrum[half : 2 * half], spectrum[2 * half :]
    y = jnp.concatenate([xa * ha - xb * hb, xa * hb + xb * hc], axis=0)
    return dot(inverse, y.astype(BF16))


def columns(step, ct):
    return pl.ds(pl.multiple_of(step * ct, ct), ct)


SLOTS = 3


def weight_copies(first, depth, count, places, weight_ref, ring_ref, sem, tile):
    ct = ring_ref.shape[3]
    slot = lax.rem(tile, SLOTS)
    return [
        pltpu.make_async_copy(
            weight_ref.at[:, pl.ds(pl.multiple_of(places[first + i] * depth, depth), depth), columns(tile, ct)],
            ring_ref.at[slot, :, pl.ds(i * depth, depth)],
            sem.at[slot, i],
        )
        for i in range(count)
    ]


def scaled(x_ref, gain, xg_ref, at):
    x = x_ref[...].astype(F32)
    xg_ref[:, at] = (x * gain).astype(BF16)
    return jnp.sum(x * x, axis=1, keepdims=True)


def products(copies, tiles, xg_ref, ring_ref, loaded, use):
    ahead = min(SLOTS - 1, tiles)

    def step(tile, _):
        @pl.when(tile + ahead < tiles)
        def _():
            for copy in copies(tile + ahead):
                copy.start()

        @pl.when(tile >= loaded)
        def _():
            for copy in copies(tile):
                copy.wait()

        slot = lax.rem(tile, SLOTS)
        use(tile, [dot(xg_ref[...], ring_ref[slot, j]) for j in range(3)])
        return 0

    lax.fori_loop(0, tiles, step, 0)


def local_kernel(first, places, own_ref, beside_ref, gain_ref, weight_ref, out_w_ref, acc_ref, ssq_ref, held_w_ref,
                 own_held, xg_ref, ring_ref, sem, own_sem, out_sem):
    ct, depth = ring_ref.shape[3], own_ref.shape[1]
    tiles = weight_ref.shape[2] // ct
    piece = out_w_ref.shape[0] // tiles
    copies = functools.partial(weight_copies, first, depth, 2, places, weight_ref, ring_ref, sem)

    def piece_copy(tile):
        rows = pl.ds(pl.multiple_of(tile * piece, piece), piece)
        return pltpu.make_async_copy(out_w_ref.at[rows], held_w_ref.at[rows], out_sem.at[tile])

    def use(tile, streams):
        piece_copy(tile).start()
        for j in range(3):
            acc_ref[j, :, columns(tile, ct)] = streams[j].astype(BF16)

    load = pltpu.make_async_copy(own_ref, own_held, own_sem)
    load.start()
    for tile in range(min(SLOTS - 1, tiles)):
        for copy in copies(tile):
            copy.start()
    total = scaled(beside_ref, gain_ref[places[first + 1]], xg_ref, slice(depth, 2 * depth))
    load.wait()
    total = total + scaled(own_held, gain_ref[places[first]], xg_ref, slice(0, depth))
    ssq_ref[...] = jnp.broadcast_to(total, ssq_ref.shape)
    products(copies, tiles, xg_ref, ring_ref, 0, use)
    for tile in range(tiles):
        piece_copy(tile).wait()


def ready_kernel(first, depth, count, places, taps_ref, skip_ref, of_filter_ref, weight_ref, _, spec_ref, ring_ref,
                 taps_held, taps_sem, sem):
    load = pltpu.make_async_copy(taps_ref, taps_held, taps_sem)
    load.start()
    tiles = weight_ref.shape[2] // ring_ref.shape[3]
    copies = functools.partial(weight_copies, first, depth, count, places, weight_ref, ring_ref, sem)
    ahead = min(SLOTS - 1, tiles)
    for tile in range(ahead):
        for copy in copies(tile):
            copy.start()
    load.wait()
    channels = taps_ref.shape[1]
    wide = column_tile(channels, 512)
    for at in range(0, channels, wide):
        at = slice(at, at + wide)
        h = taps_held[:, at]
        at_first = lax.broadcasted_iota(jnp.int32, h.shape, 0) == 0
        h = h + jnp.where(at_first, skip_ref[:, at], 0.0)
        high = h.astype(BF16)
        low = (h - high.astype(F32)).astype(BF16)
        spec_ref[:, at] = dot(of_filter_ref[...], jnp.concatenate([high, low], axis=0))
    for tile in range(ahead):
        for copy in copies(tile):
            copy.wait()


def scaled_kernel(first, n_lhs, places, *refs):
    tokens = refs[:n_lhs]
    gain_ref, ssq_in_ref, xg_ref, ssq_ref = refs[n_lhs:]
    depth = tokens[0].shape[1]
    total = ssq_in_ref[...]
    for i, x_ref in enumerate(tokens):
        total = total + scaled(x_ref, gain_ref[places[first + i]], xg_ref, slice(i * depth, (i + 1) * depth))
    ssq_ref[...] = total


def gate(before, now, query, at, spec_ref, fwd_ref, inv_ref):
    window = jnp.concatenate([before, now], axis=0)
    filtered = convolved(window, spec_ref[:, at], fwd_ref[...], inv_ref[...])
    return (query.astype(F32) * filtered).astype(BF16)


def last_kernel(first, d_model, taps, n_lhs, places, *refs):
    tokens = refs[:n_lhs]
    gain_ref, weight_ref, acc_ref, ssq_ref, spec_ref, fwd_ref, inv_ref, _, _ = refs[n_lhs : n_lhs + 9]
    tail_ref, q_ref, mixed_ref, gated_ref, xg_ref, ring_ref, q_rest, mixed_rest, sem = refs[n_lhs + 9 :]
    channels, ct = weight_ref.shape[2], ring_ref.shape[3]
    tiles = channels // ct
    depth = tokens[0].shape[1]
    copies = functools.partial(weight_copies, first, depth, 2 * n_lhs, places, weight_ref, ring_ref, sem)

    total = ssq_ref[:, :1]
    for i, x_ref in enumerate(tokens, n_lhs):
        total = total + scaled(x_ref, gain_ref[places[first + i]], xg_ref, slice(i * depth, (i + 1) * depth))
    scale = lax.rsqrt(total / d_model + 1e-06)

    def use(tile, streams):
        at = columns(tile, ct)
        query, keys, values = [((acc_ref[j, :, at].astype(F32) + streams[j]) * scale).astype(BF16) for j in range(3)]
        mixed = (keys.astype(F32) * values.astype(F32)).astype(BF16)
        q_ref[:, at] = query[:taps]
        q_rest[:, at] = query[taps:]
        mixed_ref[:, at] = mixed[:taps]
        mixed_rest[:, at] = mixed[taps:]
        tail_ref[:, at] = mixed[mixed.shape[0] - taps :]

    products(copies, tiles, xg_ref, ring_ref, min(SLOTS - 1, tiles), use)
    wide = column_tile(channels, 2048)
    for at in range(0, channels, wide):
        at = slice(at, at + wide)
        before = mixed_ref[:, at]
        for row in range(0, mixed_rest.shape[0], taps):
            rows = slice(row, row + taps)
            now = mixed_rest[rows, at]
            gated_ref[rows, at] = gate(before, now, q_rest[rows, at], at, spec_ref, fwd_ref, inv_ref)
            before = now


def block_columns(places, first, group, width, piece=0, pieces=1):
    return pl.ds(pl.multiple_of((places[first + group] * pieces + piece) * width, width), width)


def first_kernel(has_before, first, places, halo_ref, mixed_ref, q_ref, spec_ref, fwd_ref, inv_ref, w_ref, *refs):
    gated_ref, far_ref = refs[-2:]
    channels = q_ref.shape[1]
    ct = column_tile(channels, 2048)
    for at in range(0, channels, ct):
        at = slice(at, at + ct)
        before = jnp.where(places[has_before] > 0, halo_ref[:, at].astype(F32), 0.0).astype(BF16)
        gated_ref[:, at] = gate(before, mixed_ref[:, at], q_ref[:, at], at, spec_ref, fwd_ref, inv_ref)
    n_far, _, width = far_ref.shape
    for g in range(n_far):
        far_ref[g] = dot(gated_ref[...], w_ref[:, block_columns(places, first, g, width)]).astype(BF16)


def params(mib, steps=1):
    return pltpu.CompilerParams(dimension_semantics=("arbitrary",) * steps, vmem_limit_bytes=mib * MIB)


def in_hbm(x):
    return pltpu.with_memory_space_constraint(x, pltpu.HBM)


def in_vmem(x):
    return pltpu.with_memory_space_constraint(x, pltpu.VMEM)


RESIDENT = pl.BlockSpec(memory_space=pltpu.VMEM)


def whole(shape):
    return pl.BlockSpec(shape, lambda ch, *_: (0,) * len(shape))


def cost(rows, depth, width, extra=0):
    return pl.CostEstimate(
        flops=2 * rows * depth * width, bytes_accessed=2 * (rows * depth + depth * width) + extra, transcendentals=0
    )


def column_tile(channels, most=256):
    return most if channels % most == 0 else channels


def nothing_kernel(*refs):
    pass


def held_until(x, *others):
    return pl.pallas_call(
        nothing_kernel,
        in_specs=[pl.BlockSpec(memory_space=pl.ANY)] * (1 + len(others)),
        out_specs=pl.BlockSpec(memory_space=pl.ANY),
        out_shape=jax.ShapeDtypeStruct(x.shape, x.dtype),
        input_output_aliases={0: 0},
        compiler_params=pltpu.CompilerParams(vmem_limit_bytes=2 * MIB),
        name="held_until",
    )(x, *others)


BRIEF = pl.CostEstimate(flops=1, bytes_accessed=1, transcendentals=0)
IN_PLACE = pl.BlockSpec(memory_space=pl.ANY)
SCALARS = pl.BlockSpec(memory_space=pltpu.SMEM)


def ring_of(depth, channels):
    return pltpu.VMEM((SLOTS, 3, depth, column_tile(channels)), BF16)


def gain_rows(norm_gain, depth):
    return in_hbm(norm_gain.reshape(-1, 1, depth))


def project_local(own, beside, places, first, norm_gain, in_weight, out_weight):
    rows, depth = own.shape
    channels = in_weight.shape[2]
    ct = column_tile(channels)
    held = 2 * (rows * depth * 3 + SLOTS * 3 * 2 * depth * ct)
    return pl.pallas_call(
        functools.partial(local_kernel, first),
        in_specs=[SCALARS, IN_PLACE, RESIDENT, RESIDENT, IN_PLACE, IN_PLACE],
        out_specs=[RESIDENT] * 3,
        out_shape=[
            pltpu.VMEM((3, rows, channels), BF16),
            pltpu.VMEM((rows, 128), F32),
            pltpu.VMEM(out_weight.shape, BF16),
        ],
        scratch_shapes=[
            pltpu.VMEM((rows, depth), BF16),
            pltpu.VMEM((rows, 2 * depth), BF16),
            ring_of(2 * depth, channels),
            pltpu.SemaphoreType.DMA((SLOTS, 2)),
            pltpu.SemaphoreType.DMA,
            pltpu.SemaphoreType.DMA((channels // ct,)),
        ],
        compiler_params=pltpu.CompilerParams(vmem_limit_bytes=held + 10 * MIB),
        cost_estimate=cost(rows, depth * 2, 3 * channels),
        name="project_local",
    )(places, in_hbm(own), in_vmem(beside), gain_rows(norm_gain, depth), in_hbm(in_weight), in_hbm(out_weight))


def get_ready(places, first, depth, count, filter_taps, conv_skip, of_filter, in_weight, wait):
    taps, channels = filter_taps.shape
    return pl.pallas_call(
        functools.partial(ready_kernel, first, depth, count),
        in_specs=[SCALARS, IN_PLACE, RESIDENT, RESIDENT, IN_PLACE, IN_PLACE],
        out_specs=[RESIDENT] * 2,
        out_shape=[pltpu.VMEM((3 * taps, channels), F32), ring_of(depth * count, channels)],
        scratch_shapes=[
            pltpu.VMEM((taps, channels), F32),
            pltpu.SemaphoreType.DMA,
            pltpu.SemaphoreType.DMA((SLOTS, count)),
        ],
        compiler_params=pltpu.CompilerParams(vmem_limit_bytes=8 * MIB),
        cost_estimate=BRIEF,
        name="get_ready",
    )(places, in_hbm(filter_taps), conv_skip.reshape(1, -1), of_filter, in_hbm(in_weight), wait)


def scale_far(far, places, first, norm_gain, ssq):
    n, (rows, depth) = len(far), far[0].shape
    return pl.pallas_call(
        functools.partial(scaled_kernel, first, n),
        in_specs=[SCALARS] + [RESIDENT] * (n + 2),
        out_specs=[RESIDENT] * 2,
        out_shape=[pltpu.VMEM((rows, 2 * n * depth), BF16), pltpu.VMEM(ssq.shape, F32)],
        compiler_params=pltpu.CompilerParams(vmem_limit_bytes=8 * MIB),
        cost_estimate=BRIEF,
        name="scale_far",
    )(places, *[in_vmem(x) for x in far], gain_rows(norm_gain, depth), in_vmem(ssq))


def project_rest(lhs, places, first, norm_gain, in_weight, resident, xg, ring, d_model, taps):
    n, (rows, depth) = len(lhs), lhs[0].shape
    channels = in_weight.shape[2]
    rest = rows - taps
    at = n + 3 + len(resident)
    out = pl.pallas_call(
        functools.partial(last_kernel, first, d_model, taps, n),
        in_specs=[SCALARS] + [RESIDENT] * (n + 1) + [IN_PLACE] + [RESIDENT] * (len(resident) + 2),
        out_specs=[RESIDENT] * 6,
        out_shape=[pltpu.VMEM((r, channels), BF16) for r in (taps, taps, taps, rest)]
        + [pltpu.VMEM(x.shape, BF16) for x in (xg, ring)],
        input_output_aliases={at: 4, at + 1: 5},
        scratch_shapes=[pltpu.VMEM((rest, channels), BF16)] * 2 + [pltpu.SemaphoreType.DMA((SLOTS, 2 * n))],
        compiler_params=pltpu.CompilerParams(vmem_limit_bytes=4 * rest * channels + 10 * MIB),
        cost_estimate=cost(rows, d_model // 2, 3 * channels),
        name="project_rest",
    )(
        places,
        *[in_vmem(x) for x in lhs],
        gain_rows(norm_gain, depth),
        in_hbm(in_weight),
        *[in_vmem(x) for x in (*resident, xg, ring)],
    )
    return out[:4]


def gate_first(halo, mixed, query, spectrum, forward, inverse, out_weight, places, has_before, first, n_far, width, waits):
    taps, channels = mixed.shape
    resident = (halo, mixed, query, spectrum, forward, inverse, out_weight)
    return pl.pallas_call(
        functools.partial(first_kernel, has_before, first),
        in_specs=[SCALARS] + [RESIDENT] * len(resident) + [IN_PLACE] * len(waits),
        out_specs=[RESIDENT] * 2,
        out_shape=[pltpu.VMEM((taps, channels), BF16), pltpu.VMEM((n_far, taps, width), BF16)],
        compiler_params=pltpu.CompilerParams(vmem_limit_bytes=12 * MIB),
        cost_estimate=BRIEF,
        name="gate_first",
    )(places, *[in_vmem(x) for x in resident], *waits)


def out_kernel(n_add, first, piece, pieces, places, *refs):
    part_ref, w_ref, add, o_ref = refs[0], refs[1], refs[2 : 2 + n_add], refs[-1]
    width = o_ref.shape[-1]
    for g in range(o_ref.shape[0]):
        at = block_columns(places, first, g, width, piece, pieces)
        product = dot(part_ref[...], w_ref[:, at])
        if not add:
            o_ref[g] = product.astype(o_ref.dtype)
        for i, x in enumerate(add):
            at = slice(i * width // n_add, (i + 1) * width // n_add)
            o_ref[g, :, at] = (product[:, at] + x[g].astype(F32)).astype(o_ref.dtype)


def add_kernel(a_ref, b_ref, o_ref):
    o_ref[...] = (a_ref[...] + b_ref[...].astype(F32)).astype(o_ref.dtype)


def added(a, b):
    return pl.pallas_call(
        add_kernel,
        in_specs=[RESIDENT] * 2,
        out_specs=RESIDENT,
        out_shape=pltpu.VMEM(b.shape, b.dtype),
        compiler_params=pltpu.CompilerParams(vmem_limit_bytes=8 * MIB),
        cost_estimate=BRIEF,
        name="added",
    )(in_vmem(a), in_vmem(b))


def project_out(part, out_weight, places, first, n_groups, width, name, add=(), dtype=BF16, waits=(), piece=0, pieces=1):
    rows = part.shape[0]
    return pl.pallas_call(
        functools.partial(out_kernel, len(add), first, piece, pieces),
        in_specs=[SCALARS] + [RESIDENT] * (2 + len(add)) + [IN_PLACE] * len(waits),
        out_specs=RESIDENT,
        out_shape=pltpu.VMEM((n_groups, rows, width // pieces), dtype),
        compiler_params=pltpu.CompilerParams(vmem_limit_bytes=12 * MIB),
        cost_estimate=BRIEF,
        name=name,
    )(places, *[in_vmem(x) for x in (part, out_weight, *add)], *waits)


def total_kernel(n_come, first_row, *refs):
    near_ref, come = refs[0], refs[1 : 1 + n_come]
    out_ref, held, sem = refs[-3:]
    total = near_ref[0]
    for x in come:
        total = total + x[...].astype(F32)
    held[...] = total.astype(BF16)
    copy = pltpu.make_async_copy(held, out_ref.at[pl.ds(first_row, held.shape[0])], sem)
    copy.start()
    copy.wait()


def total_rows(near, come, first_row, rows, into):
    part, width = come[0].shape
    given = [] if into is None else [into]
    n = 1 + len(come)
    return pl.pallas_call(
        functools.partial(total_kernel, len(come), first_row),
        in_specs=[RESIDENT] * n + [IN_PLACE] * len(given),
        out_specs=IN_PLACE,
        out_shape=jax.ShapeDtypeStruct((rows, width), BF16),
        input_output_aliases={n: 0} if given else {},
        scratch_shapes=[pltpu.VMEM((part, width), BF16), pltpu.SemaphoreType.DMA],
        compiler_params=pltpu.CompilerParams(vmem_limit_bytes=8 * MIB),
        cost_estimate=BRIEF,
        name="total_rows",
    )(*[in_vmem(x) for x in (near, *come)], *given)


def on_device(tokens, norm_gain, in_weight, filter_taps, conv_skip, out_weight):
    n_row, n_col, n_seq = lax.axis_size("trow"), lax.axis_size("tcol"), lax.axis_size("seq")
    r, c = lax.axis_index("trow"), lax.axis_index("tcol")
    rows, depth = tokens.shape
    taps = filter_taps.shape[0]
    d_model = depth * n_row * n_col
    assert n_row == 2 and rows % taps == 0
    forward, inverse, of_filter = (jnp.asarray(m) for m in dft_matrices(taps))

    def other_core(x):
        return lax.ppermute(x, "trow", [(0, 1), (1, 0)])

    def chips_along(x, s):
        return lax.ppermute(x, "tcol", [(i, (i + s) % n_col) for i in range(n_col)])

    def block_of(row, s):
        return row * n_col + lax.rem(c + s + n_col, n_col)

    shifts = range(1, n_col)
    n_far = n_col - 1
    beside = other_core(tokens)
    far = [chips_along(tokens, s) for s in shifts]
    places = jnp.stack(
        [block_of(r, 0), block_of(1 - r, 0)]
        + [block_of(row, -s) for row in (r, 1 - r) for s in shifts]
        + [block_of(row, s) for row in (1 - r, r) for s in (*shifts, 0)]
        + [jnp.minimum(lax.axis_index("seq"), 1)]
    )
    has_before = 2 + 4 * n_far + 2
    theirs_far = 2 + 2 * n_far
    theirs_near, mine_far = theirs_far + n_far, theirs_far + n_col
    mine_near = mine_far + n_far
    acc, ssq, held_weight = project_local(tokens, beside, places, 0, norm_gain, in_weight, out_weight)
    spectrum, ring = get_ready(places, 2, depth, 2 * n_far, filter_taps, conv_skip, of_filter, in_weight, ssq)
    far = [held_until(x, spectrum) for x in far]
    lhs = [other_core(x) for x in far]
    xg, ssq = scale_far(far, places, 2, norm_gain, ssq)
    resident = [acc, ssq, spectrum, forward, inverse]
    tail, q_low, mixed_low, gated_rest = project_rest(
        lhs, places, 2, norm_gain, in_weight, resident, xg, ring, d_model, taps
    )
    halo = lax.ppermute(tail, "seq", [(i, (i + 1) % n_seq) for i in range(n_seq)])

    project = functools.partial(project_out, out_weight=held_weight, places=places, width=depth)

    theirs = other_core(project(gated_rest, first=theirs_far, n_groups=n_far, name="rest_theirs_far"))
    sent = project(gated_rest, first=mine_far, n_groups=n_far, name="rest_mine_far", add=[theirs])
    come = [chips_along(sent[s - 1], s) for s in shifts]
    halves = [
        project(gated_rest, first=theirs_near, n_groups=1, name="rest_theirs_near", piece=i, pieces=2, waits=[sent])
        for i in range(2)
    ]

    gated_first, theirs = gate_first(
        halo, mixed_low, q_low, spectrum, forward, inverse, held_weight, places, has_before, theirs_far, n_far, depth, halves
    )
    mine = project(gated_first, first=mine_far, n_groups=n_far, name="first_mine_far", dtype=F32)
    sent_first = added(mine, other_core(theirs))
    come_first = [chips_along(sent_first[s - 1], s) for s in shifts]
    halves_first = [
        project(gated_first, first=theirs_near, n_groups=1, name="first_theirs_near", piece=i, pieces=2, waits=[sent_first])
        for i in range(2)
    ]

    near, near_first = [
        project(part, first=mine_near, n_groups=1, name=name, add=[other_core(x) for x in pieces], dtype=F32)
        for part, name, pieces in (
            (gated_rest, "rest_mine_near", halves),
            (gated_first, "first_mine_near", halves_first),
        )
    ]
    out = total_rows(near, come, taps, rows, None)
    return total_rows(near_first, come_first, 0, rows, out)


def solution(mesh):
    placed = (
        P("seq", ("trow", "tcol")),
        P(),
        P(None, None, ("trow", "tcol")),
        P(None, ("trow", "tcol")),
        P(("trow", "tcol")),
        P(("trow", "tcol"), None),
    )
    return jax.shard_map(
        on_device, mesh=mesh, in_specs=placed, out_specs=P("seq", ("trow", "tcol")), check_vma=False
    )
```

```python
import functools

import jax
import jax.numpy as jnp
import numpy as np
from jax import lax
from jax.experimental import pallas as pl
from jax.experimental.pallas import tpu as pltpu
from jax.sharding import PartitionSpec as P

BF16 = jnp.bfloat16
F32 = jnp.float32
MIB = 1024 * 1024


def dft_matrices(taps):
    size = 2 * taps
    t = np.arange(size)[None, :]
    k = np.arange(taps)[:, None]
    angle = 2.0 * np.pi * ((k * t) % size) / size
    cos, sin = np.cos(angle), np.sin(angle)
    alternating = (-1.0) ** t
    forward = np.concatenate([cos, alternating, -sin[1:]], axis=0)
    inverse = np.concatenate([cos[:1], 2.0 * cos[1:], alternating, -2.0 * sin[1:]], axis=0).T / size
    short = slice(0, taps)
    of_filter = np.concatenate(
        [cos[:, short], 0.0 * sin[:1, short], -sin[1:, short], alternating[:, short], cos[1:, short]], axis=0
    )
    of_filter = np.concatenate([of_filter, of_filter], axis=1)
    return forward.astype(BF16), inverse[taps:].astype(BF16), of_filter.astype(BF16)


def dot(a, b):
    return jnp.dot(a, b, preferred_element_type=F32)


def convolved(window, spectrum, forward, inverse):
    half = window.shape[0] // 2
    x = dot(forward, window)
    xa, xb = x[:half], x[half:]
    ha, hb, hc = spectrum[:half], spectrum[half : 2 * half], spectrum[2 * half :]
    y = jnp.concatenate([xa * ha - xb * hb, xa * hb + xb * hc], axis=0)
    return dot(inverse, y.astype(BF16))


def columns(step, ct):
    return pl.ds(pl.multiple_of(step * ct, ct), ct)


SLOTS = 3


def weight_copies(first, depth, count, places, weight_ref, ring_ref, sem, tile):
    ct = ring_ref.shape[3]
    slot = lax.rem(tile, SLOTS)
    return [
        pltpu.make_async_copy(
            weight_ref.at[:, pl.ds(pl.multiple_of(places[first + i] * depth, depth), depth), columns(tile, ct)],
            ring_ref.at[slot, :, pl.ds(i * depth, depth)],
            sem.at[slot, i],
        )
        for i in range(count)
    ]


def scaled(x_ref, gain, xg_ref, at):
    x = x_ref[...].astype(F32)
    xg_ref[:, at] = (x * gain).astype(BF16)
    return jnp.sum(x * x, axis=1, keepdims=True)


def products(copies, tiles, xg_ref, ring_ref, loaded, use):
    ahead = min(SLOTS - 1, tiles)

    def step(tile, _):
        @pl.when(tile + ahead < tiles)
        def _():
            for copy in copies(tile + ahead):
                copy.start()

        @pl.when(tile >= loaded)
        def _():
            for copy in copies(tile):
                copy.wait()

        slot = lax.rem(tile, SLOTS)
        use(tile, [dot(xg_ref[...], ring_ref[slot, j]) for j in range(3)])
        return 0

    lax.fori_loop(0, tiles, step, 0)


def local_kernel(first, places, own_ref, beside_ref, gain_ref, weight_ref, out_w_ref, acc_ref, ssq_ref, held_w_ref,
                 own_held, xg_ref, ring_ref, sem, own_sem, out_sem):
    ct, depth = ring_ref.shape[3], own_ref.shape[1]
    tiles = weight_ref.shape[2] // ct
    piece = out_w_ref.shape[0] // tiles
    copies = functools.partial(weight_copies, first, depth, 2, places, weight_ref, ring_ref, sem)

    def piece_copy(tile):
        rows = pl.ds(pl.multiple_of(tile * piece, piece), piece)
        return pltpu.make_async_copy(out_w_ref.at[rows], held_w_ref.at[rows], out_sem.at[tile])

    def use(tile, streams):
        piece_copy(tile).start()
        for j in range(3):
            acc_ref[j, :, columns(tile, ct)] = streams[j].astype(BF16)

    load = pltpu.make_async_copy(own_ref, own_held, own_sem)
    load.start()
    for tile in range(min(SLOTS - 1, tiles)):
        for copy in copies(tile):
            copy.start()
    total = scaled(beside_ref, gain_ref[places[first + 1]], xg_ref, slice(depth, 2 * depth))
    load.wait()
    total = total + scaled(own_held, gain_ref[places[first]], xg_ref, slice(0, depth))
    ssq_ref[...] = jnp.broadcast_to(total, ssq_ref.shape)
    products(copies, tiles, xg_ref, ring_ref, 0, use)
    for tile in range(tiles):
        piece_copy(tile).wait()


def ready_kernel(first, depth, count, places, taps_ref, skip_ref, of_filter_ref, weight_ref, _, spec_ref, ring_ref,
                 taps_held, taps_sem, sem):
    load = pltpu.make_async_copy(taps_ref, taps_held, taps_sem)
    load.start()
    tiles = weight_ref.shape[2] // ring_ref.shape[3]
    copies = functools.partial(weight_copies, first, depth, count, places, weight_ref, ring_ref, sem)
    ahead = min(SLOTS - 1, tiles)
    for tile in range(ahead):
        for copy in copies(tile):
            copy.start()
    load.wait()
    channels = taps_ref.shape[1]
    wide = column_tile(channels, 512)
    for at in range(0, channels, wide):
        at = slice(at, at + wide)
        h = taps_held[:, at]
        at_first = lax.broadcasted_iota(jnp.int32, h.shape, 0) == 0
        h = h + jnp.where(at_first, skip_ref[:, at], 0.0)
        high = h.astype(BF16)
        low = (h - high.astype(F32)).astype(BF16)
        spec_ref[:, at] = dot(of_filter_ref[...], jnp.concatenate([high, low], axis=0))
    for tile in range(ahead):
        for copy in copies(tile):
            copy.wait()


def scaled_kernel(first, n_lhs, places, *refs):
    tokens = refs[:n_lhs]
    gain_ref, ssq_in_ref, xg_ref, ssq_ref = refs[n_lhs:]
    depth = tokens[0].shape[1]
    total = ssq_in_ref[...]
    for i, x_ref in enumerate(tokens):
        total = total + scaled(x_ref, gain_ref[places[first + i]], xg_ref, slice(i * depth, (i + 1) * depth))
    ssq_ref[...] = total


def gate(before, now, query, at, spec_ref, fwd_ref, inv_ref):
    window = jnp.concatenate([before, now], axis=0)
    filtered = convolved(window, spec_ref[:, at], fwd_ref[...], inv_ref[...])
    return (query.astype(F32) * filtered).astype(BF16)


def last_kernel(first, d_model, taps, n_lhs, places, *refs):
    tokens = refs[:n_lhs]
    gain_ref, weight_ref, acc_ref, ssq_ref, spec_ref, fwd_ref, inv_ref, _, _ = refs[n_lhs : n_lhs + 9]
    tail_ref, q_ref, mixed_ref, gated_ref, xg_ref, ring_ref, q_rest, mixed_rest, sem = refs[n_lhs + 9 :]
    channels, ct = weight_ref.shape[2], ring_ref.shape[3]
    tiles = channels // ct
    depth = tokens[0].shape[1]
    copies = functools.partial(weight_copies, first, depth, 2 * n_lhs, places, weight_ref, ring_ref, sem)

    total = ssq_ref[:, :1]
    for i, x_ref in enumerate(tokens, n_lhs):
        total = total + scaled(x_ref, gain_ref[places[first + i]], xg_ref, slice(i * depth, (i + 1) * depth))
    scale = lax.rsqrt(total / d_model + 1e-06)

    def use(tile, streams):
        at = columns(tile, ct)
        query, keys, values = [((acc_ref[j, :, at].astype(F32) + streams[j]) * scale).astype(BF16) for j in range(3)]
        mixed = (keys.astype(F32) * values.astype(F32)).astype(BF16)
        q_ref[:, at] = query[:taps]
        q_rest[:, at] = query[taps:]
        mixed_ref[:, at] = mixed[:taps]
        mixed_rest[:, at] = mixed[taps:]
        tail_ref[:, at] = mixed[mixed.shape[0] - taps :]

    products(copies, tiles, xg_ref, ring_ref, min(SLOTS - 1, tiles), use)
    wide = column_tile(channels, 2048)
    for at in range(0, channels, wide):
        at = slice(at, at + wide)
        before = mixed_ref[:, at]
        for row in range(0, mixed_rest.shape[0], taps):
            rows = slice(row, row + taps)
            now = mixed_rest[rows, at]
            gated_ref[rows, at] = gate(before, now, q_rest[rows, at], at, spec_ref, fwd_ref, inv_ref)
            before = now


def block_columns(places, first, group, width):
    return pl.ds(pl.multiple_of(places[first + group] * width, width), width)


def first_kernel(has_before, first, places, halo_ref, mixed_ref, q_ref, spec_ref, fwd_ref, inv_ref, w_ref, *refs):
    gated_ref, far_ref = refs[-2:]
    channels = q_ref.shape[1]
    ct = column_tile(channels, 2048)
    for at in range(0, channels, ct):
        at = slice(at, at + ct)
        before = jnp.where(places[has_before] > 0, halo_ref[:, at].astype(F32), 0.0).astype(BF16)
        gated_ref[:, at] = gate(before, mixed_ref[:, at], q_ref[:, at], at, spec_ref, fwd_ref, inv_ref)
    n_far, _, width = far_ref.shape
    for g in range(n_far):
        far_ref[g] = dot(gated_ref[...], w_ref[:, block_columns(places, first, g, width)]).astype(BF16)


def params(mib, steps=1):
    return pltpu.CompilerParams(dimension_semantics=("arbitrary",) * steps, vmem_limit_bytes=mib * MIB)


def in_hbm(x):
    return pltpu.with_memory_space_constraint(x, pltpu.HBM)


def in_vmem(x):
    return pltpu.with_memory_space_constraint(x, pltpu.VMEM)


RESIDENT = pl.BlockSpec(memory_space=pltpu.VMEM)


def whole(shape):
    return pl.BlockSpec(shape, lambda ch, *_: (0,) * len(shape))


def cost(rows, depth, width, extra=0):
    return pl.CostEstimate(
        flops=2 * rows * depth * width, bytes_accessed=2 * (rows * depth + depth * width) + extra, transcendentals=0
    )


def column_tile(channels, most=256):
    return most if channels % most == 0 else channels


def nothing_kernel(*refs):
    pass


def held_until(x, *others):
    return pl.pallas_call(
        nothing_kernel,
        in_specs=[pl.BlockSpec(memory_space=pl.ANY)] * (1 + len(others)),
        out_specs=pl.BlockSpec(memory_space=pl.ANY),
        out_shape=jax.ShapeDtypeStruct(x.shape, x.dtype),
        input_output_aliases={0: 0},
        compiler_params=pltpu.CompilerParams(vmem_limit_bytes=2 * MIB),
        name="held_until",
    )(x, *others)


BRIEF = pl.CostEstimate(flops=1, bytes_accessed=1, transcendentals=0)
IN_PLACE = pl.BlockSpec(memory_space=pl.ANY)
SCALARS = pl.BlockSpec(memory_space=pltpu.SMEM)


def ring_of(depth, channels):
    return pltpu.VMEM((SLOTS, 3, depth, column_tile(channels)), BF16)


def gain_rows(norm_gain, depth):
    return in_hbm(norm_gain.reshape(-1, 1, depth))


def project_local(own, beside, places, first, norm_gain, in_weight, out_weight):
    rows, depth = own.shape
    channels = in_weight.shape[2]
    ct = column_tile(channels)
    held = 2 * (rows * depth * 3 + SLOTS * 3 * 2 * depth * ct)
    return pl.pallas_call(
        functools.partial(local_kernel, first),
        in_specs=[SCALARS, IN_PLACE, RESIDENT, RESIDENT, IN_PLACE, IN_PLACE],
        out_specs=[RESIDENT] * 3,
        out_shape=[
            pltpu.VMEM((3, rows, channels), BF16),
            pltpu.VMEM((rows, 128), F32),
            pltpu.VMEM(out_weight.shape, BF16),
        ],
        scratch_shapes=[
            pltpu.VMEM((rows, depth), BF16),
            pltpu.VMEM((rows, 2 * depth), BF16),
            ring_of(2 * depth, channels),
            pltpu.SemaphoreType.DMA((SLOTS, 2)),
            pltpu.SemaphoreType.DMA,
            pltpu.SemaphoreType.DMA((channels // ct,)),
        ],
        compiler_params=pltpu.CompilerParams(vmem_limit_bytes=held + 10 * MIB),
        cost_estimate=cost(rows, depth * 2, 3 * channels),
        name="project_local",
    )(places, in_hbm(own), in_vmem(beside), gain_rows(norm_gain, depth), in_hbm(in_weight), in_hbm(out_weight))


def get_ready(places, first, depth, count, filter_taps, conv_skip, of_filter, in_weight, wait):
    taps, channels = filter_taps.shape
    return pl.pallas_call(
        functools.partial(ready_kernel, first, depth, count),
        in_specs=[SCALARS, IN_PLACE, RESIDENT, RESIDENT, IN_PLACE, IN_PLACE],
        out_specs=[RESIDENT] * 2,
        out_shape=[pltpu.VMEM((3 * taps, channels), F32), ring_of(depth * count, channels)],
        scratch_shapes=[
            pltpu.VMEM((taps, channels), F32),
            pltpu.SemaphoreType.DMA,
            pltpu.SemaphoreType.DMA((SLOTS, count)),
        ],
        compiler_params=pltpu.CompilerParams(vmem_limit_bytes=8 * MIB),
        cost_estimate=BRIEF,
        name="get_ready",
    )(places, in_hbm(filter_taps), conv_skip.reshape(1, -1), of_filter, in_hbm(in_weight), wait)


def scale_far(far, places, first, norm_gain, ssq):
    n, (rows, depth) = len(far), far[0].shape
    return pl.pallas_call(
        functools.partial(scaled_kernel, first, n),
        in_specs=[SCALARS] + [RESIDENT] * (n + 2),
        out_specs=[RESIDENT] * 2,
        out_shape=[pltpu.VMEM((rows, 2 * n * depth), BF16), pltpu.VMEM(ssq.shape, F32)],
        compiler_params=pltpu.CompilerParams(vmem_limit_bytes=8 * MIB),
        cost_estimate=BRIEF,
        name="scale_far",
    )(places, *[in_vmem(x) for x in far], gain_rows(norm_gain, depth), in_vmem(ssq))


def project_rest(lhs, places, first, norm_gain, in_weight, resident, xg, ring, d_model, taps):
    n, (rows, depth) = len(lhs), lhs[0].shape
    channels = in_weight.shape[2]
    rest = rows - taps
    at = n + 3 + len(resident)
    out = pl.pallas_call(
        functools.partial(last_kernel, first, d_model, taps, n),
        in_specs=[SCALARS] + [RESIDENT] * (n + 1) + [IN_PLACE] + [RESIDENT] * (len(resident) + 2),
        out_specs=[RESIDENT] * 6,
        out_shape=[pltpu.VMEM((r, channels), BF16) for r in (taps, taps, taps, rest)]
        + [pltpu.VMEM(x.shape, BF16) for x in (xg, ring)],
        input_output_aliases={at: 4, at + 1: 5},
        scratch_shapes=[pltpu.VMEM((rest, channels), BF16)] * 2 + [pltpu.SemaphoreType.DMA((SLOTS, 2 * n))],
        compiler_params=pltpu.CompilerParams(vmem_limit_bytes=4 * rest * channels + 10 * MIB),
        cost_estimate=cost(rows, d_model // 2, 3 * channels),
        name="project_rest",
    )(
        places,
        *[in_vmem(x) for x in lhs],
        gain_rows(norm_gain, depth),
        in_hbm(in_weight),
        *[in_vmem(x) for x in (*resident, xg, ring)],
    )
    return out[:4]


def gate_first(halo, mixed, query, spectrum, forward, inverse, out_weight, places, has_before, first, n_far, width, waits):
    taps, channels = mixed.shape
    resident = (halo, mixed, query, spectrum, forward, inverse, out_weight)
    return pl.pallas_call(
        functools.partial(first_kernel, has_before, first),
        in_specs=[SCALARS] + [RESIDENT] * len(resident) + [IN_PLACE] * len(waits),
        out_specs=[RESIDENT] * 2,
        out_shape=[pltpu.VMEM((taps, channels), BF16), pltpu.VMEM((n_far, taps, width), BF16)],
        compiler_params=pltpu.CompilerParams(vmem_limit_bytes=12 * MIB),
        cost_estimate=BRIEF,
        name="gate_first",
    )(places, *[in_vmem(x) for x in resident], *waits)


def out_kernel(n_add, n_out, first, places, *refs):
    part_ref, w_ref, add, out = refs[0], refs[1], refs[2 : 2 + n_add], refs[-n_out:]
    width = out[0].shape[-1] * n_out
    for g in range(out[0].shape[0]):
        product = dot(part_ref[...], w_ref[:, block_columns(places, first, g, width)])
        if n_out > 1:
            for i, o_ref in enumerate(out):
                o_ref[g] = product[:, i * width // n_out : (i + 1) * width // n_out].astype(o_ref.dtype)
        elif not add:
            out[0][g] = product.astype(out[0].dtype)
        for i, x in enumerate(add):
            at = slice(i * width // n_add, (i + 1) * width // n_add)
            out[0][g, :, at] = (product[:, at] + x[g].astype(F32)).astype(out[0].dtype)


def add_kernel(a_ref, b_ref, o_ref):
    o_ref[...] = (a_ref[...] + b_ref[...].astype(F32)).astype(o_ref.dtype)


def added(a, b):
    return pl.pallas_call(
        add_kernel,
        in_specs=[RESIDENT] * 2,
        out_specs=RESIDENT,
        out_shape=pltpu.VMEM(b.shape, b.dtype),
        compiler_params=pltpu.CompilerParams(vmem_limit_bytes=8 * MIB),
        cost_estimate=BRIEF,
        name="added",
    )(in_vmem(a), in_vmem(b))


def project_out(part, out_weight, places, first, n_groups, width, name, add=(), dtype=BF16, waits=(), n_out=1):
    rows = part.shape[0]
    out = pl.pallas_call(
        functools.partial(out_kernel, len(add), n_out, first),
        in_specs=[SCALARS] + [RESIDENT] * (2 + len(add)) + [IN_PLACE] * len(waits),
        out_specs=[RESIDENT] * n_out,
        out_shape=[pltpu.VMEM((n_groups, rows, width // n_out), dtype)] * n_out,
        compiler_params=pltpu.CompilerParams(vmem_limit_bytes=12 * MIB),
        cost_estimate=BRIEF,
        name=name,
    )(places, *[in_vmem(x) for x in (part, out_weight, *add)], *waits)
    return out if n_out > 1 else out[0]


def total_kernel(n_come, first_row, *refs):
    near_ref, come = refs[0], refs[1 : 1 + n_come]
    out_ref, held, sem = refs[-3:]
    total = near_ref[0]
    for x in come:
        total = total + x[...].astype(F32)
    held[...] = total.astype(BF16)
    copy = pltpu.make_async_copy(held, out_ref.at[pl.ds(first_row, held.shape[0])], sem)
    copy.start()
    copy.wait()


def total_rows(near, come, first_row, rows, into):
    part, width = come[0].shape
    given = [] if into is None else [into]
    n = 1 + len(come)
    return pl.pallas_call(
        functools.partial(total_kernel, len(come), first_row),
        in_specs=[RESIDENT] * n + [IN_PLACE] * len(given),
        out_specs=IN_PLACE,
        out_shape=jax.ShapeDtypeStruct((rows, width), BF16),
        input_output_aliases={n: 0} if given else {},
        scratch_shapes=[pltpu.VMEM((part, width), BF16), pltpu.SemaphoreType.DMA],
        compiler_params=pltpu.CompilerParams(vmem_limit_bytes=8 * MIB),
        cost_estimate=BRIEF,
        name="total_rows",
    )(*[in_vmem(x) for x in (near, *come)], *given)


def on_device(tokens, norm_gain, in_weight, filter_taps, conv_skip, out_weight):
    n_row, n_col, n_seq = lax.axis_size("trow"), lax.axis_size("tcol"), lax.axis_size("seq")
    r, c = lax.axis_index("trow"), lax.axis_index("tcol")
    rows, depth = tokens.shape
    taps = filter_taps.shape[0]
    d_model = depth * n_row * n_col
    assert n_row == 2 and rows % taps == 0
    forward, inverse, of_filter = (jnp.asarray(m) for m in dft_matrices(taps))

    def other_core(x):
        return lax.ppermute(x, "trow", [(0, 1), (1, 0)])

    def chips_along(x, s):
        return lax.ppermute(x, "tcol", [(i, (i + s) % n_col) for i in range(n_col)])

    def block_of(row, s):
        return row * n_col + lax.rem(c + s + n_col, n_col)

    shifts = range(1, n_col)
    n_far = n_col - 1
    beside = other_core(tokens)
    far = [chips_along(tokens, s) for s in shifts]
    places = jnp.stack(
        [block_of(r, 0), block_of(1 - r, 0)]
        + [block_of(row, -s) for row in (r, 1 - r) for s in shifts]
        + [block_of(row, s) for row in (1 - r, r) for s in (*shifts, 0)]
        + [jnp.minimum(lax.axis_index("seq"), 1)]
    )
    has_before = 2 + 4 * n_far + 2
    theirs_far = 2 + 2 * n_far
    theirs_near, mine_far = theirs_far + n_far, theirs_far + n_col
    mine_near = mine_far + n_far
    acc, ssq, held_weight = project_local(tokens, beside, places, 0, norm_gain, in_weight, out_weight)
    spectrum, ring = get_ready(places, 2, depth, 2 * n_far, filter_taps, conv_skip, of_filter, in_weight, ssq)
    far = [held_until(x, spectrum) for x in far]
    lhs = [other_core(x) for x in far]
    xg, ssq = scale_far(far, places, 2, norm_gain, ssq)
    resident = [acc, ssq, spectrum, forward, inverse]
    tail, q_low, mixed_low, gated_rest = project_rest(
        lhs, places, 2, norm_gain, in_weight, resident, xg, ring, d_model, taps
    )
    halo = lax.ppermute(tail, "seq", [(i, (i + 1) % n_seq) for i in range(n_seq)])

    project = functools.partial(project_out, out_weight=held_weight, places=places, width=depth)

    theirs = other_core(project(gated_rest, first=theirs_far, n_groups=n_far, name="rest_theirs_far"))
    sent = project(gated_rest, first=mine_far, n_groups=n_far, name="rest_mine_far", add=[theirs])
    come = [chips_along(sent[s - 1], s) for s in shifts]
    halves = project(gated_rest, first=theirs_near, n_groups=1, name="rest_theirs_near", waits=[sent], n_out=2)

    gated_first, theirs = gate_first(
        halo, mixed_low, q_low, spectrum, forward, inverse, held_weight, places, has_before, theirs_far, n_far, depth, halves
    )
    mine = project(gated_first, first=mine_far, n_groups=n_far, name="first_mine_far", dtype=F32)
    sent_first = added(mine, other_core(theirs))
    come_first = [chips_along(sent_first[s - 1], s) for s in shifts]
    halves_first = project(
        gated_first, first=theirs_near, n_groups=1, name="first_theirs_near", waits=[sent_first], n_out=2
    )

    near, near_first = [
        project(part, first=mine_near, n_groups=1, name=name, add=[other_core(x) for x in pieces], dtype=F32)
        for part, name, pieces in (
            (gated_rest, "rest_mine_near", halves),
            (gated_first, "first_mine_near", halves_first),
        )
    ]
    out = total_rows(near, come, taps, rows, None)
    return total_rows(near_first, come_first, 0, rows, out)


def solution(mesh):
    placed = (
        P("seq", ("trow", "tcol")),
        P(),
        P(None, None, ("trow", "tcol")),
        P(None, ("trow", "tcol")),
        P(("trow", "tcol")),
        P(("trow", "tcol"), None),
    )
    return jax.shard_map(
        on_device, mesh=mesh, in_specs=placed, out_specs=P("seq", ("trow", "tcol")), check_vma=False
    )
```

```python
import functools

import jax
import jax.numpy as jnp
import numpy as np
from jax import lax
from jax.experimental import pallas as pl
from jax.experimental.pallas import tpu as pltpu
from jax.sharding import PartitionSpec as P

BF16 = jnp.bfloat16
F32 = jnp.float32
MIB = 1024 * 1024


def dft_matrices(taps):
    size = 2 * taps
    t = np.arange(size)[None, :]
    k = np.arange(taps)[:, None]
    angle = 2.0 * np.pi * ((k * t) % size) / size
    cos, sin = np.cos(angle), np.sin(angle)
    alternating = (-1.0) ** t
    forward = np.concatenate([cos, alternating, -sin[1:]], axis=0)
    inverse = np.concatenate([cos[:1], 2.0 * cos[1:], alternating, -2.0 * sin[1:]], axis=0).T / size
    short = slice(0, taps)
    of_filter = np.concatenate(
        [cos[:, short], 0.0 * sin[:1, short], -sin[1:, short], alternating[:, short], cos[1:, short]], axis=0
    )
    of_filter = np.concatenate([of_filter, of_filter], axis=1)
    return forward.astype(BF16), inverse[taps:].astype(BF16), of_filter.astype(BF16)


def dot(a, b):
    return jnp.dot(a, b, preferred_element_type=F32)


def convolved(window, spectrum, forward, inverse):
    half = window.shape[0] // 2
    x = dot(forward, window)
    xa, xb = x[:half], x[half:]
    ha, hb, hc = spectrum[:half], spectrum[half : 2 * half], spectrum[2 * half :]
    y = jnp.concatenate([xa * ha - xb * hb, xa * hb + xb * hc], axis=0)
    return dot(inverse, y.astype(BF16))


def columns(step, ct):
    return pl.ds(pl.multiple_of(step * ct, ct), ct)


SLOTS = 3


def weight_copies(first, depth, count, places, weight_ref, ring_ref, sem, tile):
    ct = ring_ref.shape[3]
    slot = lax.rem(tile, SLOTS)
    return [
        pltpu.make_async_copy(
            weight_ref.at[:, pl.ds(pl.multiple_of(places[first + i] * depth, depth), depth), columns(tile, ct)],
            ring_ref.at[slot, :, pl.ds(i * depth, depth)],
            sem.at[slot, i],
        )
        for i in range(count)
    ]


def scaled(x_ref, gain, xg_ref, at):
    x = x_ref[...].astype(F32)
    xg_ref[:, at] = (x * gain).astype(BF16)
    return jnp.sum(x * x, axis=1, keepdims=True)


def products(copies, tiles, xg_ref, ring_ref, loaded, use, begun_ref=None, done=0):
    ahead = min(SLOTS - 1, tiles)

    def step(tile, _):
        @pl.when(tile + ahead < tiles)
        def _():
            for copy in copies(tile + ahead):
                copy.start()

        @pl.when(tile >= loaded)
        def _():
            for copy in copies(tile):
                copy.wait()

        slot = lax.rem(tile, SLOTS)
        use(tile, [dot(xg_ref[...], ring_ref[slot, j]) for j in range(3)])
        return 0

    if done:
        if ahead < tiles:
            for copy in copies(ahead):
                copy.start()
        use(0, [begun_ref[j].astype(F32) + dot(xg_ref[:, done:], ring_ref[0, j, done:]) for j in range(3)])
    lax.fori_loop(1 if done else 0, tiles, step, 0)


def local_kernel(first, places, own_ref, beside_ref, gain_ref, weight_ref, out_w_ref, acc_ref, ssq_ref, held_w_ref,
                 own_held, xg_ref, ring_ref, sem, own_sem, out_sem):
    ct, depth = ring_ref.shape[3], own_ref.shape[1]
    tiles = weight_ref.shape[2] // ct
    piece = out_w_ref.shape[0] // tiles
    copies = functools.partial(weight_copies, first, depth, 2, places, weight_ref, ring_ref, sem)

    def piece_copy(tile):
        rows = pl.ds(pl.multiple_of(tile * piece, piece), piece)
        return pltpu.make_async_copy(out_w_ref.at[rows], held_w_ref.at[rows], out_sem.at[tile])

    def use(tile, streams):
        piece_copy(tile).start()
        for j in range(3):
            acc_ref[j, :, columns(tile, ct)] = streams[j].astype(BF16)

    load = pltpu.make_async_copy(own_ref, own_held, own_sem)
    load.start()
    for tile in range(min(SLOTS - 1, tiles)):
        for copy in copies(tile):
            copy.start()
    total = scaled(beside_ref, gain_ref[places[first + 1]], xg_ref, slice(depth, 2 * depth))
    load.wait()
    total = total + scaled(own_held, gain_ref[places[first]], xg_ref, slice(0, depth))
    ssq_ref[...] = jnp.broadcast_to(total, ssq_ref.shape)
    products(copies, tiles, xg_ref, ring_ref, 0, use)
    for tile in range(tiles):
        piece_copy(tile).wait()


def ready_kernel(first, depth, count, places, taps_ref, skip_ref, of_filter_ref, weight_ref, _, spec_ref, ring_ref,
                 taps_held, taps_sem, sem):
    load = pltpu.make_async_copy(taps_ref, taps_held, taps_sem)
    load.start()
    tiles = weight_ref.shape[2] // ring_ref.shape[3]
    copies = functools.partial(weight_copies, first, depth, count, places, weight_ref, ring_ref, sem)
    ahead = min(SLOTS - 1, tiles)
    for tile in range(ahead):
        for copy in copies(tile):
            copy.start()
    load.wait()
    channels = taps_ref.shape[1]
    wide = column_tile(channels, 512)
    for at in range(0, channels, wide):
        at = slice(at, at + wide)
        h = taps_held[:, at]
        at_first = lax.broadcasted_iota(jnp.int32, h.shape, 0) == 0
        h = h + jnp.where(at_first, skip_ref[:, at], 0.0)
        high = h.astype(BF16)
        low = (h - high.astype(F32)).astype(BF16)
        spec_ref[:, at] = dot(of_filter_ref[...], jnp.concatenate([high, low], axis=0))
    for tile in range(ahead):
        for copy in copies(tile):
            copy.wait()


def scaled_kernel(first, n_lhs, places, *refs):
    tokens = refs[:n_lhs]
    gain_ref, ssq_in_ref, ring_ref, xg_ref, ssq_ref, begun_ref = refs[n_lhs:]
    depth = tokens[0].shape[1]
    total = ssq_in_ref[...]
    for i, x_ref in enumerate(tokens):
        total = total + scaled(x_ref, gain_ref[places[first + i]], xg_ref, slice(i * depth, (i + 1) * depth))
    ssq_ref[...] = total
    half = n_lhs * depth
    for j in range(3):
        begun_ref[j] = dot(xg_ref[:, :half], ring_ref[0, j, :half]).astype(BF16)


def gate(before, now, query, at, spec_ref, fwd_ref, inv_ref):
    window = jnp.concatenate([before, now], axis=0)
    filtered = convolved(window, spec_ref[:, at], fwd_ref[...], inv_ref[...])
    return (query.astype(F32) * filtered).astype(BF16)


def last_kernel(first, d_model, taps, n_lhs, places, *refs):
    tokens = refs[:n_lhs]
    gain_ref, weight_ref, acc_ref, ssq_ref, begun_ref, spec_ref, fwd_ref, inv_ref, _, _ = refs[n_lhs : n_lhs + 10]
    tail_ref, q_ref, mixed_ref, gated_ref, xg_ref, ring_ref, mixed_rest, sem = refs[n_lhs + 10 :]
    channels, ct = weight_ref.shape[2], ring_ref.shape[3]
    tiles = channels // ct
    depth = tokens[0].shape[1]
    copies = functools.partial(weight_copies, first, depth, 2 * n_lhs, places, weight_ref, ring_ref, sem)

    total = ssq_ref[:, :1]
    for i, x_ref in enumerate(tokens, n_lhs):
        total = total + scaled(x_ref, gain_ref[places[first + i]], xg_ref, slice(i * depth, (i + 1) * depth))
    scale = lax.rsqrt(total / d_model + 1e-06)

    def use(tile, streams):
        at = columns(tile, ct)
        query, keys, values = [((acc_ref[j, :, at].astype(F32) + streams[j]) * scale).astype(BF16) for j in range(3)]
        mixed = (keys.astype(F32) * values.astype(F32)).astype(BF16)
        q_ref[:, at] = query[:taps]
        gated_ref[:, at] = query[taps:]
        mixed_ref[:, at] = mixed[:taps]
        mixed_rest[:, at] = mixed[taps:]
        tail_ref[:, at] = mixed[mixed.shape[0] - taps :]

    products(copies, tiles, xg_ref, ring_ref, min(SLOTS - 1, tiles), use, begun_ref, n_lhs * depth)
    wide = column_tile(channels, 2048)
    for at in range(0, channels, wide):
        at = slice(at, at + wide)
        before = mixed_ref[:, at]
        for row in range(0, mixed_rest.shape[0], taps):
            rows = slice(row, row + taps)
            now = mixed_rest[rows, at]
            gated_ref[rows, at] = gate(before, now, gated_ref[rows, at], at, spec_ref, fwd_ref, inv_ref)
            before = now


def block_columns(places, first, group, width):
    return pl.ds(pl.multiple_of(places[first + group] * width, width), width)


def first_kernel(has_before, first, places, halo_ref, mixed_ref, q_ref, spec_ref, fwd_ref, inv_ref, w_ref, *refs):
    gated_ref, far_ref = refs[-2:]
    channels = q_ref.shape[1]
    ct = column_tile(channels, 2048)
    for at in range(0, channels, ct):
        at = slice(at, at + ct)
        before = jnp.where(places[has_before] > 0, halo_ref[:, at].astype(F32), 0.0).astype(BF16)
        gated_ref[:, at] = gate(before, mixed_ref[:, at], q_ref[:, at], at, spec_ref, fwd_ref, inv_ref)
    n_far, _, width = far_ref.shape
    for g in range(n_far):
        far_ref[g] = dot(gated_ref[...], w_ref[:, block_columns(places, first, g, width)]).astype(BF16)


def params(mib, steps=1):
    return pltpu.CompilerParams(dimension_semantics=("arbitrary",) * steps, vmem_limit_bytes=mib * MIB)


def in_hbm(x):
    return pltpu.with_memory_space_constraint(x, pltpu.HBM)


def in_vmem(x):
    return pltpu.with_memory_space_constraint(x, pltpu.VMEM)


RESIDENT = pl.BlockSpec(memory_space=pltpu.VMEM)


def whole(shape):
    return pl.BlockSpec(shape, lambda ch, *_: (0,) * len(shape))


def cost(rows, depth, width, extra=0):
    return pl.CostEstimate(
        flops=2 * rows * depth * width, bytes_accessed=2 * (rows * depth + depth * width) + extra, transcendentals=0
    )


def column_tile(channels, most=256):
    return most if channels % most == 0 else channels


def nothing_kernel(*refs):
    pass


def held_until(x, *others):
    return pl.pallas_call(
        nothing_kernel,
        in_specs=[pl.BlockSpec(memory_space=pl.ANY)] * (1 + len(others)),
        out_specs=pl.BlockSpec(memory_space=pl.ANY),
        out_shape=jax.ShapeDtypeStruct(x.shape, x.dtype),
        input_output_aliases={0: 0},
        compiler_params=pltpu.CompilerParams(vmem_limit_bytes=2 * MIB),
        name="held_until",
    )(x, *others)


BRIEF = pl.CostEstimate(flops=1, bytes_accessed=1, transcendentals=0)
IN_PLACE = pl.BlockSpec(memory_space=pl.ANY)
SCALARS = pl.BlockSpec(memory_space=pltpu.SMEM)


def ring_of(depth, channels):
    return pltpu.VMEM((SLOTS, 3, depth, column_tile(channels)), BF16)


def gain_rows(norm_gain, depth):
    return in_hbm(norm_gain.reshape(-1, 1, depth))


def project_local(own, beside, places, first, norm_gain, in_weight, out_weight):
    rows, depth = own.shape
    channels = in_weight.shape[2]
    ct = column_tile(channels)
    held = 2 * (rows * depth * 3 + SLOTS * 3 * 2 * depth * ct)
    return pl.pallas_call(
        functools.partial(local_kernel, first),
        in_specs=[SCALARS, IN_PLACE, RESIDENT, RESIDENT, IN_PLACE, IN_PLACE],
        out_specs=[RESIDENT] * 3,
        out_shape=[
            pltpu.VMEM((3, rows, channels), BF16),
            pltpu.VMEM((rows, 128), F32),
            pltpu.VMEM(out_weight.shape, BF16),
        ],
        scratch_shapes=[
            pltpu.VMEM((rows, depth), BF16),
            pltpu.VMEM((rows, 2 * depth), BF16),
            ring_of(2 * depth, channels),
            pltpu.SemaphoreType.DMA((SLOTS, 2)),
            pltpu.SemaphoreType.DMA,
            pltpu.SemaphoreType.DMA((channels // ct,)),
        ],
        compiler_params=pltpu.CompilerParams(vmem_limit_bytes=held + 10 * MIB),
        cost_estimate=cost(rows, depth * 2, 3 * channels),
        name="project_local",
    )(places, in_hbm(own), in_vmem(beside), gain_rows(norm_gain, depth), in_hbm(in_weight), in_hbm(out_weight))


def get_ready(places, first, depth, count, filter_taps, conv_skip, of_filter, in_weight, wait):
    taps, channels = filter_taps.shape
    return pl.pallas_call(
        functools.partial(ready_kernel, first, depth, count),
        in_specs=[SCALARS, IN_PLACE, RESIDENT, RESIDENT, IN_PLACE, IN_PLACE],
        out_specs=[RESIDENT] * 2,
        out_shape=[pltpu.VMEM((3 * taps, channels), F32), ring_of(depth * count, channels)],
        scratch_shapes=[
            pltpu.VMEM((taps, channels), F32),
            pltpu.SemaphoreType.DMA,
            pltpu.SemaphoreType.DMA((SLOTS, count)),
        ],
        compiler_params=pltpu.CompilerParams(vmem_limit_bytes=8 * MIB),
        cost_estimate=BRIEF,
        name="get_ready",
    )(places, in_hbm(filter_taps), conv_skip.reshape(1, -1), of_filter, in_hbm(in_weight), wait)


def scale_far(far, places, first, norm_gain, ssq, ring):
    n, (rows, depth) = len(far), far[0].shape
    return pl.pallas_call(
        functools.partial(scaled_kernel, first, n),
        in_specs=[SCALARS] + [RESIDENT] * (n + 3),
        out_specs=[RESIDENT] * 3,
        out_shape=[
            pltpu.VMEM((rows, 2 * n * depth), BF16),
            pltpu.VMEM(ssq.shape, F32),
            pltpu.VMEM((3, rows, ring.shape[3]), BF16),
        ],
        compiler_params=pltpu.CompilerParams(vmem_limit_bytes=8 * MIB),
        cost_estimate=BRIEF,
        name="scale_far",
    )(places, *[in_vmem(x) for x in far], gain_rows(norm_gain, depth), *[in_vmem(x) for x in (ssq, ring)])


def project_rest(lhs, places, first, norm_gain, in_weight, resident, xg, ring, d_model, taps):
    n, (rows, depth) = len(lhs), lhs[0].shape
    channels = in_weight.shape[2]
    rest = rows - taps
    at = n + 3 + len(resident)
    out = pl.pallas_call(
        functools.partial(last_kernel, first, d_model, taps, n),
        in_specs=[SCALARS] + [RESIDENT] * (n + 1) + [IN_PLACE] + [RESIDENT] * (len(resident) + 2),
        out_specs=[RESIDENT] * 6,
        out_shape=[pltpu.VMEM((r, channels), BF16) for r in (taps, taps, taps, rest)]
        + [pltpu.VMEM(x.shape, BF16) for x in (xg, ring)],
        input_output_aliases={at: 4, at + 1: 5},
        scratch_shapes=[pltpu.VMEM((rest, channels), BF16)] + [pltpu.SemaphoreType.DMA((SLOTS, 2 * n))],
        compiler_params=pltpu.CompilerParams(vmem_limit_bytes=2 * rest * channels + 6 * MIB),
        cost_estimate=cost(rows, d_model // 2, 3 * channels),
        name="project_rest",
    )(
        places,
        *[in_vmem(x) for x in lhs],
        gain_rows(norm_gain, depth),
        in_hbm(in_weight),
        *[in_vmem(x) for x in (*resident, xg, ring)],
    )
    return out[:4]


def gate_first(halo, mixed, query, spectrum, forward, inverse, out_weight, places, has_before, first, n_far, width, waits):
    taps, channels = mixed.shape
    resident = (halo, mixed, query, spectrum, forward, inverse, out_weight)
    return pl.pallas_call(
        functools.partial(first_kernel, has_before, first),
        in_specs=[SCALARS] + [RESIDENT] * len(resident) + [IN_PLACE] * len(waits),
        out_specs=[RESIDENT] * 2,
        out_shape=[pltpu.VMEM((taps, channels), BF16), pltpu.VMEM((n_far, taps, width), BF16)],
        compiler_params=pltpu.CompilerParams(vmem_limit_bytes=10 * MIB),
        cost_estimate=BRIEF,
        name="gate_first",
    )(places, *[in_vmem(x) for x in resident], *waits)


def out_kernel(n_add, n_out, first, places, *refs):
    part_ref, w_ref, add, out = refs[0], refs[1], refs[2 : 2 + n_add], refs[-n_out:]
    width = out[0].shape[-1] * n_out
    for g in range(out[0].shape[0]):
        product = dot(part_ref[...], w_ref[:, block_columns(places, first, g, width)])
        if n_out > 1:
            for i, o_ref in enumerate(out):
                o_ref[g] = product[:, i * width // n_out : (i + 1) * width // n_out].astype(o_ref.dtype)
        elif not add:
            out[0][g] = product.astype(out[0].dtype)
        for i, x in enumerate(add):
            at = slice(i * width // n_add, (i + 1) * width // n_add)
            out[0][g, :, at] = (product[:, at] + x[g].astype(F32)).astype(out[0].dtype)


def add_kernel(a_ref, b_ref, o_ref):
    o_ref[...] = (a_ref[...] + b_ref[...].astype(F32)).astype(o_ref.dtype)


def added(a, b):
    return pl.pallas_call(
        add_kernel,
        in_specs=[RESIDENT] * 2,
        out_specs=RESIDENT,
        out_shape=pltpu.VMEM(b.shape, b.dtype),
        compiler_params=pltpu.CompilerParams(vmem_limit_bytes=8 * MIB),
        cost_estimate=BRIEF,
        name="added",
    )(in_vmem(a), in_vmem(b))


def project_out(part, out_weight, places, first, n_groups, width, name, add=(), dtype=BF16, waits=(), n_out=1):
    rows = part.shape[0]
    out = pl.pallas_call(
        functools.partial(out_kernel, len(add), n_out, first),
        in_specs=[SCALARS] + [RESIDENT] * (2 + len(add)) + [IN_PLACE] * len(waits),
        out_specs=[RESIDENT] * n_out,
        out_shape=[pltpu.VMEM((n_groups, rows, width // n_out), dtype)] * n_out,
        compiler_params=pltpu.CompilerParams(vmem_limit_bytes=10 * MIB),
        cost_estimate=BRIEF,
        name=name,
    )(places, *[in_vmem(x) for x in (part, out_weight, *add)], *waits)
    return out if n_out > 1 else out[0]


def total_kernel(n_come, first_row, *refs):
    near_ref, come = refs[0], refs[1 : 1 + n_come]
    out_ref, held, sem = refs[-3:]
    total = near_ref[0]
    for x in come:
        total = total + x[...].astype(F32)
    held[...] = total.astype(BF16)
    copy = pltpu.make_async_copy(held, out_ref.at[pl.ds(first_row, held.shape[0])], sem)
    copy.start()
    copy.wait()


def total_rows(near, come, first_row, rows, into):
    part, width = come[0].shape
    given = [] if into is None else [into]
    n = 1 + len(come)
    return pl.pallas_call(
        functools.partial(total_kernel, len(come), first_row),
        in_specs=[RESIDENT] * n + [IN_PLACE] * len(given),
        out_specs=IN_PLACE,
        out_shape=jax.ShapeDtypeStruct((rows, width), BF16),
        input_output_aliases={n: 0} if given else {},
        scratch_shapes=[pltpu.VMEM((part, width), BF16), pltpu.SemaphoreType.DMA],
        compiler_params=pltpu.CompilerParams(vmem_limit_bytes=8 * MIB),
        cost_estimate=BRIEF,
        name="total_rows",
    )(*[in_vmem(x) for x in (near, *come)], *given)


def on_device(tokens, norm_gain, in_weight, filter_taps, conv_skip, out_weight):
    n_row, n_col, n_seq = lax.axis_size("trow"), lax.axis_size("tcol"), lax.axis_size("seq")
    r, c = lax.axis_index("trow"), lax.axis_index("tcol")
    rows, depth = tokens.shape
    taps = filter_taps.shape[0]
    d_model = depth * n_row * n_col
    assert n_row == 2 and rows % taps == 0
    forward, inverse, of_filter = (jnp.asarray(m) for m in dft_matrices(taps))

    def other_core(x):
        return lax.ppermute(x, "trow", [(0, 1), (1, 0)])

    def chips_along(x, s):
        return lax.ppermute(x, "tcol", [(i, (i + s) % n_col) for i in range(n_col)])

    def block_of(row, s):
        return row * n_col + lax.rem(c + s + n_col, n_col)

    shifts = range(1, n_col)
    n_far = n_col - 1
    beside = other_core(tokens)
    far = [chips_along(tokens, s) for s in shifts]
    places = jnp.stack(
        [block_of(r, 0), block_of(1 - r, 0)]
        + [block_of(row, -s) for row in (r, 1 - r) for s in shifts]
        + [block_of(row, s) for row in (1 - r, r) for s in (*shifts, 0)]
        + [jnp.minimum(lax.axis_index("seq"), 1)]
    )
    has_before = 2 + 4 * n_far + 2
    theirs_far = 2 + 2 * n_far
    theirs_near, mine_far = theirs_far + n_far, theirs_far + n_col
    mine_near = mine_far + n_far
    acc, ssq, held_weight = project_local(tokens, beside, places, 0, norm_gain, in_weight, out_weight)
    spectrum, ring = get_ready(places, 2, depth, 2 * n_far, filter_taps, conv_skip, of_filter, in_weight, ssq)
    far = [held_until(x, spectrum) for x in far]
    lhs = [other_core(x) for x in far]
    xg, ssq, begun = scale_far(far, places, 2, norm_gain, ssq, ring)
    resident = [acc, ssq, begun, spectrum, forward, inverse]
    tail, q_low, mixed_low, gated_rest = project_rest(
        lhs, places, 2, norm_gain, in_weight, resident, xg, ring, d_model, taps
    )
    halo = lax.ppermute(tail, "seq", [(i, (i + 1) % n_seq) for i in range(n_seq)])

    project = functools.partial(project_out, out_weight=held_weight, places=places, width=depth)

    theirs = other_core(project(gated_rest, first=theirs_far, n_groups=n_far, name="rest_theirs_far"))
    sent = project(gated_rest, first=mine_far, n_groups=n_far, name="rest_mine_far", add=[theirs])
    come = [chips_along(sent[s - 1], s) for s in shifts]
    halves = project(gated_rest, first=theirs_near, n_groups=1, name="rest_theirs_near", waits=[sent], n_out=2)

    gated_first, theirs = gate_first(
        halo, mixed_low, q_low, spectrum, forward, inverse, held_weight, places, has_before, theirs_far, n_far, depth, halves
    )
    mine = project(gated_first, first=mine_far, n_groups=n_far, name="first_mine_far", dtype=F32)
    sent_first = added(mine, other_core(theirs))
    come_first = [chips_along(sent_first[s - 1], s) for s in shifts]
    halves_first = project(
        gated_first, first=theirs_near, n_groups=1, name="first_theirs_near", waits=[sent_first], n_out=2
    )

    near, near_first = [
        project(part, first=mine_near, n_groups=1, name=name, add=[other_core(x) for x in pieces], dtype=F32)
        for part, name, pieces in (
            (gated_rest, "rest_mine_near", halves),
            (gated_first, "first_mine_near", halves_first),
        )
    ]
    out = total_rows(near, come, taps, rows, None)
    return total_rows(near_first, come_first, 0, rows, out)


def solution(mesh):
    placed = (
        P("seq", ("trow", "tcol")),
        P(),
        P(None, None, ("trow", "tcol")),
        P(None, ("trow", "tcol")),
        P(("trow", "tcol")),
        P(("trow", "tcol"), None),
    )
    return jax.shard_map(
        on_device, mesh=mesh, in_specs=placed, out_specs=P("seq", ("trow", "tcol")), check_vma=False
    )
```

```python
import functools

import jax
import jax.numpy as jnp
import numpy as np
from jax import lax
from jax.experimental import pallas as pl
from jax.experimental.pallas import tpu as pltpu
from jax.sharding import PartitionSpec as P

BF16 = jnp.bfloat16
F32 = jnp.float32
MIB = 1024 * 1024


def dft_matrices(taps):
    size = 2 * taps
    t = np.arange(size)[None, :]
    k = np.arange(taps)[:, None]
    angle = 2.0 * np.pi * ((k * t) % size) / size
    cos, sin = np.cos(angle), np.sin(angle)
    alternating = (-1.0) ** t
    forward = np.concatenate([cos, alternating, -sin[1:]], axis=0)
    inverse = np.concatenate([cos[:1], 2.0 * cos[1:], alternating, -2.0 * sin[1:]], axis=0).T / size
    short = slice(0, taps)
    of_filter = np.concatenate(
        [cos[:, short], 0.0 * sin[:1, short], -sin[1:, short], alternating[:, short], cos[1:, short]], axis=0
    )
    of_filter = np.concatenate([of_filter, of_filter], axis=1)
    return forward.astype(BF16), inverse[taps:].astype(BF16), of_filter.astype(BF16)


def dot(a, b):
    return jnp.dot(a, b, preferred_element_type=F32)


def convolved(window, spectrum, forward, inverse):
    half = window.shape[0] // 2
    x = dot(forward, window)
    xa, xb = x[:half], x[half:]
    ha, hb, hc = spectrum[:half], spectrum[half : 2 * half], spectrum[2 * half :]
    y = jnp.concatenate([xa * ha - xb * hb, xa * hb + xb * hc], axis=0)
    return dot(inverse, y.astype(BF16))


def columns(step, ct):
    return pl.ds(pl.multiple_of(step * ct, ct), ct)


SLOTS = 3


def weight_copies(first, depth, count, places, weight_ref, ring_ref, sem, tile):
    ct = ring_ref.shape[3]
    slot = lax.rem(tile, SLOTS)
    return [
        pltpu.make_async_copy(
            weight_ref.at[:, pl.ds(pl.multiple_of(places[first + i] * depth, depth), depth), columns(tile, ct)],
            ring_ref.at[slot, :, pl.ds(i * depth, depth)],
            sem.at[slot, i],
        )
        for i in range(count)
    ]


def scaled(x_ref, gain, xg_ref, at):
    x = x_ref[...].astype(F32)
    xg_ref[:, at] = (x * gain).astype(BF16)
    return jnp.sum(x * x, axis=1, keepdims=True)


def products(copies, tiles, xg_ref, ring_ref, loaded, use, begun_ref=None, done=0):
    ahead = min(SLOTS - 1, tiles)

    def step(tile, _):
        @pl.when(tile + ahead < tiles)
        def _():
            for copy in copies(tile + ahead):
                copy.start()

        @pl.when(tile >= loaded)
        def _():
            for copy in copies(tile):
                copy.wait()

        slot = lax.rem(tile, SLOTS)
        use(tile, [dot(xg_ref[...], ring_ref[slot, j]) for j in range(3)])
        return 0

    if done:
        if ahead < tiles:
            for copy in copies(ahead):
                copy.start()
        use(0, [begun_ref[j].astype(F32) + dot(xg_ref[:, done:], ring_ref[0, j, done:]) for j in range(3)])
    lax.fori_loop(1 if done else 0, tiles, step, 0)


def local_kernel(first, places, own_ref, beside_ref, gain_ref, weight_ref, out_w_ref, acc_ref, ssq_ref, held_w_ref,
                 own_held, xg_ref, ring_ref, sem, own_sem, out_sem):
    ct, depth = ring_ref.shape[3], own_ref.shape[1]
    tiles = weight_ref.shape[2] // ct
    piece = out_w_ref.shape[0] // tiles
    copies = functools.partial(weight_copies, first, depth, 2, places, weight_ref, ring_ref, sem)

    def piece_copy(tile):
        rows = pl.ds(pl.multiple_of(tile * piece, piece), piece)
        return pltpu.make_async_copy(out_w_ref.at[rows], held_w_ref.at[rows], out_sem.at[tile])

    def use(tile, streams):
        piece_copy(tile).start()
        for j in range(3):
            acc_ref[j, :, columns(tile, ct)] = streams[j].astype(BF16)

    load = pltpu.make_async_copy(own_ref, own_held, own_sem)
    load.start()
    for tile in range(min(SLOTS - 1, tiles)):
        for copy in copies(tile):
            copy.start()
    total = scaled(beside_ref, gain_ref[places[first + 1]], xg_ref, slice(depth, 2 * depth))
    load.wait()
    total = total + scaled(own_held, gain_ref[places[first]], xg_ref, slice(0, depth))
    ssq_ref[...] = jnp.broadcast_to(total, ssq_ref.shape)
    products(copies, tiles, xg_ref, ring_ref, 0, use)
    for tile in range(tiles):
        piece_copy(tile).wait()


def ready_kernel(first, depth, count, places, taps_ref, skip_ref, of_filter_ref, weight_ref, _, spec_ref, ring_ref,
                 taps_held, taps_sem, sem):
    load = pltpu.make_async_copy(taps_ref, taps_held, taps_sem)
    load.start()
    tiles = weight_ref.shape[2] // ring_ref.shape[3]
    copies = functools.partial(weight_copies, first, depth, count, places, weight_ref, ring_ref, sem)
    ahead = min(SLOTS - 1, tiles)
    for tile in range(ahead):
        for copy in copies(tile):
            copy.start()
    load.wait()
    channels = taps_ref.shape[1]
    wide = column_tile(channels, 512)
    for at in range(0, channels, wide):
        at = slice(at, at + wide)
        h = taps_held[:, at]
        at_first = lax.broadcasted_iota(jnp.int32, h.shape, 0) == 0
        h = h + jnp.where(at_first, skip_ref[:, at], 0.0)
        high = h.astype(BF16)
        low = (h - high.astype(F32)).astype(BF16)
        spec_ref[:, at] = dot(of_filter_ref[...], jnp.concatenate([high, low], axis=0))
    for tile in range(ahead):
        for copy in copies(tile):
            copy.wait()


def scaled_kernel(first, n_lhs, places, *refs):
    tokens = refs[:n_lhs]
    gain_ref, ssq_in_ref, ring_ref, xg_ref, ssq_ref, begun_ref = refs[n_lhs:]
    depth = tokens[0].shape[1]
    total = ssq_in_ref[...]
    for i, x_ref in enumerate(tokens):
        total = total + scaled(x_ref, gain_ref[places[first + i]], xg_ref, slice(i * depth, (i + 1) * depth))
    ssq_ref[...] = total
    half = n_lhs * depth
    for j in range(3):
        begun_ref[j] = dot(xg_ref[:, :half], ring_ref[0, j, :half]).astype(BF16)


def gate(before, now, query, at, spec_ref, fwd_ref, inv_ref):
    window = jnp.concatenate([before, now], axis=0)
    filtered = convolved(window, spec_ref[:, at], fwd_ref[...], inv_ref[...])
    return (query.astype(F32) * filtered).astype(BF16)


def last_kernel(first, d_model, taps, n_lhs, places, *refs):
    tokens = refs[:n_lhs]
    gain_ref, weight_ref, acc_ref, ssq_ref, begun_ref, spec_ref, fwd_ref, inv_ref, _, _ = refs[n_lhs : n_lhs + 10]
    tail_ref, q_ref, mixed_ref, gated_ref, xg_ref, ring_ref, mixed_rest, sem = refs[n_lhs + 10 :]
    channels, ct = weight_ref.shape[2], ring_ref.shape[3]
    tiles = channels // ct
    depth = tokens[0].shape[1]
    copies = functools.partial(weight_copies, first, depth, 2 * n_lhs, places, weight_ref, ring_ref, sem)

    total = ssq_ref[:, :1]
    for i, x_ref in enumerate(tokens, n_lhs):
        total = total + scaled(x_ref, gain_ref[places[first + i]], xg_ref, slice(i * depth, (i + 1) * depth))
    scale = lax.rsqrt(total / d_model + 1e-06)

    def use(tile, streams):
        at = columns(tile, ct)
        query, keys, values = [((acc_ref[j, :, at].astype(F32) + streams[j]) * scale).astype(BF16) for j in range(3)]
        mixed = (keys.astype(F32) * values.astype(F32)).astype(BF16)
        q_ref[:, at] = query[:taps]
        gated_ref[:, at] = query[taps:]
        mixed_ref[:, at] = mixed[:taps]
        mixed_rest[:, at] = mixed[taps:]
        tail_ref[:, at] = mixed[mixed.shape[0] - taps :]

    products(copies, tiles, xg_ref, ring_ref, min(SLOTS - 1, tiles), use, begun_ref, n_lhs * depth)
    wide = column_tile(channels, 2048)
    for at in range(0, channels, wide):
        at = slice(at, at + wide)
        before = mixed_ref[:, at]
        for row in range(0, mixed_rest.shape[0], taps):
            rows = slice(row, row + taps)
            now = mixed_rest[rows, at]
            gated_ref[rows, at] = gate(before, now, gated_ref[rows, at], at, spec_ref, fwd_ref, inv_ref)
            before = now


def block_columns(places, first, group, width):
    return pl.ds(pl.multiple_of(places[first + group] * width, width), width)


def first_kernel(has_before, first, places, halo_ref, mixed_ref, q_ref, spec_ref, fwd_ref, inv_ref, w_ref, *refs):
    gated_ref, far_ref = refs[-2:]
    channels = q_ref.shape[1]
    ct = column_tile(channels, 2048)
    for at in range(0, channels, ct):
        at = slice(at, at + ct)
        before = jnp.where(places[has_before] > 0, halo_ref[:, at], jnp.zeros_like(halo_ref[:, at]))
        gated_ref[:, at] = gate(before, mixed_ref[:, at], q_ref[:, at], at, spec_ref, fwd_ref, inv_ref)
    n_far, _, width = far_ref.shape
    for g in range(n_far):
        far_ref[g] = dot(gated_ref[...], w_ref[:, block_columns(places, first, g, width)]).astype(BF16)


def params(mib, steps=1):
    return pltpu.CompilerParams(dimension_semantics=("arbitrary",) * steps, vmem_limit_bytes=mib * MIB)


def in_hbm(x):
    return pltpu.with_memory_space_constraint(x, pltpu.HBM)


def in_vmem(x):
    return pltpu.with_memory_space_constraint(x, pltpu.VMEM)


RESIDENT = pl.BlockSpec(memory_space=pltpu.VMEM)


def whole(shape):
    return pl.BlockSpec(shape, lambda ch, *_: (0,) * len(shape))


def cost(rows, depth, width, extra=0):
    return pl.CostEstimate(
        flops=2 * rows * depth * width, bytes_accessed=2 * (rows * depth + depth * width) + extra, transcendentals=0
    )


def column_tile(channels, most=256):
    return most if channels % most == 0 else channels


def nothing_kernel(*refs):
    pass


def held_until(x, *others):
    return pl.pallas_call(
        nothing_kernel,
        in_specs=[pl.BlockSpec(memory_space=pl.ANY)] * (1 + len(others)),
        out_specs=pl.BlockSpec(memory_space=pl.ANY),
        out_shape=jax.ShapeDtypeStruct(x.shape, x.dtype),
        input_output_aliases={0: 0},
        compiler_params=pltpu.CompilerParams(vmem_limit_bytes=2 * MIB),
        name="held_until",
    )(x, *others)


BRIEF = pl.CostEstimate(flops=1, bytes_accessed=1, transcendentals=0)
IN_PLACE = pl.BlockSpec(memory_space=pl.ANY)
SCALARS = pl.BlockSpec(memory_space=pltpu.SMEM)


def ring_of(depth, channels):
    return pltpu.VMEM((SLOTS, 3, depth, column_tile(channels)), BF16)


def gain_rows(norm_gain, depth):
    return in_hbm(norm_gain.reshape(-1, 1, depth))


def project_local(own, beside, places, first, norm_gain, in_weight, out_weight):
    rows, depth = own.shape
    channels = in_weight.shape[2]
    ct = column_tile(channels)
    held = 2 * (rows * depth * 3 + SLOTS * 3 * 2 * depth * ct)
    return pl.pallas_call(
        functools.partial(local_kernel, first),
        in_specs=[SCALARS, IN_PLACE, RESIDENT, RESIDENT, IN_PLACE, IN_PLACE],
        out_specs=[RESIDENT] * 3,
        out_shape=[
            pltpu.VMEM((3, rows, channels), BF16),
            pltpu.VMEM((rows, 128), F32),
            pltpu.VMEM(out_weight.shape, BF16),
        ],
        scratch_shapes=[
            pltpu.VMEM((rows, depth), BF16),
            pltpu.VMEM((rows, 2 * depth), BF16),
            ring_of(2 * depth, channels),
            pltpu.SemaphoreType.DMA((SLOTS, 2)),
            pltpu.SemaphoreType.DMA,
            pltpu.SemaphoreType.DMA((channels // ct,)),
        ],
        compiler_params=pltpu.CompilerParams(vmem_limit_bytes=held + 10 * MIB),
        cost_estimate=cost(rows, depth * 2, 3 * channels),
        name="project_local",
    )(places, in_hbm(own), in_vmem(beside), gain_rows(norm_gain, depth), in_hbm(in_weight), in_hbm(out_weight))


def get_ready(places, first, depth, count, filter_taps, conv_skip, of_filter, in_weight, wait):
    taps, channels = filter_taps.shape
    return pl.pallas_call(
        functools.partial(ready_kernel, first, depth, count),
        in_specs=[SCALARS, IN_PLACE, RESIDENT, RESIDENT, IN_PLACE, IN_PLACE],
        out_specs=[RESIDENT] * 2,
        out_shape=[pltpu.VMEM((3 * taps, channels), F32), ring_of(depth * count, channels)],
        scratch_shapes=[
            pltpu.VMEM((taps, channels), F32),
            pltpu.SemaphoreType.DMA,
            pltpu.SemaphoreType.DMA((SLOTS, count)),
        ],
        compiler_params=pltpu.CompilerParams(vmem_limit_bytes=8 * MIB),
        cost_estimate=BRIEF,
        name="get_ready",
    )(places, in_hbm(filter_taps), conv_skip.reshape(1, -1), of_filter, in_hbm(in_weight), wait)


def scale_far(far, places, first, norm_gain, ssq, ring):
    n, (rows, depth) = len(far), far[0].shape
    return pl.pallas_call(
        functools.partial(scaled_kernel, first, n),
        in_specs=[SCALARS] + [RESIDENT] * (n + 3),
        out_specs=[RESIDENT] * 3,
        out_shape=[
            pltpu.VMEM((rows, 2 * n * depth), BF16),
            pltpu.VMEM(ssq.shape, F32),
            pltpu.VMEM((3, rows, ring.shape[3]), BF16),
        ],
        compiler_params=pltpu.CompilerParams(vmem_limit_bytes=8 * MIB),
        cost_estimate=BRIEF,
        name="scale_far",
    )(places, *[in_vmem(x) for x in far], gain_rows(norm_gain, depth), *[in_vmem(x) for x in (ssq, ring)])


def project_rest(lhs, places, first, norm_gain, in_weight, resident, xg, ring, d_model, taps):
    n, (rows, depth) = len(lhs), lhs[0].shape
    channels = in_weight.shape[2]
    rest = rows - taps
    at = n + 3 + len(resident)
    out = pl.pallas_call(
        functools.partial(last_kernel, first, d_model, taps, n),
        in_specs=[SCALARS] + [RESIDENT] * (n + 1) + [IN_PLACE] + [RESIDENT] * (len(resident) + 2),
        out_specs=[RESIDENT] * 6,
        out_shape=[pltpu.VMEM((r, channels), BF16) for r in (taps, taps, taps, rest)]
        + [pltpu.VMEM(x.shape, BF16) for x in (xg, ring)],
        input_output_aliases={at: 4, at + 1: 5},
        scratch_shapes=[pltpu.VMEM((rest, channels), BF16)] + [pltpu.SemaphoreType.DMA((SLOTS, 2 * n))],
        compiler_params=pltpu.CompilerParams(vmem_limit_bytes=2 * rest * channels + 6 * MIB),
        cost_estimate=cost(rows, d_model // 2, 3 * channels),
        name="project_rest",
    )(
        places,
        *[in_vmem(x) for x in lhs],
        gain_rows(norm_gain, depth),
        in_hbm(in_weight),
        *[in_vmem(x) for x in (*resident, xg, ring)],
    )
    return out[:4]


def gate_first(halo, mixed, query, spectrum, forward, inverse, out_weight, places, has_before, first, n_far, width, waits):
    taps, channels = mixed.shape
    resident = (halo, mixed, query, spectrum, forward, inverse, out_weight)
    return pl.pallas_call(
        functools.partial(first_kernel, has_before, first),
        in_specs=[SCALARS] + [RESIDENT] * len(resident) + [IN_PLACE] * len(waits),
        out_specs=[RESIDENT] * 2,
        out_shape=[pltpu.VMEM((taps, channels), BF16), pltpu.VMEM((n_far, taps, width), BF16)],
        compiler_params=pltpu.CompilerParams(vmem_limit_bytes=10 * MIB),
        cost_estimate=BRIEF,
        name="gate_first",
    )(places, *[in_vmem(x) for x in resident], *waits)


def out_kernel(n_add, n_out, first, places, *refs):
    part_ref, w_ref, add, out = refs[0], refs[1], refs[2 : 2 + n_add], refs[-n_out:]
    width = out[0].shape[-1] * n_out
    for g in range(out[0].shape[0]):
        product = dot(part_ref[...], w_ref[:, block_columns(places, first, g, width)])
        if n_out > 1:
            for i, o_ref in enumerate(out):
                o_ref[g] = product[:, i * width // n_out : (i + 1) * width // n_out].astype(o_ref.dtype)
        elif not add:
            out[0][g] = product.astype(out[0].dtype)
        for i, x in enumerate(add):
            at = slice(i * width // n_add, (i + 1) * width // n_add)
            out[0][g, :, at] = (product[:, at] + x[g].astype(F32)).astype(out[0].dtype)


def add_kernel(a_ref, b_ref, o_ref):
    o_ref[...] = (a_ref[...] + b_ref[...].astype(F32)).astype(o_ref.dtype)


def added(a, b):
    return pl.pallas_call(
        add_kernel,
        in_specs=[RESIDENT] * 2,
        out_specs=RESIDENT,
        out_shape=pltpu.VMEM(b.shape, b.dtype),
        compiler_params=pltpu.CompilerParams(vmem_limit_bytes=8 * MIB),
        cost_estimate=BRIEF,
        name="added",
    )(in_vmem(a), in_vmem(b))


def project_out(part, out_weight, places, first, n_groups, width, name, add=(), dtype=BF16, waits=(), n_out=1):
    rows = part.shape[0]
    out = pl.pallas_call(
        functools.partial(out_kernel, len(add), n_out, first),
        in_specs=[SCALARS] + [RESIDENT] * (2 + len(add)) + [IN_PLACE] * len(waits),
        out_specs=[RESIDENT] * n_out,
        out_shape=[pltpu.VMEM((n_groups, rows, width // n_out), dtype)] * n_out,
        compiler_params=pltpu.CompilerParams(vmem_limit_bytes=10 * MIB),
        cost_estimate=BRIEF,
        name=name,
    )(places, *[in_vmem(x) for x in (part, out_weight, *add)], *waits)
    return out if n_out > 1 else out[0]


def total_kernel(n_come, first_row, *refs):
    near_ref, come = refs[0], refs[1 : 1 + n_come]
    out_ref, held, sem = refs[-3:]
    total = near_ref[0]
    for x in come:
        total = total + x[...].astype(F32)
    held[...] = total.astype(BF16)
    copy = pltpu.make_async_copy(held, out_ref.at[pl.ds(first_row, held.shape[0])], sem)
    copy.start()
    copy.wait()


def total_rows(near, come, first_row, rows, into):
    part, width = come[0].shape
    given = [] if into is None else [into]
    n = 1 + len(come)
    return pl.pallas_call(
        functools.partial(total_kernel, len(come), first_row),
        in_specs=[RESIDENT] * n + [IN_PLACE] * len(given),
        out_specs=IN_PLACE,
        out_shape=jax.ShapeDtypeStruct((rows, width), BF16),
        input_output_aliases={n: 0} if given else {},
        scratch_shapes=[pltpu.VMEM((part, width), BF16), pltpu.SemaphoreType.DMA],
        compiler_params=pltpu.CompilerParams(vmem_limit_bytes=8 * MIB),
        cost_estimate=BRIEF,
        name="total_rows",
    )(*[in_vmem(x) for x in (near, *come)], *given)


def on_device(tokens, norm_gain, in_weight, filter_taps, conv_skip, out_weight):
    n_row, n_col, n_seq = lax.axis_size("trow"), lax.axis_size("tcol"), lax.axis_size("seq")
    r, c = lax.axis_index("trow"), lax.axis_index("tcol")
    rows, depth = tokens.shape
    taps = filter_taps.shape[0]
    d_model = depth * n_row * n_col
    assert n_row == 2 and rows % taps == 0
    forward, inverse, of_filter = (jnp.asarray(m) for m in dft_matrices(taps))

    def other_core(x):
        return lax.ppermute(x, "trow", [(0, 1), (1, 0)])

    def chips_along(x, s):
        return lax.ppermute(x, "tcol", [(i, (i + s) % n_col) for i in range(n_col)])

    def block_of(row, s):
        return row * n_col + lax.rem(c + s + n_col, n_col)

    shifts = range(1, n_col)
    n_far = n_col - 1
    beside = other_core(tokens)
    far = [chips_along(tokens, s) for s in shifts]
    places = jnp.stack(
        [block_of(r, 0), block_of(1 - r, 0)]
        + [block_of(row, -s) for row in (r, 1 - r) for s in shifts]
        + [block_of(row, s) for row in (1 - r, r) for s in (*shifts, 0)]
        + [jnp.minimum(lax.axis_index("seq"), 1)]
    )
    has_before = 2 + 4 * n_far + 2
    theirs_far = 2 + 2 * n_far
    theirs_near, mine_far = theirs_far + n_far, theirs_far + n_col
    mine_near = mine_far + n_far
    acc, ssq, held_weight = project_local(tokens, beside, places, 0, norm_gain, in_weight, out_weight)
    spectrum, ring = get_ready(places, 2, depth, 2 * n_far, filter_taps, conv_skip, of_filter, in_weight, ssq)
    far = [held_until(x, spectrum) for x in far]
    lhs = [other_core(x) for x in far]
    xg, ssq, begun = scale_far(far, places, 2, norm_gain, ssq, ring)
    resident = [acc, ssq, begun, spectrum, forward, inverse]
    tail, q_low, mixed_low, gated_rest = project_rest(
        lhs, places, 2, norm_gain, in_weight, resident, xg, ring, d_model, taps
    )
    halo = lax.ppermute(tail, "seq", [(i, (i + 1) % n_seq) for i in range(n_seq)])

    project = functools.partial(project_out, out_weight=held_weight, places=places, width=depth)

    theirs = other_core(project(gated_rest, first=theirs_far, n_groups=n_far, name="rest_theirs_far"))
    sent = project(gated_rest, first=mine_far, n_groups=n_far, name="rest_mine_far", add=[theirs])
    come = [chips_along(sent[s - 1], s) for s in shifts]
    halves = project(gated_rest, first=theirs_near, n_groups=1, name="rest_theirs_near", waits=[sent], n_out=2)

    gated_first, theirs = gate_first(
        halo, mixed_low, q_low, spectrum, forward, inverse, held_weight, places, has_before, theirs_far, n_far, depth, halves
    )
    mine = project(gated_first, first=mine_far, n_groups=n_far, name="first_mine_far", dtype=F32)
    sent_first = added(mine, other_core(theirs))
    come_first = [chips_along(sent_first[s - 1], s) for s in shifts]
    halves_first = project(
        gated_first, first=theirs_near, n_groups=1, name="first_theirs_near", waits=[sent_first], n_out=2
    )

    near, near_first = [
        project(part, first=mine_near, n_groups=1, name=name, add=[other_core(x) for x in pieces], dtype=F32)
        for part, name, pieces in (
            (gated_rest, "rest_mine_near", halves),
            (gated_first, "first_mine_near", halves_first),
        )
    ]
    out = total_rows(near, come, taps, rows, None)
    return total_rows(near_first, come_first, 0, rows, out)


def solution(mesh):
    placed = (
        P("seq", ("trow", "tcol")),
        P(),
        P(None, None, ("trow", "tcol")),
        P(None, ("trow", "tcol")),
        P(("trow", "tcol")),
        P(("trow", "tcol"), None),
    )
    return jax.shard_map(
        on_device, mesh=mesh, in_specs=placed, out_specs=P("seq", ("trow", "tcol")), check_vma=False
    )
```
